32 devices in a mesh: cell: 16 (over z, x, core), blk: 2 (over y).
Axes of the slice: x: 2, y: 2, z: 4, core: 2. Of those that a mesh axis runs over, the one named last changes fastest.
Arguments:
- hidden_in: bfloat16 [32, 1024, 1280], P('cell', 'blk'), may hold values from -6 to 6
- lengths: int32 [32], P('cell'), may hold values from 256 to 1024, as said below
- ln1_gain: float32 [1280], replicated, may hold values from 0.1 to 1.9
- ln1_bias: float32 [1280], replicated, may hold values from -1.75 to 1.75
- w_qkv: bfloat16 [1280, 3840], P('cell'), may hold values from -0.15625 to 0.15625
- q_bias: float32 [1280], replicated, may hold values from -3 to 3
- v_bias: float32 [1280], replicated, may hold values from -0.3125 to 0.3125
- w_out: bfloat16 [1280, 1280], P('cell'), may hold values from -2.5 to 2.5
- out_bias: float32 [1280], replicated, may hold values from -1.75 to 1.75
- ln2_gain: float32 [1280], replicated, may hold values from 0.1 to 1.9
- ln2_bias: float32 [1280], replicated, may hold values from -1.75 to 1.75
- w_up: bfloat16 [5120, 1280], P('cell'), may hold values from -0.15625 to 0.15625
- up_bias: float32 [5120], replicated, may hold values from -3 to 3
- w_down: bfloat16 [5120, 1280], P('cell'), may hold values from -0.078125 to 0.078125
- down_bias: float32 [1280], replicated, may hold values from -1.75 to 1.75
- cotangent: bfloat16 [32, 1024, 1280], P('cell', 'blk'), may hold values from -6 to 6
Outputs:
- out_hidden: bfloat16 [32, 1024, 1280], P('cell', 'blk')
- in_grad: float32 [32, 1024, 1280], P('cell', 'blk')
- ln1_gain_grad: float32 [1280], replicated
- ln1_bias_grad: float32 [1280], replicated
- w_qkv_grad: float32 [1280, 3840], P('cell')
- q_bias_grad: float32 [1280], replicated
- v_bias_grad: float32 [1280], replicated
- w_out_grad: float32 [1280, 1280], P('cell')
- out_bias_grad: float32 [1280], replicated
- ln2_gain_grad: float32 [1280], replicated
- ln2_bias_grad: float32 [1280], replicated
- w_up_grad: float32 [5120, 1280], P('cell')
- up_bias_grad: float32 [5120], replicated
- w_down_grad: float32 [5120, 1280], P('cell')
- down_bias_grad: float32 [1280], replicated
The draws below stay inside these ranges and needn't reach their ends.
Inputs may be any that keep to these rules, and one draw needn't show every extreme that they name: `lengths`: in each aligned block of 2 cells, one cell drawn from the seed has exactly 1024 valid genes; the others have 1024 // 4 to 1024.
All inputs are finite; a program needn't handle non-finite values.
Results may differ from the reference program's by a relative error of at most 0.015.
Values may be sent and summed in bfloat16 or wider, within the bound.
No kernel may reach another device: no remote copies, remote signals or barrier semaphores. Data moves between devices by JAX's collectives and lax.ppermute only.
A program may use at most 576 MiB of HBM per device.

```python
import math
import jax
import jax.numpy as jnp
from jax import lax

D = 1280
HEADS = 20
HEAD_DIM = 64
FF = 5120
GENES = 1024
CELL_DEV = 2
CELLS = 32


def draw_lengths(key, part):
    key = jax.random.fold_in(key, 7)
    pick_key, length_key = jax.random.split(key)
    group_count = CELLS // CELL_DEV
    chosen = jax.random.randint(pick_key, (group_count, 1), 0, CELL_DEV)
    others = jax.random.randint(length_key, (group_count, CELL_DEV), GENES // 4, GENES + 1)
    member = jnp.arange(CELL_DEV, dtype=jnp.int32)[None, :]
    return jnp.where(member == chosen, GENES, others).reshape(CELLS).astype(jnp.int32)


def spiked(values, own_key, source, target, parts, factor):
    def block_of(position):
        return (jnp.arange(values.shape[position]) // (values.shape[position] // parts)).reshape((-1,) + (1,) * (values.ndim - 1 - position))

    one_side = jax.random.permutation(own_key, parts)[block_of(target)]
    second = (block_of(target) + parts // 2) % parts
    return jnp.where((block_of(source) == one_side) | (block_of(source) == second), factor * values, values)


def block_scale(key, extent, cuts, low, high):
    def one(dim, shards_of):
        heights = jax.random.uniform(jax.random.fold_in(jax.random.fold_in(key, 6), dim), (shards_of,), jnp.float32, low / len(cuts), high / len(cuts))
        return jnp.repeat(jnp.exp(heights), extent[dim] // shards_of).reshape((-1,) + (1,) * (len(extent) - dim - 1))

    gain = one(*cuts[0])
    for cut in cuts[1:]:
        gain = gain * one(*cut)
    return gain


def gaussian(rng, extent, deviation, reach, shards=(), kind=jnp.bfloat16):
    level = block_scale(rng, extent, shards, -0.22, 0.18) if shards else 1.0
    drawn = jax.random.normal(rng, extent, jnp.float32) * deviation * level
    return jnp.minimum(jnp.maximum(drawn, -reach), reach).astype(kind)


def gaussian_with(rng, extent, deviation, limit, cuts, heavy, held_as=jnp.bfloat16):
    entries = deviation * jax.random.normal(rng, extent, jnp.float32)
    if cuts:
        entries = entries * block_scale(rng, extent, cuts, -0.22, 0.18)
    return jnp.clip(spiked(entries, jax.random.fold_in(rng, 3), *heavy), -limit, limit).astype(held_as)


def setup_inputs(seed: int = 0) -> dict:
    arg_keys = jax.random.split(jax.random.key(seed), 17)
    hidden_in = gaussian_with(arg_keys[0], (CELLS, GENES, D), 1.0, 6.0, ((0, 16), (1, 2)), (0, 2, 16, 2.0))
    lengths = draw_lengths(jax.random.fold_in(arg_keys[16], 71), 0)
    ln1_gain = jnp.clip(1.0 + 0.18 * jax.random.normal(arg_keys[2], (D,), jnp.float32), 0.1, 1.9)
    ln1_bias = gaussian(arg_keys[3], (D,), 0.3, 1.75, (), jnp.float32)
    w_qkv = gaussian(arg_keys[4], (D, 3 * D), D ** -0.5, 0.15625, ((0, 16),))
    q_bias = gaussian(arg_keys[5], (D,), 0.5, 3.0, (), jnp.float32)
    v_bias = gaussian(arg_keys[6], (D,), 0.05, 0.3125, (), jnp.float32)
    w_out = gaussian(arg_keys[7], (D, D), (max(1, D * 4 // GENES)) ** -0.5, 2.5, ((0, 16),))
    out_bias = gaussian(arg_keys[8], (D,), 0.3, 1.75, (), jnp.float32)
    ln2_gain = jnp.clip(1.0 + 0.18 * jax.random.normal(arg_keys[9], (D,), jnp.float32), 0.1, 1.9)
    ln2_bias = gaussian(arg_keys[10], (D,), 0.3, 1.75, (), jnp.float32)
    w_up = gaussian(arg_keys[11], (FF, D), D ** -0.5, 0.15625, ((0, 16),))
    up_bias = gaussian(arg_keys[12], (FF,), 0.5, 3.0, (), jnp.float32)
    w_down = gaussian(arg_keys[13], (FF, D), FF ** -0.5, 0.078125, ((0, 16),))
    down_bias = gaussian(arg_keys[14], (D,), 0.3, 1.75, (), jnp.float32)
    cotangent = gaussian(arg_keys[15], (CELLS, GENES, D), 1.0, 6.0, ((0, 16), (1, 2)))
    return dict(hidden_in=hidden_in, lengths=lengths, ln1_gain=ln1_gain, ln1_bias=ln1_bias, w_qkv=w_qkv, q_bias=q_bias, v_bias=v_bias, w_out=w_out, out_bias=out_bias, ln2_gain=ln2_gain, ln2_bias=ln2_bias, w_up=w_up, up_bias=up_bias, w_down=w_down, down_bias=down_bias, cotangent=cotangent)


epsilon = 1e-05
far_below = -1e+30

@jax.custom_vjp
def low(v):
    return lax.optimization_barrier(v.astype(jnp.bfloat16)).astype(jnp.float32)

@jax.custom_vjp
def low_back(v):
    return v

def low_keep(v):
    return (low(v), None)

def low_pass(kept, grad):
    return (grad,)

def back_keep(v):
    return (v, None)

def back_low(kept, grad):
    return (low(grad),)
low.defvjp(low_keep, low_pass)
low_back.defvjp(back_keep, back_low)

def layer_norm(source, gain_vec, shift_vec):
    row_mean = lax.optimization_barrier(jnp.mean(source, axis=-1, keepdims=True))
    centered = source - row_mean
    row_var = lax.optimization_barrier(jnp.mean(centered * centered, axis=-1, keepdims=True))
    return centered * lax.rsqrt(row_var + epsilon) * gain_vec + shift_vec

def product(left, right):
    return jnp.dot(left, right, precision=lax.Precision.HIGHEST)

def cell_forward(params, cell_rows, is_valid):
    ln1_gain, ln1_bias, w_qkv, q_bias, v_bias, w_out, out_bias, ln2_gain, ln2_bias, w_up, up_bias, w_down, down_bias = params
    head_shape = (GENES, HEADS, HEAD_DIM)
    normed = low(layer_norm(cell_rows, ln1_gain, ln1_bias))
    joined = product(normed, w_qkv)
    queries = low_back(low(joined[:, :D] + q_bias)).reshape(head_shape)
    keys_all = low_back(low(joined[:, D:2 * D])).reshape(head_shape)
    values_all = low_back(low(joined[:, 2 * D:] + v_bias)).reshape(head_shape)
    scores = jnp.einsum('qhd,khd->hqk', queries, keys_all, precision=lax.Precision.HIGHEST) / math.sqrt(HEAD_DIM)
    scores = low_back(scores)
    masked = jnp.where(is_valid[None, None, :], scores, far_below)
    row_top = lax.optimization_barrier(jnp.max(masked, axis=-1, keepdims=True))
    raised = jnp.exp(masked - row_top)
    weights = low(raised / lax.optimization_barrier(jnp.sum(raised, axis=-1, keepdims=True)))
    mixed_rows = jnp.einsum('hqk,khd->qhd', weights, values_all, precision=lax.Precision.HIGHEST).reshape(GENES, D)
    mixed_rows = low_back(low(jnp.where(is_valid[:, None], mixed_rows, 0.0)))
    branch = low_back(product(mixed_rows, w_out) + out_bias)
    middle = cell_rows + branch
    normed2 = low(layer_norm(middle, ln2_gain, ln2_bias))
    pre_gelu = low_back(product(normed2, w_up.T) + up_bias)
    hidden = low(jax.nn.gelu(pre_gelu, approximate=False))
    return middle + product(hidden, w_down) + down_bias

def reference(hidden_in, lengths, ln1_gain, ln1_bias, w_qkv, q_bias, v_bias, w_out, out_bias, ln2_gain, ln2_bias, w_up, up_bias, w_down, down_bias, cotangent):
    params = (ln1_gain, ln1_bias, w_qkv.astype(jnp.float32), q_bias, v_bias, w_out.astype(jnp.float32), out_bias, ln2_gain, ln2_bias, w_up.astype(jnp.float32), up_bias, w_down.astype(jnp.float32), down_bias)
    positions = jnp.arange(GENES, dtype=jnp.int32)

    def cell_step(totals, cell_item):
        cell_rows, cell_cot, cell_length = cell_item
        is_valid = positions < cell_length

        def forward(param_set, rows_in):
            return cell_forward(param_set, rows_in, is_valid)
        result, pull_back = jax.vjp(forward, params, cell_rows.astype(jnp.float32))
        param_grads, row_grads = pull_back(cell_cot.astype(jnp.float32))
        totals = jax.tree.map(jnp.add, totals, param_grads)
        return (totals, (result.astype(jnp.bfloat16), row_grads))
    zero_grads = jax.tree.map(jnp.zeros_like, params)
    totals, (out_hidden, in_grad) = lax.scan(cell_step, zero_grads, (hidden_in, cotangent, lengths))
    return (out_hidden, in_grad, totals[0], totals[1], totals[2], totals[3], totals[4], totals[5], totals[6], totals[7], totals[8], totals[9], totals[10], totals[11], totals[12])
```

```python
from functools import partial
import math

import jax
import jax.numpy as jnp
from jax import lax
from jax.experimental import pallas as pl
from jax.experimental.pallas import tpu as pltpu
from jax.sharding import PartitionSpec as P

HEAD_DIM = 64


epsilon = 1e-05
far_below = -1e30
row_contract = (((0,), (0,)), ((), ()))
col_contract = (((1,), (1,)), ((), ()))


def passed_along(x, axis, by):
    count = lax.axis_size(axis)
    return lax.ppermute(x, axis, [(i, (i + by) % count) for i in range(count)])


def layer_norm(source, gain_vec, shift_vec):
    row_mean = jnp.mean(source, axis=-1, keepdims=True)
    centered = source - row_mean
    row_var = jnp.mean(centered * centered, axis=-1, keepdims=True)
    return centered * lax.rsqrt(row_var + epsilon) * gain_vec + shift_vec


def local(
    hidden_in,
    lengths,
    ln1_gain,
    ln1_bias,
    w_qkv,
    q_bias,
    v_bias,
    w_out,
    out_bias,
    ln2_gain,
    ln2_bias,
    w_up,
    up_bias,
    w_down,
    down_bias,
    cotangent,
):
    cell_count, local_genes, model_width = hidden_in.shape
    row_count = cell_count * local_genes
    head_count = model_width // HEAD_DIM
    score_scale = 1.0 / math.sqrt(HEAD_DIM)
    cycle_size = lax.axis_size("blk")
    cycle_place = lax.axis_index("blk")
    ratio_ff = up_bias.shape[0] // model_width
    head_shape = (cell_count, local_genes, head_count, HEAD_DIM)
    stat_shape = (cell_count, head_count, local_genes)
    inputs = hidden_in.astype(jnp.float32).reshape(row_count, model_width)
    cot_rows = cotangent.reshape(row_count, model_width)
    gene_index = jnp.arange(local_genes, dtype=jnp.int32)
    query_valid = (cycle_place * local_genes + gene_index)[None, :] < lengths[:, None]
    normed, ln1_pull = jax.vjp(layer_norm, inputs, ln1_gain, ln1_bias)
    normed_low = normed.astype(jnp.bfloat16)
    part_cols = normed_low
    joined = jnp.dot(
        part_cols,
        lax.all_gather(w_qkv, "cell", axis=0, tiled=True),
        preferred_element_type=jnp.float32,
    )
    queries = (joined[:, :model_width] + q_bias).astype(jnp.bfloat16).reshape(head_shape)
    keys_own = joined[:, model_width : 2 * model_width].astype(jnp.bfloat16).reshape(head_shape)
    values_own = (joined[:, 2 * model_width :] + v_bias).astype(jnp.bfloat16).reshape(head_shape)

    def block_scores(key_block, owner_index):
        scores = (
            jnp.einsum("cqhd,ckhd->chqk", queries, key_block, preferred_element_type=jnp.float32)
            * score_scale
        )
        key_valid = (owner_index * local_genes + gene_index)[None, :] < lengths[:, None]
        return (scores, key_valid[:, None, None, :])

    def stats_turn(owner_index, carried, key_block):
        row_top, row_total = carried
        scores, is_valid = block_scores(key_block, owner_index)
        new_top = jnp.maximum(row_top, jnp.max(jnp.where(is_valid, scores, far_below), axis=-1))
        raised = jnp.where(is_valid, jnp.exp(scores - new_top[..., None]), 0.0)
        return (new_top, row_total * jnp.exp(row_top - new_top) + jnp.sum(raised, axis=-1))

    first_stats = stats_turn(
        cycle_place,
        (jnp.full(stat_shape, far_below, jnp.float32), jnp.zeros(stat_shape, jnp.float32)),
        keys_own,
    )

    def stats_step(step_index, carried):
        stats_now, key_block = carried
        key_block = passed_along(key_block, "blk", 1)
        return (
            stats_turn((cycle_place - step_index) % cycle_size, stats_now, key_block),
            key_block,
        )

    final_stats = lax.fori_loop(1, cycle_size, stats_step, (first_stats, keys_own))[0]
    log_total = final_stats[0] + jnp.log(final_stats[1])

    def block_weights(key_block, owner_index):
        scores, is_valid = block_scores(key_block, owner_index)
        return jnp.where(is_valid, jnp.exp(scores - log_total[..., None]), 0.0)

    def mix_turn(owner_index, mixed_sum, key_block, value_block):
        weights = block_weights(key_block, owner_index).astype(jnp.bfloat16)
        return mixed_sum + jnp.einsum(
            "chqk,ckhd->cqhd", weights, value_block, preferred_element_type=jnp.float32
        )

    mixed_start = mix_turn(cycle_place, jnp.zeros(head_shape, jnp.float32), keys_own, values_own)

    def pair_step(step_index, carried):
        inner, key_block, value_block = carried
        key_block, value_block = passed_along((key_block, value_block), "blk", 1)
        return (
            mix_turn((cycle_place - step_index) % cycle_size, inner, key_block, value_block),
            key_block,
            value_block,
        )

    mixed_sum = lax.fori_loop(1, cycle_size, pair_step, (mixed_start, keys_own, values_own))[0]
    mixed_low = (
        jnp.where(query_valid[:, :, None, None], mixed_sum, 0.0)
        .astype(jnp.bfloat16)
        .reshape(row_count, model_width)
    )
    part_cols = mixed_low
    branch = jnp.dot(
        part_cols,
        lax.all_gather(w_out, "cell", axis=0, tiled=True),
        preferred_element_type=jnp.float32,
    )
    middle = inputs + branch + out_bias
    normed2, ln2_pull = jax.vjp(layer_norm, middle, ln2_gain, ln2_bias)
    normed2_low = normed2.astype(jnp.bfloat16)
    gelu_exact = partial(jax.nn.gelu, approximate=False)
    ff_total = up_bias.shape[0]
    out_sum = jnp.zeros((row_count, model_width), jnp.float32)
    ffn_hidden = jnp.zeros((row_count, ff_total), jnp.bfloat16)
    up_piece = lax.all_gather(w_up, "cell", axis=0, tiled=True)
    down_piece = lax.all_gather(w_down, "cell", axis=0, tiled=True)
    pre_gelu = lax.dot_general(
        normed2_low, up_piece, col_contract, preferred_element_type=jnp.float32
    )
    pre_gelu = pre_gelu + up_bias
    activation, gelu_pull = jax.vjp(gelu_exact, pre_gelu)
    active_low = activation.astype(jnp.bfloat16)
    out_sum = out_sum + jnp.dot(active_low, down_piece, preferred_element_type=jnp.float32)
    grad_active = lax.dot_general(
        cot_rows, down_piece, col_contract, preferred_element_type=jnp.float32
    )
    pre_low = gelu_pull(grad_active)[0].astype(jnp.bfloat16)
    back_sum = jnp.dot(pre_low, up_piece, preferred_element_type=jnp.float32)
    ffn_hidden = lax.dynamic_update_slice_in_dim(ffn_hidden, active_low, jnp.int32(0), 1)
    out_sum, back_sum, pre_grads, hidden = (out_sum, back_sum, pre_low, ffn_hidden)
    out_hidden = (middle + out_sum + down_bias).astype(jnp.bfloat16).reshape(hidden_in.shape)
    grad_ln2, ln2_gain_part, ln2_bias_part = ln2_pull(back_sum)
    grad_middle = cot_rows.astype(jnp.float32) + grad_ln2
    branch_grad = grad_middle.astype(jnp.bfloat16)
    grad_mixed = lax.dot_general(
        branch_grad,
        lax.all_gather(w_out, "cell", axis=0, tiled=True),
        col_contract,
        preferred_element_type=jnp.float32,
    )
    grad_out = jnp.where(
        query_valid[:, :, None, None], grad_mixed.astype(jnp.bfloat16).reshape(head_shape), 0.0
    )
    delta = jnp.einsum("cqhd,cqhd->chq", grad_out.astype(jnp.float32), mixed_sum)

    def grad_step(step_index, carried):
        query_grad, key_block, value_block, key_grad, value_grad = carried
        owner_index = (cycle_place - step_index) % cycle_size
        weights = block_weights(key_block, owner_index)
        grad_weights = jnp.einsum(
            "cqhd,ckhd->chqk", grad_out, value_block, preferred_element_type=jnp.float32
        )
        score_grad = (weights * (grad_weights - delta[..., None])).astype(jnp.bfloat16)
        query_grad = (
            query_grad
            + jnp.einsum(
                "chqk,ckhd->cqhd", score_grad, key_block, preferred_element_type=jnp.float32
            )
            * score_scale
        )
        key_grad = (
            key_grad
            + jnp.einsum("chqk,cqhd->ckhd", score_grad, queries, preferred_element_type=jnp.float32)
            * score_scale
        )
        value_grad = value_grad + jnp.einsum(
            "chqk,cqhd->ckhd",
            weights.astype(jnp.bfloat16),
            grad_out,
            preferred_element_type=jnp.float32,
        )
        key_block, value_block, key_grad, value_grad = (
            passed_along(key_block, "blk", 1),
            passed_along(value_block, "blk", 1),
            passed_along(key_grad.astype(jnp.bfloat16), "blk", 1).astype(key_grad.dtype),
            passed_along(value_grad.astype(jnp.bfloat16), "blk", 1).astype(value_grad.dtype),
        )
        return (query_grad, key_block, value_block, key_grad, value_grad)

    zero_heads = jnp.zeros(head_shape, jnp.float32)
    cycle_done = lax.fori_loop(
        0, cycle_size, grad_step, (zero_heads, keys_own, values_own, zero_heads, zero_heads)
    )
    query_low = cycle_done[0].astype(jnp.bfloat16).reshape(row_count, model_width)
    key_low = cycle_done[3].astype(jnp.bfloat16).reshape(row_count, model_width)
    value_low = cycle_done[4].astype(jnp.bfloat16).reshape(row_count, model_width)
    grad_joined = jnp.concatenate([query_low, key_low, value_low], axis=1)
    grad_normed = lax.dot_general(
        grad_joined,
        lax.all_gather(w_qkv, "cell", axis=0, tiled=True),
        col_contract,
        preferred_element_type=jnp.float32,
    )
    grad_ln1, ln1_gain_part, ln1_bias_part = ln1_pull(grad_normed)
    in_grad = (grad_middle + grad_ln1).reshape(hidden_in.shape)
    qkv_term = lax.dot_general(
        normed_low, grad_joined, row_contract, preferred_element_type=jnp.float32
    )
    out_term = lax.dot_general(
        mixed_low, branch_grad, row_contract, preferred_element_type=jnp.float32
    )
    up_term = lax.dot_general(
        pre_grads, normed2_low, row_contract, preferred_element_type=jnp.float32
    )
    down_term = lax.dot_general(hidden, cot_rows, row_contract, preferred_element_type=jnp.float32)
    ffn_term = jnp.concatenate([up_term, down_term], axis=1).reshape(
        lax.axis_size("cell") * (model_width // lax.axis_size("cell")), ratio_ff * 2 * model_width
    )
    summed = lax.psum_scatter(
        jnp.concatenate([qkv_term, out_term, ffn_term], axis=1).astype(jnp.bfloat16),
        "cell",
        scatter_dimension=0,
        tiled=True,
    ).astype(jnp.float32)
    summed = lax.psum(summed.astype(jnp.bfloat16), "blk").astype(jnp.float32)
    own_rows = summed.shape[0]
    w_qkv_grad = summed[:, : 3 * model_width]
    w_out_grad = summed[:, 3 * model_width : 4 * model_width]
    ffn_grads = summed[:, 4 * model_width :].reshape(own_rows * ratio_ff, 2 * model_width)
    w_up_grad = ffn_grads[:, :model_width]
    w_down_grad = ffn_grads[:, model_width:]
    vectors = lax.psum(
        (
            ln1_gain_part,
            ln1_bias_part,
            jnp.sum(query_low, axis=0, dtype=jnp.float32),
            jnp.sum(value_low, axis=0, dtype=jnp.float32),
            jnp.sum(branch_grad, axis=0, dtype=jnp.float32),
            ln2_gain_part,
            ln2_bias_part,
            jnp.sum(pre_grads, axis=0, dtype=jnp.float32),
            jnp.sum(cot_rows, axis=0, dtype=jnp.float32),
        ),
        ("cell", "blk"),
    )
    return (
        out_hidden,
        in_grad,
        vectors[0],
        vectors[1],
        w_qkv_grad,
        vectors[2],
        vectors[3],
        w_out_grad,
        vectors[4],
        vectors[5],
        vectors[6],
        w_up_grad,
        vectors[7],
        w_down_grad,
        vectors[8],
    )


bf16 = jnp.bfloat16
f32 = jnp.float32
NN = (((1,), (0,)), ((), ()))
NT = (((1,), (1,)), ((), ()))
TN = (((0,), (0,)), ((), ()))
AXES = ("cell", "blk")
VMEM_LIMIT = 60 * 2**20
ROWS = 256
OFFSETS = (0, -1, -2, -3, -4, 1, 2, 3)


def swappable(mesh):
    return dict(mesh.shape) == {"cell": 16, "blk": 2}


def dot(a, b, dims):
    return lax.dot_general(a, b, dims, preferred_element_type=f32)


def params():
    return pltpu.CompilerParams(vmem_limit_bytes=VMEM_LIMIT)


def cost(flops, nbytes, trans=0):
    return pl.CostEstimate(
        flops=int(flops), bytes_accessed=int(nbytes), transcendentals=int(trans)
    )


def shape(dims, dtype):
    return jax.ShapeDtypeStruct(dims, dtype)


ANY = pl.BlockSpec(memory_space=pl.ANY)


def fixed(dims):
    return pl.BlockSpec(dims, lambda *_: (0,) * len(dims))


def rowed(rows, width):
    return pl.BlockSpec((rows, width), lambda i, *_: (i, 0))


class Ring:
    def __init__(self, sizes):
        self.cells, self.blks = sizes["cell"], sizes["blk"]
        self.chips = self.cells // 2
        depth = self.chips // 2
        self.order = [2 * z for z in range(depth)] + [2 * z + 1 for z in reversed(range(depth))]
        self.place = [self.order.index(c) for c in range(self.chips)]

    def permute(self, x, target):
        pairs = []
        for cell in range(self.cells):
            for blk in range(self.blks):
                to_cell, to_blk = target(cell, blk)
                pairs.append((cell * self.blks + blk, to_cell * self.blks + to_blk))
        return lax.ppermute(x, AXES, pairs)

    def shift(self, x, by):
        def target(cell, blk):
            chip, core = cell // 2, cell % 2
            way = 1 - 2 * ((core + blk) % 2)
            return self.order[(self.place[chip] + way * by) % self.chips] * 2 + core, blk

        return self.permute(x, target)

    def swap_core(self, x):
        return self.permute(x, lambda cell, blk: (cell ^ 1, blk))

    def swap_blk(self, x):
        return self.permute(x, lambda cell, blk: (cell, 1 - blk))

    def chips_of_slots(self, core):
        chip = lax.axis_index("cell") // 2
        way = 1 - 2 * ((core + lax.axis_index("blk")) % 2)
        place = jnp.array(self.place, jnp.int32)[chip]
        return jnp.array(self.order, jnp.int32)[
            (place + way * jnp.array(OFFSETS, jnp.int32)) % self.chips
        ]

    def gather(self, x, back):
        ahead = [x]
        for _ in range(4):
            ahead.append(self.shift(ahead[-1], 1))
        behind = []
        for k in range(1, 4):
            if k <= back:
                behind.append(self.shift(behind[-1] if behind else x, -1))
            else:
                behind.append(self.swap_blk(ahead[k]))
        return ahead + behind

    def reduce(self, parts, back):
        def added(terms):
            total = terms[0].astype(f32)
            for t in terms[1:]:
                total = total + t.astype(f32)
            return total

        across = {}
        for k in range(back + 1, 4):
            across[k] = self.swap_blk(added(parts(4 + k)).astype(bf16))
        run = added(parts(4)).astype(bf16)
        for k in (3, 2, 1):
            extra = [across[k]] if k in across else []
            run = added([self.shift(run, -1)] + parts(k) + extra).astype(bf16)
        last = [self.shift(run, -1)]
        run = None
        for k in range(back, 0, -1):
            moved = [] if run is None else [self.shift(run, 1)]
            run = added(moved + parts(4 + k)).astype(bf16)
        if run is not None:
            last.append(self.shift(run, 1))
        total = added(last + parts(0)).astype(bf16)
        return total.astype(f32) + self.swap_blk(total).astype(f32)

    def total(self, x):
        bit = 1
        while bit < self.cells * self.blks:
            other = bit
            x = x + self.permute(
                x,
                lambda cell, blk: divmod((cell * self.blks + blk) ^ other, self.blks),
            )
            bit *= 2
        return x


def norm_parts(x):
    mean = jnp.mean(x, axis=-1, keepdims=True)
    centered = x - mean
    var = jnp.mean(centered * centered, axis=-1, keepdims=True)
    scale = lax.rsqrt(var + epsilon)
    return centered * scale, scale


def norm_back(xh, scale, gain, grad):
    e = grad * gain
    return scale * (
        e - jnp.mean(e, axis=-1, keepdims=True) - xh * jnp.mean(e * xh, axis=-1, keepdims=True)
    )


def colsum(x):
    return jnp.sum(x, axis=0, keepdims=True)


def place_rows(slots, target, place_ref, sem, height, first=0):
    return [
        pltpu.make_async_copy(
            slot,
            target.at[pl.ds(pl.multiple_of(place_ref[first + i] * height, 16), height), :],
            sem.at[first + i],
        )
        for i, slot in enumerate(slots)
    ]


def qkv_kernel(n, place_ref, x_ref, gain_ref, bias_ref, qb_ref, vb_ref, *refs):
    slots, (a_ref, q_ref, k_ref, v_ref, w, sem) = refs[:n], refs[n:]
    height = slots[0].shape[0]
    width = x_ref.shape[1]
    copies = place_rows(slots, w, place_ref, sem, height)

    @pl.when(pl.program_id(0) == 0)
    def _():
        for c in copies:
            c.start()
        for c in copies:
            c.wait()

    xh, _ = norm_parts(x_ref[...].astype(f32))
    a = (xh * gain_ref[...] + bias_ref[...]).astype(bf16)
    a_ref[...] = a
    q_ref[...] = (dot(a, w[:, :width], NN) + qb_ref[...]).astype(bf16)
    k_ref[...] = dot(a, w[:, width : 2 * width], NN).astype(bf16)
    v_ref[...] = (dot(a, w[:, 2 * width :], NN) + vb_ref[...]).astype(bf16)


def qkv_call(place, x, gain, bias, qb, vb, slots):
    rows, width = x.shape
    n = len(slots)
    block = rowed(ROWS, width)
    vec = fixed((1, width))
    return pl.pallas_call(
        partial(qkv_kernel, n),
        grid_spec=pltpu.PrefetchScalarGridSpec(
            num_scalar_prefetch=1,
            grid=(rows // ROWS,),
            in_specs=[block, vec, vec, vec, vec] + [ANY] * n,
            out_specs=[block] * 4,
            scratch_shapes=[
                pltpu.VMEM((width, 3 * width), bf16),
                pltpu.SemaphoreType.DMA((n,)),
            ],
        ),
        out_shape=[shape((rows, width), bf16)] * 4,
        compiler_params=params(),
        cost_estimate=cost(6 * rows * width * width, 2 * width * (5 * rows + 3 * width)),
        name="qkv",
    )(place, x, gain, bias, qb, vb, *slots)


def attend_kernel(qrows, mask_ref, keep_ref, q_ref, k_ref, v_ref, o_ref, lse_ref):
    n = q_ref.shape[0]
    lane = lax.broadcasted_iota(jnp.int32, (n, 128), 1)
    k, v, mask = k_ref[...], v_ref[...], mask_ref[...]
    for half in range(2):
        mine = (lane < HEAD_DIM) if half == 0 else (lane >= HEAD_DIM)
        here = mine[:qrows]
        one = ((lane == HEAD_DIM) if half == 0 else (lane == 0))[:qrows]
        keys = jnp.where(mine, k.astype(f32), mask).astype(bf16)
        vals = jnp.where(mine, v.astype(f32), 1.0).astype(bf16)
        for i in range(n // qrows):
            rows = pl.ds(i * qrows, qrows)
            q = q_ref[rows, :].astype(f32) * (1.0 / math.sqrt(HEAD_DIM))
            q = jnp.where(here, q, jnp.where(one, 1.0, 0.0)).astype(bf16)
            s = dot(q, keys, NT)
            top = jnp.max(s, axis=1, keepdims=True)
            mixed = dot(jnp.exp(s - top).astype(bf16), vals, NN)
            total = pltpu.roll(mixed, HEAD_DIM, 1)
            o = (mixed / total * keep_ref[rows, :]).astype(bf16)
            if half == 0:
                o_ref[rows, :] = o
            else:
                o_ref[rows, :] = jnp.where(here, o, o_ref[rows, :])
            lse = jnp.transpose(top + jnp.log(total))
            first = half * HEAD_DIM
            lse_ref[half, :, rows] = lse[first : first + 1, :]


def attend_call(mask, keep, q, k, v, first, count, qrows=512):
    n = q.shape[0]
    block = pl.BlockSpec((n, 128), lambda h: (0, h + first))
    return pl.pallas_call(
        partial(attend_kernel, qrows),
        grid=(count,),
        in_specs=[fixed((n, 1)), fixed((n, 1)), block, block, block],
        out_specs=[
            pl.BlockSpec((n, 128), lambda h: (0, h)),
            pl.BlockSpec((2, 1, n), lambda h: (h, 0, 0)),
        ],
        out_shape=[shape((n, 128 * count), bf16), shape((2 * count, 1, n), f32)],
        compiler_params=params(),
        cost_estimate=cost(20 * count * n * n * 128, 8 * n * 128 * count, 2 * count * n * n),
        name="attend",
    )(mask, keep, q, k, v)


def attend_back_kernel(
    qrows, mask_ref, q_ref, k_ref, v_ref, o_ref, go_ref, lse_ref,
    gq_ref, gk_ref, gv_ref, sq_ref, sv_ref, gk_sum, gv_sum,
):
    n = q_ref.shape[0]
    lane = lax.broadcasted_iota(jnp.int32, (n, 128), 1)
    k, v, mask = k_ref[...], v_ref[...], mask_ref[...]
    scale = 1.0 / math.sqrt(HEAD_DIM)
    prod = jnp.transpose(o_ref[...].astype(f32) * go_ref[...].astype(f32))
    for half in range(2):
        mine = (lane < HEAD_DIM) if half == 0 else (lane >= HEAD_DIM)
        here = mine[:qrows]
        one = ((lane == HEAD_DIM) if half == 0 else (lane == 0))[:qrows]
        keys = jnp.where(mine, k.astype(f32), mask).astype(bf16)
        vals = jnp.where(mine, v, jnp.zeros_like(v))
        delta = colsum(prod[half * HEAD_DIM : (half + 1) * HEAD_DIM, :])
        for i in range(n // qrows):
            rows = pl.ds(i * qrows, qrows)
            q_raw, go = q_ref[rows, :], go_ref[rows, :]
            q = jnp.where(here, q_raw.astype(f32) * scale, jnp.where(one, 1.0, 0.0)).astype(bf16)
            p = jnp.exp(dot(keys, q, NT) - lse_ref[half, :, rows])
            gp = dot(vals, go, NT)
            gs = (p * (gp - delta[:, i * qrows : (i + 1) * qrows])).astype(bf16)
            gv = dot(p.astype(bf16), go, NN)
            gk = dot(gs, q_raw, NN)
            if i == 0:
                gv_sum[half], gk_sum[half] = gv, gk
            else:
                gv_sum[half] += gv
                gk_sum[half] += gk
            gq = (dot(gs, k, TN) * scale).astype(bf16)
            if half == 0:
                gq_ref[rows, :] = gq
            else:
                gq_ref[rows, :] = jnp.where(here, gq, gq_ref[rows, :])
    low = lane < HEAD_DIM
    gk_ref[...] = (jnp.where(low, gk_sum[0], gk_sum[1]) * scale).astype(bf16)
    gv = jnp.where(low, gv_sum[0], gv_sum[1]).astype(bf16)
    gv_ref[...] = gv
    sq_ref[...] = colsum(gq_ref[...].astype(f32))
    sv_ref[...] = colsum(gv.astype(f32))


def attend_back_call(mask, q, k, v, o, go, lse, first, count, qrows=512):
    n = q.shape[0]
    block = pl.BlockSpec((n, 128), lambda h: (0, h + first))
    own = pl.BlockSpec((n, 128), lambda h: (0, h))
    vec = pl.BlockSpec((1, 128), lambda h: (0, h))
    return pl.pallas_call(
        partial(attend_back_kernel, qrows),
        grid=(count,),
        in_specs=[
            fixed((n, 1)), block, block, block, own, block,
            pl.BlockSpec((2, 1, n), lambda h: (h, 0, 0)),
        ],
        out_specs=[own, own, own, vec, vec],
        out_shape=[shape((n, 128 * count), bf16)] * 3 + [shape((1, 128 * count), f32)] * 2,
        scratch_shapes=[pltpu.VMEM((2, n, 128), f32)] * 2,
        compiler_params=params(),
        cost_estimate=cost(32 * count * n * n * 128, 16 * n * 128 * count, 2 * count * n * n),
        name="attend_back",
    )(mask, q, k, v, o, go, lse)


def out_kernel(parts, place_ref, x_ref, bias_ref, gain_ref, shift_ref, own_ref, sib_ref, *refs):
    o_refs, (m_ref, b_ref, w, sem) = refs[:parts], refs[parts:]
    copies = wout_copies(own_ref, sib_ref, w, place_ref, sem)

    @pl.when(pl.program_id(0) == 0)
    def _():
        for c in copies:
            c.start()
        for c in copies:
            c.wait()

    m = x_ref[...].astype(f32) + bias_ref[...]
    first = 0
    for o_ref in o_refs:
        m = m + dot(o_ref[...], w[first : first + o_ref.shape[1], :], NN)
        first += o_ref.shape[1]
    m_ref[...] = m
    xh, _ = norm_parts(m)
    b_ref[...] = (xh * gain_ref[...] + shift_ref[...]).astype(bf16)


def wout_copies(own_ref, sib_ref, w, place_ref, sem):
    n = len(OFFSETS)
    height = own_ref.shape[0] // n
    return place_rows(
        [ref.at[pl.ds(height * i, height), :] for ref in (own_ref, sib_ref) for i in range(n)],
        w,
        place_ref,
        sem,
        height,
    )


def out_call(place, x, o_parts, own, sib, bias, gain, shift):
    rows, width = x.shape
    vec = fixed((1, width))
    block = rowed(ROWS, width)
    return pl.pallas_call(
        partial(out_kernel, len(o_parts)),
        grid_spec=pltpu.PrefetchScalarGridSpec(
            num_scalar_prefetch=1,
            grid=(rows // ROWS,),
            in_specs=[block, vec, vec, vec, ANY, ANY] + [rowed(ROWS, o.shape[1]) for o in o_parts],
            out_specs=[block, block],
            scratch_shapes=[
                pltpu.VMEM((width, width), bf16),
                pltpu.SemaphoreType.DMA((2 * len(OFFSETS),)),
            ],
        ),
        out_shape=[shape((rows, width), f32), shape((rows, width), bf16)],
        compiler_params=params(),
        cost_estimate=cost(4 * rows * width * width, width * (10 * rows + 2 * width)),
        name="out",
    )(place, x, bias, gain, shift, own, sib, *o_parts)


def gelu_both(z, gh):
    t = 1.0 / (1.0 + jnp.abs(z) * (0.3275911 / math.sqrt(2.0)))
    e = jnp.exp(z * z * -0.5)
    half = (0.254829592, -0.284496736, 1.421413741, -1.453152027, 1.061405429)
    tail = half[4] * 0.5
    for c in half[3::-1]:
        tail = tail * t + 0.5 * c
    tail = tail * t * e
    phi = jnp.where(z > 0, 1.0 - tail, tail)
    return z * phi, gh * (phi + z * e * (1.0 / math.sqrt(2.0 * math.pi)))


def ffn_kernel(n, later, *refs):
    b_own, b_sib, g_own, g_sib, ub_ref = refs[:5]
    slots = refs[5 : 5 + n]
    refs = refs[5 + n :]
    if later:
        acc_o, acc_g = refs[:2]
        refs = refs[2:]
        h_ref, gz_ref, sum_ref, oo_ref, go_ref, os_ref, gs_ref, us, ds, sem = refs
    else:
        h_ref, gz_ref, sum_ref, oo_ref, go_ref, us, ds, sem = refs
    units = us.shape[0] // n
    i = pl.program_id(0)
    near = i < pl.num_programs(0) // 2
    copies = []
    for s, slot in enumerate(slots):
        rows = pl.ds(s * units, units)
        copies.append(
            pltpu.make_async_copy(slot.at[pl.ds(0, units), :], us.at[rows, :], sem.at[0, s])
        )
        copies.append(
            pltpu.make_async_copy(slot.at[pl.ds(units, units), :], ds.at[rows, :], sem.at[1, s])
        )

    @pl.when(i == 0)
    def _():
        for c in copies:
            c.start()
        for c in copies:
            c.wait()
        sum_ref[...] = jnp.zeros_like(sum_ref)

    b = jnp.where(near, b_own[...], b_sib[...])
    g = jnp.where(near, g_own[...], g_sib[...])
    h, gz = gelu_both(dot(b, us[...], NT) + ub_ref[...], dot(g, ds[...], NT))
    h, gz = h.astype(bf16), gz.astype(bf16)
    h_ref[...] = h
    gz_ref[...] = gz
    sum_ref[...] += colsum(gz.astype(f32))
    out = dot(h, ds[...], NN)
    back = dot(gz, us[...], NN)
    if not later:
        oo_ref[...] = out
        go_ref[...] = back
        return
    out = out + acc_o[...]
    back = back + acc_g[...]

    @pl.when(near)
    def _():
        oo_ref[...] = out
        go_ref[...] = back

    @pl.when(jnp.logical_not(near))
    def _():
        os_ref[...] = out.astype(bf16)
        gs_ref[...] = back.astype(bf16)


def ffn_call(b_own, b_sib, g_own, g_sib, ub, slots, acc=None):
    rows, width = b_own.shape
    half = rows // ROWS
    n = len(slots)
    units = ub.shape[1]
    later = acc is not None
    near = pl.BlockSpec((ROWS, width), lambda i: (jnp.minimum(i, half - 1), 0))
    far = pl.BlockSpec((ROWS, width), lambda i: (jnp.maximum(i - half, 0), 0))
    both = rowed(ROWS, width)
    acc = list(acc or ())
    out_specs = [rowed(ROWS, units), rowed(ROWS, units), fixed((1, units))]
    out_shape = [shape((2 * rows, units), bf16)] * 2 + [shape((1, units), f32)]
    if later:
        out_specs += [near, near, far, far]
        out_shape += [shape((rows, width), f32)] * 2 + [shape((rows, width), bf16)] * 2
    else:
        out_specs += [both, both]
        out_shape += [shape((2 * rows, width), f32)] * 2
    return pl.pallas_call(
        partial(ffn_kernel, n, later),
        grid=(2 * half,),
        in_specs=[near, far, near, far, fixed((1, units))] + [ANY] * n + [both] * len(acc),
        out_specs=out_specs,
        out_shape=out_shape,
        scratch_shapes=[
            pltpu.VMEM((units, width), bf16),
            pltpu.VMEM((units, width), bf16),
            pltpu.SemaphoreType.DMA((2, n)),
        ],
        compiler_params=params(),
        cost_estimate=cost(
            24 * rows * width * units, rows * width * (24 + 16 * later), 4 * rows * units
        ),
        name="ffn",
    )(b_own, b_sib, g_own, g_sib, ub, *slots, *acc)


def ffn_weights_kernel(n, gz, h, b_own, b_sib, g_own, g_sib, *refs):
    outs = refs[:n]
    lv, rv, ov, lsem, rsem, osem = refs[n:]
    rows = b_own.shape[0]
    units = outs[0].shape[0] // 2
    loads = []
    for which, (left, parts) in enumerate(((gz, (b_own, b_sib)), (h, (g_own, g_sib)))):
        loads.append(pltpu.make_async_copy(left, lv.at[which], lsem.at[which]))
        for j, part in enumerate(parts):
            loads.append(
                pltpu.make_async_copy(
                    part, rv.at[which, pl.ds(j * rows, rows), :], rsem.at[which, j]
                )
            )
    for c in loads:
        c.start()
    stores = []
    step = 0
    for which in range(2):
        for c in loads[3 * which : 3 * which + 3]:
            c.wait()
        for pair in range(n // 2):
            slot = step % 2
            if step >= 2:
                for c in stores[2 * (step - 2) : 2 * (step - 2) + 2]:
                    c.wait()
            cols = pl.ds(pair * 2 * units, 2 * units)
            ov[slot] = dot(lv[which, :, cols], rv[which], TN).astype(bf16)
            for j in range(2):
                c = pltpu.make_async_copy(
                    ov.at[slot, pl.ds(j * units, units), :],
                    outs[2 * pair + j].at[pl.ds(which * units, units), :],
                    osem.at[slot, j],
                )
                c.start()
                stores.append(c)
            step += 1
    for c in stores[2 * (step - 2) :]:
        c.wait()


def ffn_weights_call(gz, h, b_own, b_sib, g_own, g_sib, n):
    rows, units = gz.shape
    width = b_own.shape[1]
    return pl.pallas_call(
        partial(ffn_weights_kernel, n),
        in_specs=[ANY] * 6,
        out_specs=[ANY] * n,
        out_shape=[shape((2 * units // n, width), bf16)] * n,
        scratch_shapes=[
            pltpu.VMEM((2, rows, units), bf16),
            pltpu.VMEM((2, rows, width), bf16),
            pltpu.VMEM((2, 2 * units // n, width), bf16),
            pltpu.SemaphoreType.DMA((2,)),
            pltpu.SemaphoreType.DMA((2, 2)),
            pltpu.SemaphoreType.DMA((2, 2)),
        ],
        compiler_params=params(),
        cost_estimate=cost(6 * rows * units * width, 4 * rows * (units + width)),
        name="ffn_weights",
    )(gz, h, b_own, b_sib, g_own, g_sib)


def mid_kernel(
    place_ref, oo_ref, os_ref, go_ref, gs_ref, m_ref, g_ref, keep_ref, db_ref, gain_ref, own_ref, sib_ref,
    hid_ref, gm_ref, gr_ref, gatt_ref, sums_ref, w, sem,
):
    copies = wout_copies(own_ref, sib_ref, w, place_ref, sem)

    @pl.when(pl.program_id(0) == 0)
    def _():
        for c in copies:
            c.start()
        for c in copies:
            c.wait()
        sums_ref[...] = jnp.zeros_like(sums_ref)

    m = m_ref[...]
    g = g_ref[...].astype(f32)
    hid_ref[...] = (m + oo_ref[...] + os_ref[...].astype(f32) + db_ref[...]).astype(bf16)
    gb = go_ref[...] + gs_ref[...].astype(f32)
    xh, scale = norm_parts(m)
    gm = g + norm_back(xh, scale, gain_ref[...], gb)
    gr = gm.astype(bf16)
    gm_ref[...] = gm
    gr_ref[...] = gr
    gatt_ref[...] = (dot(gr, w[...], NT) * keep_ref[...]).astype(bf16)
    sums_ref[0:1, :] += colsum(gb * xh)
    sums_ref[1:2, :] += colsum(gb)
    sums_ref[2:3, :] += colsum(gr.astype(f32))
    sums_ref[3:4, :] += colsum(g)


def mid_call(place, oo, os, go, gs, m, g, keep, db, gain, own, sib):
    rows, width = m.shape
    block = rowed(ROWS, width)
    vec = fixed((1, width))
    return pl.pallas_call(
        mid_kernel,
        grid_spec=pltpu.PrefetchScalarGridSpec(
            num_scalar_prefetch=1,
            grid=(rows // ROWS,),
            in_specs=[block] * 6 + [rowed(ROWS, 1), vec, vec, ANY, ANY],
            out_specs=[block] * 4 + [fixed((8, width))],
            scratch_shapes=[
                pltpu.VMEM((width, width), bf16),
                pltpu.SemaphoreType.DMA((2 * len(OFFSETS),)),
            ],
        ),
        out_shape=[
            shape((rows, width), bf16),
            shape((rows, width), f32),
            shape((rows, width), bf16),
            shape((rows, width), bf16),
            shape((8, width), f32),
        ],
        compiler_params=params(),
        cost_estimate=cost(4 * rows * width * width, width * (30 * rows + 2 * width)),
        name="mid",
    )(place, oo, os, go, gs, m, g, keep, db, gain, own, sib)


def att_weights_kernel(n, jobs, place_ref, *refs):
    lefts, rights = refs[: jobs[0]], refs[jobs[0] : jobs[0] + jobs[1]]
    refs = refs[jobs[0] + jobs[1] :]
    outs, refs = refs[: n + 1], refs[n + 1 :]
    lv, rv, ov, lsem, rsem, osem = refs
    table = jobs[2]
    height = outs[0].shape[0]
    loads = [pltpu.make_async_copy(r, lv.at[i], lsem.at[i]) for i, r in enumerate(lefts)]
    col = 0
    right_loads = []
    for i, r in enumerate(rights):
        right_loads.append(
            pltpu.make_async_copy(r, rv.at[:, pl.ds(col, r.shape[1])], rsem.at[i])
        )
        col += r.shape[1]
    loads[0].start()
    for c in right_loads:
        c.start()
    for c in loads[1:]:
        c.start()
    have = set()
    stores = []
    col = 0
    for step, (left, r) in enumerate(zip(table, rights, strict=True)):
        if left not in have:
            loads[left].wait()
            have.add(left)
        right_loads[step].wait()
        slot = step % 2
        if step >= 2:
            for c in stores[step - 2]:
                c.wait()
        wide = r.shape[1]
        cols = pl.ds(col, wide)
        ov[slot, :, pl.ds(0, wide)] = dot(lv[left], rv[:, cols], TN).astype(bf16)
        stores.append([])
        for i in range(2 * n):
            rows = pl.ds(pl.multiple_of(place_ref[i] * height, 16), height)
            goal = outs[i].at[:, cols] if i < n else outs[n].at[i - n, :, cols]
            c = pltpu.make_async_copy(ov.at[slot, rows, pl.ds(0, wide)], goal, osem.at[slot, i])
            c.start()
            stores[-1].append(c)
        col += wide
    for group in stores[-2:]:
        for c in group:
            c.wait()


def att_weights_call(place, lefts, rights, table):
    rows, width = lefts[0].shape
    n = len(OFFSETS)
    total = sum(r.shape[1] for r in rights)
    wide = max(r.shape[1] for r in rights)
    height = width // (2 * n)
    return pl.pallas_call(
        partial(att_weights_kernel, n, (len(lefts), len(rights), table)),
        grid_spec=pltpu.PrefetchScalarGridSpec(
            num_scalar_prefetch=1,
            grid=(1,),
            in_specs=[ANY] * (len(lefts) + len(rights)),
            out_specs=[ANY] * (n + 1),
            scratch_shapes=[
                pltpu.VMEM((len(lefts), rows, width), bf16),
                pltpu.VMEM((rows, total), bf16),
                pltpu.VMEM((2, width, wide), bf16),
                pltpu.SemaphoreType.DMA((len(lefts),)),
                pltpu.SemaphoreType.DMA((len(rights),)),
                pltpu.SemaphoreType.DMA((2, 2 * n)),
            ],
        ),
        out_shape=[shape((height, total), bf16)] * n + [shape((n, height, total), bf16)],
        compiler_params=params(),
        cost_estimate=cost(3 * rows * width * total, 2 * (rows + width) * total),
        name="att_weights",
    )(place, *lefts, *rights)


def in_kernel(n, pieces, place_ref, x_ref, gm_ref, gain_ref, *refs):
    grads, slots = refs[:pieces], refs[pieces : pieces + n]
    own_ref, send_ref, sums_ref, w, sem = refs[pieces + n :]
    height = slots[0].shape[0]
    copies = place_rows(slots, w, place_ref, sem, height)
    i = pl.program_id(0)

    @pl.when(i == 0)
    def _():
        for c in copies:
            c.start()
        for c in copies:
            c.wait()
        sums_ref[...] = jnp.zeros_like(sums_ref)

    ga = None
    col = 0
    for r in grads:
        part = dot(r[...], w[:, col : col + r.shape[1]], NT)
        ga = part if ga is None else ga + part
        col += r.shape[1]
    xh, scale = norm_parts(x_ref[...].astype(f32))
    res = gm_ref[...] + norm_back(xh, scale, gain_ref[...], ga)
    sums_ref[0:1, :] += colsum(ga * xh)
    sums_ref[1:2, :] += colsum(ga)
    half = pl.num_programs(0) // 2

    @pl.when(i < half)
    def _():
        send_ref[...] = res.astype(bf16)

    @pl.when(i >= half)
    def _():
        own_ref[...] = res


def in_call(place, x, gm, gain, grads, slots):
    rows, width = x.shape
    n = len(slots)
    half = rows // ROWS // 2

    def turned(w):
        return pl.BlockSpec((ROWS, w), lambda i, *_: ((i + half) % (2 * half), 0))

    return pl.pallas_call(
        partial(in_kernel, n, len(grads)),
        grid_spec=pltpu.PrefetchScalarGridSpec(
            num_scalar_prefetch=1,
            grid=(2 * half,),
            in_specs=[turned(width), turned(width), fixed((1, width))]
            + [turned(g.shape[1]) for g in grads]
            + [ANY] * n,
            out_specs=[
                pl.BlockSpec((ROWS, width), lambda i, *_: (jnp.maximum(i - half, 0), 0)),
                pl.BlockSpec((ROWS, width), lambda i, *_: (jnp.minimum(i, half - 1), 0)),
                fixed((8, width)),
            ],
            scratch_shapes=[
                pltpu.VMEM((width, 3 * width), bf16),
                pltpu.SemaphoreType.DMA((n,)),
            ],
        ),
        out_shape=[
            shape((rows // 2, width), f32),
            shape((rows // 2, width), bf16),
            shape((8, width), f32),
        ],
        compiler_params=params(),
        cost_estimate=cost(8 * rows * width * width, width * (14 * rows + 6 * width)),
        name="in",
    )(place, x, gm, gain, *grads, *slots)


def local_swapped(
    sizes, hidden_in, lengths, ln1_gain, ln1_bias, w_qkv, q_bias, v_bias, w_out, out_bias, ln2_gain, ln2_bias,
    w_up, up_bias, w_down, down_bias, cotangent,
):
    ring = Ring(sizes)
    blk = lax.axis_index("blk")
    core = lax.axis_index("cell") % 2
    genes, width = hidden_in.shape[1:]
    height = w_qkv.shape[0]
    units = w_up.shape[0]
    shards = ring.cells
    n = len(OFFSETS)

    def vec(v):
        return v.reshape(1, -1)

    def pick(x, which):
        return lax.dynamic_index_in_dim(x, which, 0, keepdims=False)

    x_own, x_send = pick(hidden_in, blk), pick(hidden_in, 1 - blk)
    x = jnp.concatenate([x_own, ring.swap_blk(x_send)], axis=0)
    qkv_own = ring.gather(w_qkv, 2)
    qkv_sib = [ring.swap_core(s) for s in qkv_own]
    rest_own = ring.gather(jnp.concatenate([w_up, w_down, w_out], axis=0), 1)
    g = jnp.concatenate([pick(cotangent, blk), ring.swap_blk(pick(cotangent, 1 - blk))], axis=0)
    g_sib = ring.swap_core(g)
    wo_own = jnp.concatenate([s[2 * units :] for s in rest_own], axis=0)
    wo_sib = ring.swap_core(wo_own)

    chips_own, chips_sib = ring.chips_of_slots(core), ring.chips_of_slots(1 - core)
    shard_own = 2 * chips_own + core
    shard_sib = 2 * chips_sib + 1 - core
    place = jnp.concatenate([shard_own, shard_sib])
    index = jnp.arange(genes, dtype=jnp.int32)
    index = jnp.concatenate([blk * genes + index, (1 - blk) * genes + index])
    keep = (index < pick(lengths, blk)).astype(f32)[:, None]
    mask = jnp.where(keep > 0, 0.0, far_below)

    a, q, k, v = qkv_call(
        place, x, vec(ln1_gain), vec(ln1_bias), vec(q_bias), vec(v_bias), qkv_own + qkv_sib
    )
    pairs = width // 128
    cuts = [(0, pairs // 2), (pairs // 2, pairs - pairs // 2)]
    attended = [attend_call(mask, keep, q, k, v, first, count) for first, count in cuts]
    o_parts = [t[0] for t in attended]
    m, b = out_call(
        place, x, o_parts, wo_own, wo_sib, vec(out_bias), vec(ln2_gain), vec(ln2_bias)
    )
    b_sib = ring.swap_core(b)
    ub = up_bias.reshape(shards, units)[shard_own]
    groups = ((0, 1, 2, 5), (3, 4, 6, 7))
    acc = None
    parts = [None] * n
    up_sums = [None] * n
    for group in groups:
        res = ffn_call(
            b, b_sib, g, g_sib, vec(jnp.concatenate([ub[s] for s in group])),
            [rest_own[s] for s in group], acc,
        )
        h, gz, up_sum = res[:3]
        acc = res[3:]
        made = ffn_weights_call(gz, h, b, b_sib, g, g_sib, len(group))
        for j, s in enumerate(group):
            parts[s] = made[j]
            up_sums[s] = up_sum[0, j * units : (j + 1) * units]
    oo, gb_own, os_send, gs_send = acc
    out_hidden, gm, gr, gatt, mid_sums = mid_call(
        place, oo, ring.swap_core(os_send), gb_own, ring.swap_core(gs_send), m, g, keep,
        vec(down_bias), vec(ln2_gain), wo_own, wo_sib,
    )
    ffn_rows = ring.reduce(lambda s: [parts[s]], 2)

    backs = [
        attend_back_call(mask, q, k, v, o_parts[i], gatt, attended[i][1], first, count)
        for i, (first, count) in enumerate(cuts)
    ]
    grads = [t[i] for i in range(3) for t in backs]
    made = att_weights_call(
        place, [a, jnp.concatenate(o_parts, axis=1)],
        grads + [gr], [0] * len(grads) + [1],
    )
    att_sib = ring.swap_core(made[n])
    att_rows = ring.reduce(lambda s: [made[s], att_sib[s]], 2)
    in_own, in_send, in_sums = in_call(place, x, gm, vec(ln1_gain), grads, qkv_own + qkv_sib)

    def home(own, sent):
        got = ring.swap_blk(sent).astype(own.dtype)
        return jnp.where(blk == 0, jnp.stack([own, got]), jnp.stack([got, own]))

    hidden = home(out_hidden[:genes], out_hidden[genes:])
    in_grad = home(in_own, in_send)
    up_rows = jnp.zeros((shards, units), f32).at[shard_own].set(jnp.stack(up_sums))
    early = ring.total(jnp.concatenate([mid_sums[:4].reshape(-1), up_rows.reshape(-1)]))
    late = ring.total(
        jnp.concatenate(
            [in_sums[:2].reshape(-1)]
            + [t[3].reshape(-1) for t in backs]
            + [t[4].reshape(-1) for t in backs]
        )
    )
    ln2_gain_g, ln2_bias_g, out_bias_g, down_bias_g = jnp.split(early[: 4 * width], 4)
    ln1_gain_g, ln1_bias_g, q_bias_g, v_bias_g = jnp.split(late, 4)
    return (
        hidden,
        in_grad,
        ln1_gain_g,
        ln1_bias_g,
        att_rows[:, : 3 * width],
        q_bias_g,
        v_bias_g,
        att_rows[:, 3 * width :],
        out_bias_g,
        ln2_gain_g,
        ln2_bias_g,
        ffn_rows[:units],
        early[4 * width :],
        ffn_rows[units:],
        down_bias_g,
    )


def solution(mesh):
    placed = (
        P("cell", "blk", None),
        P("cell"),
        P(),
        P(),
        P("cell", None),
        P(),
        P(),
        P("cell", None),
        P(),
        P(),
        P(),
        P("cell", None),
        P(),
        P("cell", None),
        P(),
        P("cell", "blk", None),
    )
    return jax.shard_map(
        partial(local_swapped, dict(mesh.shape)) if swappable(mesh) else local,
        mesh=mesh,
        in_specs=placed,
        out_specs=(
            P("cell", "blk", None),
            P("cell", "blk", None),
            P(),
            P(),
            P("cell", None),
            P(),
            P(),
            P("cell", None),
            P(),
            P(),
            P(),
            P("cell", None),
            P(),
            P("cell", None),
            P(),
        ),
        check_vma=False,
    )
```

```python
from functools import partial
import math

import jax
import jax.numpy as jnp
from jax import lax
from jax.experimental import pallas as pl
from jax.experimental.pallas import tpu as pltpu
from jax.sharding import PartitionSpec as P

HEAD_DIM = 64


epsilon = 1e-05
far_below = -1e30
row_contract = (((0,), (0,)), ((), ()))
col_contract = (((1,), (1,)), ((), ()))


def passed_along(x, axis, by):
    count = lax.axis_size(axis)
    return lax.ppermute(x, axis, [(i, (i + by) % count) for i in range(count)])


def layer_norm(source, gain_vec, shift_vec):
    row_mean = jnp.mean(source, axis=-1, keepdims=True)
    centered = source - row_mean
    row_var = jnp.mean(centered * centered, axis=-1, keepdims=True)
    return centered * lax.rsqrt(row_var + epsilon) * gain_vec + shift_vec


def local(
    hidden_in,
    lengths,
    ln1_gain,
    ln1_bias,
    w_qkv,
    q_bias,
    v_bias,
    w_out,
    out_bias,
    ln2_gain,
    ln2_bias,
    w_up,
    up_bias,
    w_down,
    down_bias,
    cotangent,
):
    cell_count, local_genes, model_width = hidden_in.shape
    row_count = cell_count * local_genes
    head_count = model_width // HEAD_DIM
    score_scale = 1.0 / math.sqrt(HEAD_DIM)
    cycle_size = lax.axis_size("blk")
    cycle_place = lax.axis_index("blk")
    ratio_ff = up_bias.shape[0] // model_width
    head_shape = (cell_count, local_genes, head_count, HEAD_DIM)
    stat_shape = (cell_count, head_count, local_genes)
    inputs = hidden_in.astype(jnp.float32).reshape(row_count, model_width)
    cot_rows = cotangent.reshape(row_count, model_width)
    gene_index = jnp.arange(local_genes, dtype=jnp.int32)
    query_valid = (cycle_place * local_genes + gene_index)[None, :] < lengths[:, None]
    normed, ln1_pull = jax.vjp(layer_norm, inputs, ln1_gain, ln1_bias)
    normed_low = normed.astype(jnp.bfloat16)
    part_cols = normed_low
    joined = jnp.dot(
        part_cols,
        lax.all_gather(w_qkv, "cell", axis=0, tiled=True),
        preferred_element_type=jnp.float32,
    )
    queries = (joined[:, :model_width] + q_bias).astype(jnp.bfloat16).reshape(head_shape)
    keys_own = joined[:, model_width : 2 * model_width].astype(jnp.bfloat16).reshape(head_shape)
    values_own = (joined[:, 2 * model_width :] + v_bias).astype(jnp.bfloat16).reshape(head_shape)

    def block_scores(key_block, owner_index):
        scores = (
            jnp.einsum("cqhd,ckhd->chqk", queries, key_block, preferred_element_type=jnp.float32)
            * score_scale
        )
        key_valid = (owner_index * local_genes + gene_index)[None, :] < lengths[:, None]
        return (scores, key_valid[:, None, None, :])

    def stats_turn(owner_index, carried, key_block):
        row_top, row_total = carried
        scores, is_valid = block_scores(key_block, owner_index)
        new_top = jnp.maximum(row_top, jnp.max(jnp.where(is_valid, scores, far_below), axis=-1))
        raised = jnp.where(is_valid, jnp.exp(scores - new_top[..., None]), 0.0)
        return (new_top, row_total * jnp.exp(row_top - new_top) + jnp.sum(raised, axis=-1))

    first_stats = stats_turn(
        cycle_place,
        (jnp.full(stat_shape, far_below, jnp.float32), jnp.zeros(stat_shape, jnp.float32)),
        keys_own,
    )

    def stats_step(step_index, carried):
        stats_now, key_block = carried
        key_block = passed_along(key_block, "blk", 1)
        return (
            stats_turn((cycle_place - step_index) % cycle_size, stats_now, key_block),
            key_block,
        )

    final_stats = lax.fori_loop(1, cycle_size, stats_step, (first_stats, keys_own))[0]
    log_total = final_stats[0] + jnp.log(final_stats[1])

    def block_weights(key_block, owner_index):
        scores, is_valid = block_scores(key_block, owner_index)
        return jnp.where(is_valid, jnp.exp(scores - log_total[..., None]), 0.0)

    def mix_turn(owner_index, mixed_sum, key_block, value_block):
        weights = block_weights(key_block, owner_index).astype(jnp.bfloat16)
        return mixed_sum + jnp.einsum(
            "chqk,ckhd->cqhd", weights, value_block, preferred_element_type=jnp.float32
        )

    mixed_start = mix_turn(cycle_place, jnp.zeros(head_shape, jnp.float32), keys_own, values_own)

    def pair_step(step_index, carried):
        inner, key_block, value_block = carried
        key_block, value_block = passed_along((key_block, value_block), "blk", 1)
        return (
            mix_turn((cycle_place - step_index) % cycle_size, inner, key_block, value_block),
            key_block,
            value_block,
        )

    mixed_sum = lax.fori_loop(1, cycle_size, pair_step, (mixed_start, keys_own, values_own))[0]
    mixed_low = (
        jnp.where(query_valid[:, :, None, None], mixed_sum, 0.0)
        .astype(jnp.bfloat16)
        .reshape(row_count, model_width)
    )
    part_cols = mixed_low
    branch = jnp.dot(
        part_cols,
        lax.all_gather(w_out, "cell", axis=0, tiled=True),
        preferred_element_type=jnp.float32,
    )
    middle = inputs + branch + out_bias
    normed2, ln2_pull = jax.vjp(layer_norm, middle, ln2_gain, ln2_bias)
    normed2_low = normed2.astype(jnp.bfloat16)
    gelu_exact = partial(jax.nn.gelu, approximate=False)
    ff_total = up_bias.shape[0]
    out_sum = jnp.zeros((row_count, model_width), jnp.float32)
    ffn_hidden = jnp.zeros((row_count, ff_total), jnp.bfloat16)
    up_piece = lax.all_gather(w_up, "cell", axis=0, tiled=True)
    down_piece = lax.all_gather(w_down, "cell", axis=0, tiled=True)
    pre_gelu = lax.dot_general(
        normed2_low, up_piece, col_contract, preferred_element_type=jnp.float32
    )
    pre_gelu = pre_gelu + up_bias
    activation, gelu_pull = jax.vjp(gelu_exact, pre_gelu)
    active_low = activation.astype(jnp.bfloat16)
    out_sum = out_sum + jnp.dot(active_low, down_piece, preferred_element_type=jnp.float32)
    grad_active = lax.dot_general(
        cot_rows, down_piece, col_contract, preferred_element_type=jnp.float32
    )
    pre_low = gelu_pull(grad_active)[0].astype(jnp.bfloat16)
    back_sum = jnp.dot(pre_low, up_piece, preferred_element_type=jnp.float32)
    ffn_hidden = lax.dynamic_update_slice_in_dim(ffn_hidden, active_low, jnp.int32(0), 1)
    out_sum, back_sum, pre_grads, hidden = (out_sum, back_sum, pre_low, ffn_hidden)
    out_hidden = (middle + out_sum + down_bias).astype(jnp.bfloat16).reshape(hidden_in.shape)
    grad_ln2, ln2_gain_part, ln2_bias_part = ln2_pull(back_sum)
    grad_middle = cot_rows.astype(jnp.float32) + grad_ln2
    branch_grad = grad_middle.astype(jnp.bfloat16)
    grad_mixed = lax.dot_general(
        branch_grad,
        lax.all_gather(w_out, "cell", axis=0, tiled=True),
        col_contract,
        preferred_element_type=jnp.float32,
    )
    grad_out = jnp.where(
        query_valid[:, :, None, None], grad_mixed.astype(jnp.bfloat16).reshape(head_shape), 0.0
    )
    delta = jnp.einsum("cqhd,cqhd->chq", grad_out.astype(jnp.float32), mixed_sum)

    def grad_step(step_index, carried):
        query_grad, key_block, value_block, key_grad, value_grad = carried
        owner_index = (cycle_place - step_index) % cycle_size
        weights = block_weights(key_block, owner_index)
        grad_weights = jnp.einsum(
            "cqhd,ckhd->chqk", grad_out, value_block, preferred_element_type=jnp.float32
        )
        score_grad = (weights * (grad_weights - delta[..., None])).astype(jnp.bfloat16)
        query_grad = (
            query_grad
            + jnp.einsum(
                "chqk,ckhd->cqhd", score_grad, key_block, preferred_element_type=jnp.float32
            )
            * score_scale
        )
        key_grad = (
            key_grad
            + jnp.einsum("chqk,cqhd->ckhd", score_grad, queries, preferred_element_type=jnp.float32)
            * score_scale
        )
        value_grad = value_grad + jnp.einsum(
            "chqk,cqhd->ckhd",
            weights.astype(jnp.bfloat16),
            grad_out,
            preferred_element_type=jnp.float32,
        )
        key_block, value_block, key_grad, value_grad = (
            passed_along(key_block, "blk", 1),
            passed_along(value_block, "blk", 1),
            passed_along(key_grad.astype(jnp.bfloat16), "blk", 1).astype(key_grad.dtype),
            passed_along(value_grad.astype(jnp.bfloat16), "blk", 1).astype(value_grad.dtype),
        )
        return (query_grad, key_block, value_block, key_grad, value_grad)

    zero_heads = jnp.zeros(head_shape, jnp.float32)
    cycle_done = lax.fori_loop(
        0, cycle_size, grad_step, (zero_heads, keys_own, values_own, zero_heads, zero_heads)
    )
    query_low = cycle_done[0].astype(jnp.bfloat16).reshape(row_count, model_width)
    key_low = cycle_done[3].astype(jnp.bfloat16).reshape(row_count, model_width)
    value_low = cycle_done[4].astype(jnp.bfloat16).reshape(row_count, model_width)
    grad_joined = jnp.concatenate([query_low, key_low, value_low], axis=1)
    grad_normed = lax.dot_general(
        grad_joined,
        lax.all_gather(w_qkv, "cell", axis=0, tiled=True),
        col_contract,
        preferred_element_type=jnp.float32,
    )
    grad_ln1, ln1_gain_part, ln1_bias_part = ln1_pull(grad_normed)
    in_grad = (grad_middle + grad_ln1).reshape(hidden_in.shape)
    qkv_term = lax.dot_general(
        normed_low, grad_joined, row_contract, preferred_element_type=jnp.float32
    )
    out_term = lax.dot_general(
        mixed_low, branch_grad, row_contract, preferred_element_type=jnp.float32
    )
    up_term = lax.dot_general(
        pre_grads, normed2_low, row_contract, preferred_element_type=jnp.float32
    )
    down_term = lax.dot_general(hidden, cot_rows, row_contract, preferred_element_type=jnp.float32)
    ffn_term = jnp.concatenate([up_term, down_term], axis=1).reshape(
        lax.axis_size("cell") * (model_width // lax.axis_size("cell")), ratio_ff * 2 * model_width
    )
    summed = lax.psum_scatter(
        jnp.concatenate([qkv_term, out_term, ffn_term], axis=1).astype(jnp.bfloat16),
        "cell",
        scatter_dimension=0,
        tiled=True,
    ).astype(jnp.float32)
    summed = lax.psum(summed.astype(jnp.bfloat16), "blk").astype(jnp.float32)
    own_rows = summed.shape[0]
    w_qkv_grad = summed[:, : 3 * model_width]
    w_out_grad = summed[:, 3 * model_width : 4 * model_width]
    ffn_grads = summed[:, 4 * model_width :].reshape(own_rows * ratio_ff, 2 * model_width)
    w_up_grad = ffn_grads[:, :model_width]
    w_down_grad = ffn_grads[:, model_width:]
    vectors = lax.psum(
        (
            ln1_gain_part,
            ln1_bias_part,
            jnp.sum(query_low, axis=0, dtype=jnp.float32),
            jnp.sum(value_low, axis=0, dtype=jnp.float32),
            jnp.sum(branch_grad, axis=0, dtype=jnp.float32),
            ln2_gain_part,
            ln2_bias_part,
            jnp.sum(pre_grads, axis=0, dtype=jnp.float32),
            jnp.sum(cot_rows, axis=0, dtype=jnp.float32),
        ),
        ("cell", "blk"),
    )
    return (
        out_hidden,
        in_grad,
        vectors[0],
        vectors[1],
        w_qkv_grad,
        vectors[2],
        vectors[3],
        w_out_grad,
        vectors[4],
        vectors[5],
        vectors[6],
        w_up_grad,
        vectors[7],
        w_down_grad,
        vectors[8],
    )


bf16 = jnp.bfloat16
f32 = jnp.float32
NN = (((1,), (0,)), ((), ()))
NT = (((1,), (1,)), ((), ()))
TN = (((0,), (0,)), ((), ()))
AXES = ("cell", "blk")
VMEM_LIMIT = 60 * 2**20
ROWS = 256
COST_PART = 50
OFFSETS = (0, -1, -2, -3, -4, 1, 2, 3)


def swappable(mesh):
    return dict(mesh.shape) == {"cell": 16, "blk": 2}


def dot(a, b, dims):
    return lax.dot_general(a, b, dims, preferred_element_type=f32)


def params():
    return pltpu.CompilerParams(vmem_limit_bytes=VMEM_LIMIT)


def cost(flops, nbytes, trans=0):
    return pl.CostEstimate(
        flops=int(flops) // COST_PART,
        bytes_accessed=int(nbytes) // COST_PART,
        transcendentals=int(trans) // COST_PART,
    )


def shape(dims, dtype):
    return jax.ShapeDtypeStruct(dims, dtype)


ANY = pl.BlockSpec(memory_space=pl.ANY)


def fixed(dims):
    return pl.BlockSpec(dims, lambda *_: (0,) * len(dims))


def rowed(rows, width):
    return pl.BlockSpec((rows, width), lambda i, *_: (i, 0))


class Ring:
    def __init__(self, sizes):
        self.cells, self.blks = sizes["cell"], sizes["blk"]
        self.chips = self.cells // 2
        depth = self.chips // 2
        self.order = [2 * z for z in range(depth)] + [2 * z + 1 for z in reversed(range(depth))]
        self.place = [self.order.index(c) for c in range(self.chips)]

    def permute(self, x, target):
        pairs = []
        for cell in range(self.cells):
            for blk in range(self.blks):
                to_cell, to_blk = target(cell, blk)
                pairs.append((cell * self.blks + blk, to_cell * self.blks + to_blk))
        return lax.ppermute(x, AXES, pairs)

    def shift(self, x, by):
        def target(cell, blk):
            chip, core = cell // 2, cell % 2
            way = 1 - 2 * ((core + blk) % 2)
            return self.order[(self.place[chip] + way * by) % self.chips] * 2 + core, blk

        return self.permute(x, target)

    def swap_core(self, x):
        return self.permute(x, lambda cell, blk: (cell ^ 1, blk))

    def swap_blk(self, x):
        return self.permute(x, lambda cell, blk: (cell, 1 - blk))

    def chips_of_slots(self, core):
        chip = lax.axis_index("cell") // 2
        way = 1 - 2 * ((core + lax.axis_index("blk")) % 2)
        place = jnp.array(self.place, jnp.int32)[chip]
        return jnp.array(self.order, jnp.int32)[
            (place + way * jnp.array(OFFSETS, jnp.int32)) % self.chips
        ]

    def gather(self, x, back):
        slots = [x] + [None] * 7
        for k in range(1, 5):
            slots[k] = self.shift(slots[k - 1], 1)
            if k <= back:
                slots[4 + k] = self.shift(slots[3 + k] if k > 1 else slots[0], -1)
            if k > back + 1:
                slots[3 + k] = self.swap_blk(slots[k - 1])
            slots = yield slots

    def reduce(self, parts, back):
        def added(terms):
            total = terms[0].astype(f32)
            for t in terms[1:]:
                total = total + t.astype(f32)
            return total.astype(bf16)

        ahead, behind = parts[4], [] if back == 0 else parts[4 + back]
        way = {"ahead": self.shift(added(ahead), -1)}
        if back:
            way["behind"] = self.shift(added(behind), 1)
        for k in range(3, back, -1):
            way[f"over{k}"] = self.swap_blk(added(parts[4 + k]))
        way = yield way
        for k in (3, 2, 1):
            extra = [way.pop(f"over{k}")] if f"over{k}" in way else []
            terms = [way["ahead"]] + parts[k] + extra
            way["ahead"] = self.shift(added(terms), -1)
            if back - (4 - k) >= 1:
                way["behind"] = self.shift(added([way["behind"]] + parts[4 + back - (4 - k)]), 1)
            way = yield way
        ends = [way["ahead"]] + ([way["behind"]] if back else [])
        total = added(ends + parts[0])
        way = yield {"own": total, "other": self.swap_blk(total)}
        yield way["own"].astype(f32) + way["other"].astype(f32)

    def total(self, x):
        bit = 1
        while bit < self.cells * self.blks:
            other = bit
            moved = self.permute(
                x, lambda cell, blk: divmod((cell * self.blks + blk) ^ other, self.blks)
            )
            x, moved = yield x, moved
            x = x + moved
            bit *= 2
        yield x


def norm_parts(x):
    mean = jnp.mean(x, axis=-1, keepdims=True)
    centered = x - mean
    var = jnp.mean(centered * centered, axis=-1, keepdims=True)
    scale = lax.rsqrt(var + epsilon)
    return centered * scale, scale


def norm_back(xh, scale, gain, grad):
    e = grad * gain
    return scale * (
        e - jnp.mean(e, axis=-1, keepdims=True) - xh * jnp.mean(e * xh, axis=-1, keepdims=True)
    )


def colsum(x):
    return jnp.sum(x, axis=0, keepdims=True)


def place_rows(slots, target, place_ref, sem, height, cols=None):
    cols = slice(None) if cols is None else cols
    return [
        pltpu.make_async_copy(
            slot.at[:, cols],
            target.at[pl.ds(pl.multiple_of(place_ref[i] * height, 16), height), cols],
            sem.at[i],
        )
        for i, slot in enumerate(slots)
    ]


def qkv_kernel(n, place_ref, x_ref, gain_ref, bias_ref, qb_ref, vb_ref, *refs):
    slots, (a_ref, q_ref, k_ref, v_ref, w, sem) = refs[:n], refs[n:]
    height = slots[0].shape[0]
    width = x_ref.shape[1]
    first = pl.program_id(0) == 0
    copies = [
        place_rows(slots, w, place_ref, sem.at[j], height, pl.ds(j * width, width))
        for j in range(3)
    ]

    @pl.when(first)
    def _():
        for group in copies:
            for c in group:
                c.start()

    xh, _ = norm_parts(x_ref[...].astype(f32))
    a_ref[...] = (xh * gain_ref[...] + bias_ref[...]).astype(bf16)
    for j, (res_ref, add_ref) in enumerate(((q_ref, qb_ref), (k_ref, None), (v_ref, vb_ref))):

        @pl.when(first)
        def _(group=copies[j]):
            for c in group:
                c.wait()

        res = dot(a_ref[...], w[:, j * width : (j + 1) * width], NN)
        if add_ref is not None:
            res = res + add_ref[...]
        res_ref[...] = res.astype(bf16)


def qkv_call(place, x, gain, bias, qb, vb, slots):
    rows, width = x.shape
    n = len(slots)
    block = rowed(ROWS, width)
    vec = fixed((1, width))
    return pl.pallas_call(
        partial(qkv_kernel, n),
        grid_spec=pltpu.PrefetchScalarGridSpec(
            num_scalar_prefetch=1,
            grid=(rows // ROWS,),
            in_specs=[block, vec, vec, vec, vec] + [ANY] * n,
            out_specs=[block] * 4,
            scratch_shapes=[
                pltpu.VMEM((width, 3 * width), bf16),
                pltpu.SemaphoreType.DMA((3, n)),
            ],
        ),
        out_shape=[shape((rows, width), bf16)] * 4,
        compiler_params=params(),
        cost_estimate=cost(6 * rows * width * width, 2 * width * (5 * rows + 3 * width)),
        name="qkv",
    )(place, x, gain, bias, qb, vb, *slots)


def attend_kernel(qrows, mask_ref, keep_ref, q_ref, k_ref, v_ref, o_ref, lse_ref):
    n = q_ref.shape[0]
    lane = lax.broadcasted_iota(jnp.int32, (n, 128), 1)
    k, v, mask = k_ref[...], v_ref[...], mask_ref[...]
    for half in range(2):
        mine = (lane < HEAD_DIM) if half == 0 else (lane >= HEAD_DIM)
        here = mine[:qrows]
        one = ((lane == HEAD_DIM) if half == 0 else (lane == 0))[:qrows]
        keys = jnp.where(mine, k.astype(f32), mask).astype(bf16)
        vals = jnp.where(mine, v.astype(f32), 1.0).astype(bf16)
        for i in range(n // qrows):
            rows = pl.ds(i * qrows, qrows)
            q = q_ref[rows, :].astype(f32) * (1.0 / math.sqrt(HEAD_DIM))
            q = jnp.where(here, q, jnp.where(one, 1.0, 0.0)).astype(bf16)
            s = dot(q, keys, NT)
            top = jnp.max(s, axis=1, keepdims=True)
            mixed = dot(jnp.exp(s - top).astype(bf16), vals, NN)
            total = pltpu.roll(mixed, HEAD_DIM, 1)
            o = (mixed / total * keep_ref[rows, :]).astype(bf16)
            if half == 0:
                o_ref[rows, :] = o
            else:
                o_ref[rows, :] = jnp.where(here, o, o_ref[rows, :])
            lse = jnp.transpose(top + jnp.log(total))
            first = half * HEAD_DIM
            lse_ref[half, :, rows] = lse[first : first + 1, :]


def attend_call(mask, keep, q, k, v, first, count, qrows=512):
    n = q.shape[0]
    block = pl.BlockSpec((n, 128), lambda h: (0, h + first))
    return pl.pallas_call(
        partial(attend_kernel, qrows),
        grid=(count,),
        in_specs=[fixed((n, 1)), fixed((n, 1)), block, block, block],
        out_specs=[
            pl.BlockSpec((n, 128), lambda h: (0, h)),
            pl.BlockSpec((2, 1, n), lambda h: (h, 0, 0)),
        ],
        out_shape=[shape((n, 128 * count), bf16), shape((2 * count, 1, n), f32)],
        compiler_params=params(),
        cost_estimate=cost(20 * count * n * n * 128, 8 * n * 128 * count, 2 * count * n * n),
        name="attend",
    )(mask, keep, q, k, v)


def attend_back_kernel(
    qrows, mask_ref, q_ref, k_ref, v_ref, o_ref, go_ref, lse_ref,
    gq_ref, gk_ref, gv_ref, sq_ref, sv_ref, gk_sum, gv_sum,
):
    n = q_ref.shape[0]
    lane = lax.broadcasted_iota(jnp.int32, (n, 128), 1)
    k, v, mask = k_ref[...], v_ref[...], mask_ref[...]
    scale = 1.0 / math.sqrt(HEAD_DIM)
    prod = jnp.transpose(o_ref[...].astype(f32) * go_ref[...].astype(f32))
    for half in range(2):
        mine = (lane < HEAD_DIM) if half == 0 else (lane >= HEAD_DIM)
        here = mine[:qrows]
        one = ((lane == HEAD_DIM) if half == 0 else (lane == 0))[:qrows]
        keys = jnp.where(mine, k.astype(f32), mask).astype(bf16)
        vals = jnp.where(mine, v, jnp.zeros_like(v))
        delta = colsum(prod[half * HEAD_DIM : (half + 1) * HEAD_DIM, :])
        for i in range(n // qrows):
            rows = pl.ds(i * qrows, qrows)
            q_raw, go = q_ref[rows, :], go_ref[rows, :]
            q = jnp.where(here, q_raw.astype(f32) * scale, jnp.where(one, 1.0, 0.0)).astype(bf16)
            p = jnp.exp(dot(keys, q, NT) - lse_ref[half, :, rows])
            gp = dot(vals, go, NT)
            gs = (p * (gp - delta[:, i * qrows : (i + 1) * qrows])).astype(bf16)
            gv = dot(p.astype(bf16), go, NN)
            gk = dot(gs, q_raw, NN)
            if i == 0:
                gv_sum[half], gk_sum[half] = gv, gk
            else:
                gv_sum[half] += gv
                gk_sum[half] += gk
            gq = (dot(gs, k, TN) * scale).astype(bf16)
            if half == 0:
                gq_ref[rows, :] = gq
            else:
                gq_ref[rows, :] = jnp.where(here, gq, gq_ref[rows, :])
    low = lane < HEAD_DIM
    gk_ref[...] = (jnp.where(low, gk_sum[0], gk_sum[1]) * scale).astype(bf16)
    gv = jnp.where(low, gv_sum[0], gv_sum[1]).astype(bf16)
    gv_ref[...] = gv
    sq_ref[...] = colsum(gq_ref[...].astype(f32))
    sv_ref[...] = colsum(gv.astype(f32))


def attend_back_call(mask, q, k, v, o, go, lse, first, count, qrows=512):
    n = q.shape[0]
    block = pl.BlockSpec((n, 128), lambda h: (0, h + first))
    own = pl.BlockSpec((n, 128), lambda h: (0, h))
    vec = pl.BlockSpec((1, 128), lambda h: (0, h))
    return pl.pallas_call(
        partial(attend_back_kernel, qrows),
        grid=(count,),
        in_specs=[
            fixed((n, 1)), block, block, block, own, block,
            pl.BlockSpec((2, 1, n), lambda h: (h, 0, 0)),
        ],
        out_specs=[own, own, own, vec, vec],
        out_shape=[shape((n, 128 * count), bf16)] * 3 + [shape((1, 128 * count), f32)] * 2,
        scratch_shapes=[pltpu.VMEM((2, n, 128), f32)] * 2,
        compiler_params=params(),
        cost_estimate=cost(32 * count * n * n * 128, 16 * n * 128 * count, 2 * count * n * n),
        name="attend_back",
    )(mask, q, k, v, o, go, lse)


def out_kernel(x_ref, bias_ref, gain_ref, shift_ref, w_ref, *refs):
    o_refs, (m_ref, b_ref) = refs[:-2], refs[-2:]
    m = x_ref[...].astype(f32) + bias_ref[...]
    first = 0
    for o_ref in o_refs:
        m = m + dot(o_ref[...], w_ref[first : first + o_ref.shape[1], :], NN)
        first += o_ref.shape[1]
    m_ref[...] = m
    xh, _ = norm_parts(m)
    b_ref[...] = (xh * gain_ref[...] + shift_ref[...]).astype(bf16)


def out_call(x, o_parts, w, bias, gain, shift):
    rows, width = x.shape
    vec = fixed((1, width))
    block = rowed(ROWS, width)
    return pl.pallas_call(
        out_kernel,
        grid=(rows // ROWS,),
        in_specs=[block, vec, vec, vec, fixed((width, width))]
        + [rowed(ROWS, o.shape[1]) for o in o_parts],
        out_specs=[block, block],
        out_shape=[shape((rows, width), f32), shape((rows, width), bf16)],
        compiler_params=params(),
        cost_estimate=cost(4 * rows * width * width, width * (10 * rows + 2 * width)),
        name="out",
    )(x, bias, gain, shift, w, *o_parts)


def gelu_both(z, gh):
    t = 1.0 / (1.0 + jnp.abs(z) * (0.3275911 / math.sqrt(2.0)))
    e = jnp.exp(z * z * -0.5)
    half = (0.254829592, -0.284496736, 1.421413741, -1.453152027, 1.061405429)
    tail = half[4] * 0.5
    for c in half[3::-1]:
        tail = tail * t + 0.5 * c
    tail = tail * t * e
    phi = jnp.where(z > 0, 1.0 - tail, tail)
    return z * phi, gh * (phi + z * e * (1.0 / math.sqrt(2.0 * math.pi)))


def ffn_kernel(n, later, *refs):
    b_own, b_sib, g_own, g_sib, ub_ref = refs[:5]
    slots = refs[5 : 5 + n]
    refs = refs[5 + n :]
    if later:
        acc_o, acc_g = refs[:2]
        refs = refs[2:]
        h_ref, gz_ref, sum_ref, oo_ref, go_ref, os_ref, gs_ref, us, ds, sem = refs
    else:
        h_ref, gz_ref, sum_ref, oo_ref, go_ref, us, ds, sem = refs
    units = us.shape[0] // n
    i = pl.program_id(0)
    near = i < pl.num_programs(0) // 2
    copies = []
    for s, slot in enumerate(slots):
        rows = pl.ds(s * units, units)
        copies.append(
            pltpu.make_async_copy(slot.at[pl.ds(0, units), :], us.at[rows, :], sem.at[0, s])
        )
        copies.append(
            pltpu.make_async_copy(slot.at[pl.ds(units, units), :], ds.at[rows, :], sem.at[1, s])
        )

    @pl.when(i == 0)
    def _():
        for c in copies:
            c.start()
        for c in copies:
            c.wait()
        sum_ref[...] = jnp.zeros_like(sum_ref)

    b = jnp.where(near, b_own[...], b_sib[...])
    g = jnp.where(near, g_own[...], g_sib[...])
    h, gz = gelu_both(dot(b, us[...], NT) + ub_ref[...], dot(g, ds[...], NT))
    h, gz = h.astype(bf16), gz.astype(bf16)
    h_ref[...] = h
    gz_ref[...] = gz
    sum_ref[...] += colsum(gz.astype(f32))
    out = dot(h, ds[...], NN)
    back = dot(gz, us[...], NN)
    if not later:
        oo_ref[...] = out
        go_ref[...] = back
        return
    out = out + acc_o[...]
    back = back + acc_g[...]

    @pl.when(near)
    def _():
        oo_ref[...] = out.astype(bf16)
        go_ref[...] = back.astype(bf16)

    @pl.when(jnp.logical_not(near))
    def _():
        os_ref[...] = out.astype(bf16)
        gs_ref[...] = back.astype(bf16)


def ffn_call(b_own, b_sib, g_own, g_sib, ub, slots, acc=None):
    rows, width = b_own.shape
    half = rows // ROWS
    n = len(slots)
    units = ub.shape[1]
    later = acc is not None
    near = pl.BlockSpec((ROWS, width), lambda i: (jnp.minimum(i, half - 1), 0))
    far = pl.BlockSpec((ROWS, width), lambda i: (jnp.maximum(i - half, 0), 0))
    both = rowed(ROWS, width)
    acc = list(acc or ())
    out_specs = [rowed(ROWS, units), rowed(ROWS, units), fixed((1, units))]
    out_shape = [shape((2 * rows, units), bf16)] * 2 + [shape((1, units), f32)]
    if later:
        out_specs += [near, near, far, far]
        out_shape += [shape((rows, width), bf16)] * 4
    else:
        out_specs += [both, both]
        out_shape += [shape((2 * rows, width), f32)] * 2
    return pl.pallas_call(
        partial(ffn_kernel, n, later),
        grid=(2 * half,),
        in_specs=[near, far, near, far, fixed((1, units))] + [ANY] * n + [both] * len(acc),
        out_specs=out_specs,
        out_shape=out_shape,
        scratch_shapes=[
            pltpu.VMEM((units, width), bf16),
            pltpu.VMEM((units, width), bf16),
            pltpu.SemaphoreType.DMA((2, n)),
        ],
        compiler_params=params(),
        cost_estimate=cost(
            24 * rows * width * units, rows * width * (24 + 16 * later), 4 * rows * units
        ),
        name="ffn",
    )(b_own, b_sib, g_own, g_sib, ub, *slots, *acc)


def ffn_weights_kernel(n, gz, h, b_own, b_sib, g_own, g_sib, *refs):
    outs = refs[:n]
    lv, rv, ov, lsem, rsem, osem = refs[n:]
    rows = b_own.shape[0]
    units = outs[0].shape[0] // 2
    loads = []
    for which, (left, parts) in enumerate(((gz, (b_own, b_sib)), (h, (g_own, g_sib)))):
        loads.append(pltpu.make_async_copy(left, lv.at[which], lsem.at[which]))
        for j, part in enumerate(parts):
            loads.append(
                pltpu.make_async_copy(
                    part, rv.at[which, pl.ds(j * rows, rows), :], rsem.at[which, j]
                )
            )
    for c in loads:
        c.start()
    stores = []
    step = 0
    for which in range(2):
        for c in loads[3 * which : 3 * which + 3]:
            c.wait()
        for pair in range(n // 2):
            slot = step % 2
            if step >= 2:
                for c in stores[2 * (step - 2) : 2 * (step - 2) + 2]:
                    c.wait()
            cols = pl.ds(pair * 2 * units, 2 * units)
            ov[slot] = dot(lv[which, :, cols], rv[which], TN).astype(bf16)
            for j in range(2):
                c = pltpu.make_async_copy(
                    ov.at[slot, pl.ds(j * units, units), :],
                    outs[2 * pair + j].at[pl.ds(which * units, units), :],
                    osem.at[slot, j],
                )
                c.start()
                stores.append(c)
            step += 1
    for c in stores[2 * (step - 2) :]:
        c.wait()


def ffn_weights_call(gz, h, b_own, b_sib, g_own, g_sib, n):
    rows, units = gz.shape
    width = b_own.shape[1]
    return pl.pallas_call(
        partial(ffn_weights_kernel, n),
        in_specs=[ANY] * 6,
        out_specs=[ANY] * n,
        out_shape=[shape((2 * units // n, width), bf16)] * n,
        scratch_shapes=[
            pltpu.VMEM((2, rows, units), bf16),
            pltpu.VMEM((2, rows, width), bf16),
            pltpu.VMEM((2, 2 * units // n, width), bf16),
            pltpu.SemaphoreType.DMA((2,)),
            pltpu.SemaphoreType.DMA((2, 2)),
            pltpu.SemaphoreType.DMA((2, 2)),
        ],
        compiler_params=params(),
        cost_estimate=cost(6 * rows * units * width, 4 * rows * (units + width)),
        name="ffn_weights",
    )(gz, h, b_own, b_sib, g_own, g_sib)


def mid_kernel(
    oo_ref, os_ref, go_ref, gs_ref, m_ref, g_ref, keep_ref, db_ref, gain_ref, w_ref,
    hid_ref, gr_ref, gatt_ref, sums_ref,
):
    @pl.when(pl.program_id(0) == 0)
    def _():
        sums_ref[...] = jnp.zeros_like(sums_ref)

    m = m_ref[...]
    g = g_ref[...].astype(f32)
    ff = oo_ref[...].astype(f32) + os_ref[...].astype(f32)
    hid_ref[...] = (m + ff + db_ref[...]).astype(bf16)
    gb = go_ref[...].astype(f32) + gs_ref[...].astype(f32)
    xh, scale = norm_parts(m)
    gm = g + norm_back(xh, scale, gain_ref[...], gb)
    gr = gm.astype(bf16)
    gr_ref[...] = gr
    gatt_ref[...] = (dot(gr, w_ref[...], NT) * keep_ref[...]).astype(bf16)
    sums_ref[0:1, :] += colsum(gb * xh)
    sums_ref[1:2, :] += colsum(gb)
    sums_ref[2:3, :] += colsum(gr.astype(f32))
    sums_ref[3:4, :] += colsum(g)


def mid_call(oo, os, go, gs, m, g, keep, db, gain, w):
    rows, width = m.shape
    block = rowed(ROWS, width)
    vec = fixed((1, width))
    return pl.pallas_call(
        mid_kernel,
        grid=(rows // ROWS,),
        in_specs=[block] * 6 + [rowed(ROWS, 1), vec, vec, fixed((width, width))],
        out_specs=[block] * 3 + [fixed((8, width))],
        out_shape=[
            shape((rows, width), bf16),
            shape((rows, width), bf16),
            shape((rows, width), bf16),
            shape((8, width), f32),
        ],
        compiler_params=params(),
        cost_estimate=cost(4 * rows * width * width, width * (30 * rows + 2 * width)),
        name="mid",
    )(oo, os, go, gs, m, g, keep, db, gain, w)


def att_weights_kernel(n, jobs, place_ref, *refs):
    lefts, rights = refs[: jobs[0]], refs[jobs[0] : jobs[0] + jobs[1]]
    refs = refs[jobs[0] + jobs[1] :]
    outs, refs = refs[: n + 1], refs[n + 1 :]
    lv, tv, rv, ov, lsem, rsem, osem = refs
    table = jobs[2]
    height = outs[0].shape[0]
    loads = [pltpu.make_async_copy(r, lv.at[i], lsem.at[i]) for i, r in enumerate(lefts)]
    col = 0
    right_loads = []
    for i, r in enumerate(rights):
        right_loads.append(
            pltpu.make_async_copy(r, rv.at[:, pl.ds(col, r.shape[1])], rsem.at[i])
        )
        col += r.shape[1]
    loads[0].start()
    for c in right_loads:
        c.start()
    for c in loads[1:]:
        c.start()
    have = set()
    stores = []
    col = 0
    for step, (left, r) in enumerate(zip(table, rights, strict=True)):
        if left not in have:
            loads[left].wait()
            tv[left] = jnp.transpose(lv[left])
            have.add(left)
        right_loads[step].wait()
        slot = step % 2
        if step >= 2:
            for c in stores[step - 2]:
                c.wait()
        wide = r.shape[1]
        cols = pl.ds(col, wide)
        ov[slot, :, pl.ds(0, wide)] = dot(tv[left], rv[:, cols], NN).astype(bf16)
        stores.append([])
        for i in range(2 * n):
            rows = pl.ds(pl.multiple_of(place_ref[i] * height, 16), height)
            goal = outs[i].at[:, cols] if i < n else outs[n].at[i - n, :, cols]
            c = pltpu.make_async_copy(ov.at[slot, rows, pl.ds(0, wide)], goal, osem.at[slot, i])
            c.start()
            stores[-1].append(c)
        col += wide
    for group in stores[-2:]:
        for c in group:
            c.wait()


def att_weights_call(place, lefts, rights, table):
    rows, width = lefts[0].shape
    n = len(OFFSETS)
    total = sum(r.shape[1] for r in rights)
    wide = max(r.shape[1] for r in rights)
    height = width // (2 * n)
    return pl.pallas_call(
        partial(att_weights_kernel, n, (len(lefts), len(rights), table)),
        grid_spec=pltpu.PrefetchScalarGridSpec(
            num_scalar_prefetch=1,
            grid=(1,),
            in_specs=[ANY] * (len(lefts) + len(rights)),
            out_specs=[ANY] * (n + 1),
            scratch_shapes=[
                pltpu.VMEM((len(lefts), rows, width), bf16),
                pltpu.VMEM((len(lefts), width, rows), bf16),
                pltpu.VMEM((rows, total), bf16),
                pltpu.VMEM((2, width, wide), bf16),
                pltpu.SemaphoreType.DMA((len(lefts),)),
                pltpu.SemaphoreType.DMA((len(rights),)),
                pltpu.SemaphoreType.DMA((2, 2 * n)),
            ],
        ),
        out_shape=[shape((height, total), bf16)] * n + [shape((n, height, total), bf16)],
        compiler_params=params(),
        cost_estimate=cost(3 * rows * width * total, 2 * (rows + width) * total),
        name="att_weights",
    )(place, *lefts, *rights)


def in_kernel(n, pieces, place_ref, x_ref, gr_ref, gain_ref, *refs):
    grads, slots = refs[:pieces], refs[pieces : pieces + n]
    res_ref, sums_ref, w, sem = refs[pieces + n :]
    height = slots[0].shape[0]
    copies = place_rows(slots, w, place_ref, sem, height)

    @pl.when(pl.program_id(0) == 0)
    def _():
        for c in copies:
            c.start()
        for c in copies:
            c.wait()
        sums_ref[...] = jnp.zeros_like(sums_ref)

    ga = None
    col = 0
    for r in grads:
        part = dot(r[...], w[:, col : col + r.shape[1]], NT)
        ga = part if ga is None else ga + part
        col += r.shape[1]
    xh, scale = norm_parts(x_ref[...].astype(f32))
    res = gr_ref[...].astype(f32) + norm_back(xh, scale, gain_ref[...], ga)
    sums_ref[0:1, :] += colsum(ga * xh)
    sums_ref[1:2, :] += colsum(ga)
    res_ref[...] = res.astype(res_ref.dtype)


def in_call(place, x, gr, gain, grads, slots, part, dtype):
    rows, width = x.shape
    n = len(slots)
    half = rows // ROWS // 2

    def piece(w):
        return pl.BlockSpec((ROWS, w), lambda i, *_: (i + part * half, 0))

    return pl.pallas_call(
        partial(in_kernel, n, len(grads)),
        grid_spec=pltpu.PrefetchScalarGridSpec(
            num_scalar_prefetch=1,
            grid=(half,),
            in_specs=[piece(width), piece(width), fixed((1, width))]
            + [piece(g.shape[1]) for g in grads]
            + [ANY] * n,
            out_specs=[rowed(ROWS, width), fixed((8, width))],
            scratch_shapes=[
                pltpu.VMEM((width, 3 * width), bf16),
                pltpu.SemaphoreType.DMA((n,)),
            ],
        ),
        out_shape=[shape((rows // 2, width), dtype), shape((8, width), f32)],
        compiler_params=params(),
        cost_estimate=cost(4 * rows * width * width, width * (7 * rows + 6 * width)),
        name="in",
    )(place, x, gr, gain, *grads, *slots)


def fence(*trees):
    return lax.optimization_barrier(trees)


def local_swapped(
    sizes, hidden_in, lengths, ln1_gain, ln1_bias, w_qkv, q_bias, v_bias, w_out, out_bias, ln2_gain, ln2_bias,
    w_up, up_bias, w_down, down_bias, cotangent,
):
    ring = Ring(sizes)
    blk = lax.axis_index("blk")
    core = lax.axis_index("cell") % 2
    genes, width = hidden_in.shape[1:]
    units = w_up.shape[0]
    shards = ring.cells
    n = len(OFFSETS)

    def vec(v):
        return v.reshape(1, -1)

    def pick(x, which):
        return lax.dynamic_index_in_dim(x, which, 0, keepdims=False)

    chips_own, chips_sib = ring.chips_of_slots(core), ring.chips_of_slots(1 - core)
    shard_own = 2 * chips_own + core
    shard_sib = 2 * chips_sib + 1 - core
    place = jnp.concatenate([shard_own, shard_sib])
    index = jnp.arange(genes, dtype=jnp.int32)
    index = jnp.concatenate([blk * genes + index, (1 - blk) * genes + index])
    keep = (index < pick(lengths, blk)).astype(f32)[:, None]
    mask = jnp.where(keep > 0, 0.0, far_below)

    x_got = ring.swap_blk(pick(hidden_in, 1 - blk))
    steps = ring.gather(w_qkv, 2)
    qkv_own = next(steps)
    w_pair = jnp.concatenate([w_up, w_down], axis=0)
    qkv_own[1], qkv_own[5] = fence(qkv_own[1], qkv_own[5])
    qkv_own = steps.send(qkv_own)
    qkv_own[2], qkv_own[6], x_got = fence(qkv_own[2], qkv_own[6], x_got)
    qkv_own = steps.send(qkv_own)
    x = jnp.concatenate([pick(hidden_in, blk), x_got], axis=0)
    qkv_own[3], x = fence(qkv_own[3], x)
    qkv_own = steps.send(qkv_own)
    qkv_own[4], w_pair, w_out = fence(qkv_own[4], w_pair, w_out)
    pair = [w_pair, ring.shift(w_pair, 1)] + [None] * 6
    w_out = lax.all_gather(w_out, "cell", axis=0, tiled=True)
    qkv_sib = [ring.swap_core(s) for s in qkv_own]
    g_send, qkv_sib[7] = fence(cotangent, qkv_sib[7])
    g_got = ring.swap_blk(pick(g_send, 1 - blk))

    a, q, k, v = qkv_call(
        place, x, vec(ln1_gain), vec(ln1_bias), vec(q_bias), vec(v_bias), qkv_own + qkv_sib
    )
    pairs = width // 128
    cuts = [(0, 4 * pairs // 10), (4 * pairs // 10, 2 * pairs // 10)]
    cuts.append((sum(cuts[1]), pairs - sum(cuts[1])))
    q, k, v, pair[1], g_got = fence(q, k, v, pair[1], g_got)
    pair[2] = ring.shift(pair[1], 1)
    attended = [attend_call(mask, keep, q, k, v, *cuts[0])]
    q, k, v, attended, pair[2] = fence(q, k, v, attended, pair[2])
    g = jnp.concatenate([pick(cotangent, blk), g_got], axis=0)
    g_sib = ring.swap_core(g)
    pair[3] = ring.shift(pair[2], 1)
    pair[6] = ring.swap_blk(pair[2])
    attended += [attend_call(mask, keep, q, k, v, *cut) for cut in cuts[1:]]
    attended, pair[0], pair[3] = fence(attended, pair[0], pair[3])
    o_parts = [t[0] for t in attended]
    pair[4] = ring.shift(pair[3], 1)
    pair[5] = ring.shift(pair[0], -1)
    pair[7] = ring.swap_blk(pair[3])
    m, b = out_call(x, o_parts, w_out, vec(out_bias), vec(ln2_gain), vec(ln2_bias))
    m, b, pair[6], g_sib = fence(m, b, pair[6], g_sib)
    b_sib = ring.swap_core(b)

    ub = up_bias.reshape(shards, units)[shard_own]
    near, far = (0, 1, 2, 3), (4, 5, 6, 7)
    ub_near, ub_far = [vec(jnp.concatenate([ub[s] for s in group])) for group in (near, far)]
    h_near, gz_near, sum_near, *acc = ffn_call(
        b, b_sib, g, g_sib, ub_near, [pair[s] for s in near]
    )
    h_far, gz_far, sum_far, oo, gb_own, os_send, gs_send = ffn_call(
        b, b_sib, g, g_sib, ub_far, [pair[s] for s in far], acc
    )
    up_sums = dict(
        zip(near + far, jnp.split(sum_near[0], 4) + jnp.split(sum_far[0], 4), strict=True)
    )
    mine = shard_own[None, :] == jnp.arange(shards, dtype=jnp.int32)[:, None]
    up_rows = jnp.sum(
        jnp.where(mine[:, :, None], jnp.stack([up_sums[s] for s in range(n)])[None], 0.0), axis=1
    )
    parts = [None] * n
    made = ffn_weights_call(gz_far, h_far, b, b_sib, g, g_sib, len(far))
    os_got, gs_got = ring.swap_core(os_send), ring.swap_core(gs_send)
    made, oo, os_got, gs_got = fence(made, oo, os_got, gs_got)
    for s, t in zip(far, made, strict=True):
        parts[s] = [t]
    steps = ring.reduce(parts, 1)
    way = next(steps)
    out_hidden, gr, gatt, mid_sums = mid_call(
        oo, os_got, gb_own, gs_got, m, g, keep, vec(down_bias), vec(ln2_gain), w_out
    )
    gr, gatt, gz_near = fence(gr, gatt, gz_near)
    hid_got = ring.swap_blk(out_hidden[genes:])
    made = ffn_weights_call(gz_near, h_near, b, b_sib, g, g_sib, len(near))
    made, gatt, way["ahead"], way["over3"] = fence(made, gatt, way["ahead"], way["over3"])
    for s, t in zip(near, made, strict=True):
        parts[s] = [t]
    way = steps.send(way)

    def back(part, gatt):
        return attend_back_call(mask, q, k, v, o_parts[part], gatt, attended[part][1], *cuts[part])

    backs = [back(0, gatt)]
    backs, gatt = fence(backs, gatt)
    backs.append(back(1, gatt))
    backs, gatt, way = fence(backs, gatt, way)
    way = steps.send(way)
    first = att_weights_call(
        place, [a, jnp.concatenate(o_parts, axis=1)],
        [t[i] for i in range(3) for t in backs] + [gr], [0] * 6 + [1],
    )
    first, gatt, way = fence(first, gatt, way)
    way = steps.send(way)
    first_sib = ring.swap_core(first[n])
    backs.append(back(2, gatt))
    backs, way, first, first_sib, hid_got, up_rows = fence(
        backs, way, first, first_sib, hid_got, up_rows
    )
    way = steps.send(way)
    steps_first = ring.reduce([[first[s], first_sib[s]] for s in range(n)], 3)
    way_first = next(steps_first)
    second = att_weights_call(place, [a], list(backs[2][:3]), [0] * 3)
    second_sib = ring.swap_core(second[n])
    grads = [t[i] for i in range(3) for t in backs]
    second, grads, way_first = fence(second, grads, way_first)
    way_first = steps_first.send(way_first)
    steps_second = ring.reduce([[second[s], second_sib[s]] for s in range(n)], 3)
    way_second = next(steps_second)
    weights = qkv_own + qkv_sib
    in_send, in_sums_send = in_call(place, x, gr, vec(ln1_gain), grads, weights, 1, bf16)
    in_send, grads, way_first, way_second = fence(in_send, grads, way_first, way_second)
    way_first = steps_first.send(way_first)
    way_second = steps_second.send(way_second)
    in_got = ring.swap_blk(in_send)
    in_own, in_sums = in_call(place, x, gr, vec(ln1_gain), grads, weights, 0, f32)
    in_own, in_sums, in_sums_send, way_first, way_second = fence(
        in_own, in_sums, in_sums_send, way_first, way_second
    )
    way_first = steps_first.send(way_first)
    way_second = steps_second.send(way_second)
    ln1_sums = (in_sums + in_sums_send)[:2].reshape(-1)
    steps_sums = ring.total(
        jnp.concatenate(
            [mid_sums[:4].reshape(-1), ln1_sums, up_rows.reshape(-1)]
            + [t[i].reshape(-1) for i in (3, 4) for t in backs]
        )
    )
    sums = next(steps_sums)
    sums = steps_sums.send(sums)
    way_first, way_second, sums, in_got = fence(way_first, way_second, sums, in_got)
    way_first = steps_first.send(way_first)
    way_second = steps_second.send(way_second)
    sums = steps_sums.send(sums)
    sums = steps_sums.send(sums)
    way_first, way_second, sums = fence(way_first, way_second, sums)
    ffn_rows = steps.send(way)
    first_rows = steps_first.send(way_first)
    way_second = steps_second.send(way_second)
    sums = steps_sums.send(sums)
    sums = steps_sums.send(sums)
    second_rows = steps_second.send(way_second)

    def home(own, got):
        got = got.astype(own.dtype)
        return jnp.where(blk == 0, jnp.stack([own, got]), jnp.stack([got, own]))

    hidden = home(out_hidden[:genes], hid_got)
    in_grad = home(in_own, in_got)
    ln2_gain_g, ln2_bias_g, out_bias_g, down_bias_g, ln1_gain_g, ln1_bias_g = [
        sums[i * width : (i + 1) * width] for i in range(6)
    ]
    up_bias_g = sums[6 * width : 6 * width + shards * units]
    q_bias_g, v_bias_g = jnp.split(sums[6 * width + shards * units :], 2)
    wide = cuts[2][0] * 128
    rest = width - wide
    w_qkv_grad = jnp.concatenate(
        [
            t
            for i in range(3)
            for t in (
                first_rows[:, i * wide : (i + 1) * wide],
                second_rows[:, i * rest : (i + 1) * rest],
            )
        ],
        axis=1,
    )
    return (
        hidden,
        in_grad,
        ln1_gain_g,
        ln1_bias_g,
        w_qkv_grad,
        q_bias_g,
        v_bias_g,
        first_rows[:, 3 * wide :],
        out_bias_g,
        ln2_gain_g,
        ln2_bias_g,
        ffn_rows[:units],
        up_bias_g,
        ffn_rows[units:],
        down_bias_g,
    )


def solution(mesh):
    placed = (
        P("cell", "blk", None),
        P("cell"),
        P(),
        P(),
        P("cell", None),
        P(),
        P(),
        P("cell", None),
        P(),
        P(),
        P(),
        P("cell", None),
        P(),
        P("cell", None),
        P(),
        P("cell", "blk", None),
    )
    return jax.shard_map(
        partial(local_swapped, dict(mesh.shape)) if swappable(mesh) else local,
        mesh=mesh,
        in_specs=placed,
        out_specs=(
            P("cell", "blk", None),
            P("cell", "blk", None),
            P(),
            P(),
            P("cell", None),
            P(),
            P(),
            P("cell", None),
            P(),
            P(),
            P(),
            P("cell", None),
            P(),
            P("cell", None),
            P(),
        ),
        check_vma=False,
    )
```

```python
from functools import partial
import math

import jax
import jax.numpy as jnp
from jax import lax
from jax.experimental import pallas as pl
from jax.experimental.pallas import tpu as pltpu
from jax.sharding import PartitionSpec as P

HEAD_DIM = 64


epsilon = 1e-05
far_below = -1e30
row_contract = (((0,), (0,)), ((), ()))
col_contract = (((1,), (1,)), ((), ()))


def passed_along(x, axis, by):
    count = lax.axis_size(axis)
    return lax.ppermute(x, axis, [(i, (i + by) % count) for i in range(count)])


def layer_norm(source, gain_vec, shift_vec):
    row_mean = jnp.mean(source, axis=-1, keepdims=True)
    centered = source - row_mean
    row_var = jnp.mean(centered * centered, axis=-1, keepdims=True)
    return centered * lax.rsqrt(row_var + epsilon) * gain_vec + shift_vec


def local(
    hidden_in,
    lengths,
    ln1_gain,
    ln1_bias,
    w_qkv,
    q_bias,
    v_bias,
    w_out,
    out_bias,
    ln2_gain,
    ln2_bias,
    w_up,
    up_bias,
    w_down,
    down_bias,
    cotangent,
):
    cell_count, local_genes, model_width = hidden_in.shape
    row_count = cell_count * local_genes
    head_count = model_width // HEAD_DIM
    score_scale = 1.0 / math.sqrt(HEAD_DIM)
    cycle_size = lax.axis_size("blk")
    cycle_place = lax.axis_index("blk")
    ratio_ff = up_bias.shape[0] // model_width
    head_shape = (cell_count, local_genes, head_count, HEAD_DIM)
    stat_shape = (cell_count, head_count, local_genes)
    inputs = hidden_in.astype(jnp.float32).reshape(row_count, model_width)
    cot_rows = cotangent.reshape(row_count, model_width)
    gene_index = jnp.arange(local_genes, dtype=jnp.int32)
    query_valid = (cycle_place * local_genes + gene_index)[None, :] < lengths[:, None]
    normed, ln1_pull = jax.vjp(layer_norm, inputs, ln1_gain, ln1_bias)
    normed_low = normed.astype(jnp.bfloat16)
    part_cols = normed_low
    joined = jnp.dot(
        part_cols,
        lax.all_gather(w_qkv, "cell", axis=0, tiled=True),
        preferred_element_type=jnp.float32,
    )
    queries = (joined[:, :model_width] + q_bias).astype(jnp.bfloat16).reshape(head_shape)
    keys_own = joined[:, model_width : 2 * model_width].astype(jnp.bfloat16).reshape(head_shape)
    values_own = (joined[:, 2 * model_width :] + v_bias).astype(jnp.bfloat16).reshape(head_shape)

    def block_scores(key_block, owner_index):
        scores = (
            jnp.einsum("cqhd,ckhd->chqk", queries, key_block, preferred_element_type=jnp.float32)
            * score_scale
        )
        key_valid = (owner_index * local_genes + gene_index)[None, :] < lengths[:, None]
        return (scores, key_valid[:, None, None, :])

    def stats_turn(owner_index, carried, key_block):
        row_top, row_total = carried
        scores, is_valid = block_scores(key_block, owner_index)
        new_top = jnp.maximum(row_top, jnp.max(jnp.where(is_valid, scores, far_below), axis=-1))
        raised = jnp.where(is_valid, jnp.exp(scores - new_top[..., None]), 0.0)
        return (new_top, row_total * jnp.exp(row_top - new_top) + jnp.sum(raised, axis=-1))

    first_stats = stats_turn(
        cycle_place,
        (jnp.full(stat_shape, far_below, jnp.float32), jnp.zeros(stat_shape, jnp.float32)),
        keys_own,
    )

    def stats_step(step_index, carried):
        stats_now, key_block = carried
        key_block = passed_along(key_block, "blk", 1)
        return (
            stats_turn((cycle_place - step_index) % cycle_size, stats_now, key_block),
            key_block,
        )

    final_stats = lax.fori_loop(1, cycle_size, stats_step, (first_stats, keys_own))[0]
    log_total = final_stats[0] + jnp.log(final_stats[1])

    def block_weights(key_block, owner_index):
        scores, is_valid = block_scores(key_block, owner_index)
        return jnp.where(is_valid, jnp.exp(scores - log_total[..., None]), 0.0)

    def mix_turn(owner_index, mixed_sum, key_block, value_block):
        weights = block_weights(key_block, owner_index).astype(jnp.bfloat16)
        return mixed_sum + jnp.einsum(
            "chqk,ckhd->cqhd", weights, value_block, preferred_element_type=jnp.float32
        )

    mixed_start = mix_turn(cycle_place, jnp.zeros(head_shape, jnp.float32), keys_own, values_own)

    def pair_step(step_index, carried):
        inner, key_block, value_block = carried
        key_block, value_block = passed_along((key_block, value_block), "blk", 1)
        return (
            mix_turn((cycle_place - step_index) % cycle_size, inner, key_block, value_block),
            key_block,
            value_block,
        )

    mixed_sum = lax.fori_loop(1, cycle_size, pair_step, (mixed_start, keys_own, values_own))[0]
    mixed_low = (
        jnp.where(query_valid[:, :, None, None], mixed_sum, 0.0)
        .astype(jnp.bfloat16)
        .reshape(row_count, model_width)
    )
    part_cols = mixed_low
    branch = jnp.dot(
        part_cols,
        lax.all_gather(w_out, "cell", axis=0, tiled=True),
        preferred_element_type=jnp.float32,
    )
    middle = inputs + branch + out_bias
    normed2, ln2_pull = jax.vjp(layer_norm, middle, ln2_gain, ln2_bias)
    normed2_low = normed2.astype(jnp.bfloat16)
    gelu_exact = partial(jax.nn.gelu, approximate=False)
    ff_total = up_bias.shape[0]
    out_sum = jnp.zeros((row_count, model_width), jnp.float32)
    ffn_hidden = jnp.zeros((row_count, ff_total), jnp.bfloat16)
    up_piece = lax.all_gather(w_up, "cell", axis=0, tiled=True)
    down_piece = lax.all_gather(w_down, "cell", axis=0, tiled=True)
    pre_gelu = lax.dot_general(
        normed2_low, up_piece, col_contract, preferred_element_type=jnp.float32
    )
    pre_gelu = pre_gelu + up_bias
    activation, gelu_pull = jax.vjp(gelu_exact, pre_gelu)
    active_low = activation.astype(jnp.bfloat16)
    out_sum = out_sum + jnp.dot(active_low, down_piece, preferred_element_type=jnp.float32)
    grad_active = lax.dot_general(
        cot_rows, down_piece, col_contract, preferred_element_type=jnp.float32
    )
    pre_low = gelu_pull(grad_active)[0].astype(jnp.bfloat16)
    back_sum = jnp.dot(pre_low, up_piece, preferred_element_type=jnp.float32)
    ffn_hidden = lax.dynamic_update_slice_in_dim(ffn_hidden, active_low, jnp.int32(0), 1)
    out_sum, back_sum, pre_grads, hidden = (out_sum, back_sum, pre_low, ffn_hidden)
    out_hidden = (middle + out_sum + down_bias).astype(jnp.bfloat16).reshape(hidden_in.shape)
    grad_ln2, ln2_gain_part, ln2_bias_part = ln2_pull(back_sum)
    grad_middle = cot_rows.astype(jnp.float32) + grad_ln2
    branch_grad = grad_middle.astype(jnp.bfloat16)
    grad_mixed = lax.dot_general(
        branch_grad,
        lax.all_gather(w_out, "cell", axis=0, tiled=True),
        col_contract,
        preferred_element_type=jnp.float32,
    )
    grad_out = jnp.where(
        query_valid[:, :, None, None], grad_mixed.astype(jnp.bfloat16).reshape(head_shape), 0.0
    )
    delta = jnp.einsum("cqhd,cqhd->chq", grad_out.astype(jnp.float32), mixed_sum)

    def grad_step(step_index, carried):
        query_grad, key_block, value_block, key_grad, value_grad = carried
        owner_index = (cycle_place - step_index) % cycle_size
        weights = block_weights(key_block, owner_index)
        grad_weights = jnp.einsum(
            "cqhd,ckhd->chqk", grad_out, value_block, preferred_element_type=jnp.float32
        )
        score_grad = (weights * (grad_weights - delta[..., None])).astype(jnp.bfloat16)
        query_grad = (
            query_grad
            + jnp.einsum(
                "chqk,ckhd->cqhd", score_grad, key_block, preferred_element_type=jnp.float32
            )
            * score_scale
        )
        key_grad = (
            key_grad
            + jnp.einsum("chqk,cqhd->ckhd", score_grad, queries, preferred_element_type=jnp.float32)
            * score_scale
        )
        value_grad = value_grad + jnp.einsum(
            "chqk,cqhd->ckhd",
            weights.astype(jnp.bfloat16),
            grad_out,
            preferred_element_type=jnp.float32,
        )
        key_block, value_block, key_grad, value_grad = (
            passed_along(key_block, "blk", 1),
            passed_along(value_block, "blk", 1),
            passed_along(key_grad.astype(jnp.bfloat16), "blk", 1).astype(key_grad.dtype),
            passed_along(value_grad.astype(jnp.bfloat16), "blk", 1).astype(value_grad.dtype),
        )
        return (query_grad, key_block, value_block, key_grad, value_grad)

    zero_heads = jnp.zeros(head_shape, jnp.float32)
    cycle_done = lax.fori_loop(
        0, cycle_size, grad_step, (zero_heads, keys_own, values_own, zero_heads, zero_heads)
    )
    query_low = cycle_done[0].astype(jnp.bfloat16).reshape(row_count, model_width)
    key_low = cycle_done[3].astype(jnp.bfloat16).reshape(row_count, model_width)
    value_low = cycle_done[4].astype(jnp.bfloat16).reshape(row_count, model_width)
    grad_joined = jnp.concatenate([query_low, key_low, value_low], axis=1)
    grad_normed = lax.dot_general(
        grad_joined,
        lax.all_gather(w_qkv, "cell", axis=0, tiled=True),
        col_contract,
        preferred_element_type=jnp.float32,
    )
    grad_ln1, ln1_gain_part, ln1_bias_part = ln1_pull(grad_normed)
    in_grad = (grad_middle + grad_ln1).reshape(hidden_in.shape)
    qkv_term = lax.dot_general(
        normed_low, grad_joined, row_contract, preferred_element_type=jnp.float32
    )
    out_term = lax.dot_general(
        mixed_low, branch_grad, row_contract, preferred_element_type=jnp.float32
    )
    up_term = lax.dot_general(
        pre_grads, normed2_low, row_contract, preferred_element_type=jnp.float32
    )
    down_term = lax.dot_general(hidden, cot_rows, row_contract, preferred_element_type=jnp.float32)
    ffn_term = jnp.concatenate([up_term, down_term], axis=1).reshape(
        lax.axis_size("cell") * (model_width // lax.axis_size("cell")), ratio_ff * 2 * model_width
    )
    summed = lax.psum_scatter(
        jnp.concatenate([qkv_term, out_term, ffn_term], axis=1).astype(jnp.bfloat16),
        "cell",
        scatter_dimension=0,
        tiled=True,
    ).astype(jnp.float32)
    summed = lax.psum(summed.astype(jnp.bfloat16), "blk").astype(jnp.float32)
    own_rows = summed.shape[0]
    w_qkv_grad = summed[:, : 3 * model_width]
    w_out_grad = summed[:, 3 * model_width : 4 * model_width]
    ffn_grads = summed[:, 4 * model_width :].reshape(own_rows * ratio_ff, 2 * model_width)
    w_up_grad = ffn_grads[:, :model_width]
    w_down_grad = ffn_grads[:, model_width:]
    vectors = lax.psum(
        (
            ln1_gain_part,
            ln1_bias_part,
            jnp.sum(query_low, axis=0, dtype=jnp.float32),
            jnp.sum(value_low, axis=0, dtype=jnp.float32),
            jnp.sum(branch_grad, axis=0, dtype=jnp.float32),
            ln2_gain_part,
            ln2_bias_part,
            jnp.sum(pre_grads, axis=0, dtype=jnp.float32),
            jnp.sum(cot_rows, axis=0, dtype=jnp.float32),
        ),
        ("cell", "blk"),
    )
    return (
        out_hidden,
        in_grad,
        vectors[0],
        vectors[1],
        w_qkv_grad,
        vectors[2],
        vectors[3],
        w_out_grad,
        vectors[4],
        vectors[5],
        vectors[6],
        w_up_grad,
        vectors[7],
        w_down_grad,
        vectors[8],
    )


bf16 = jnp.bfloat16
f32 = jnp.float32
NN = (((1,), (0,)), ((), ()))
NT = (((1,), (1,)), ((), ()))
TN = (((0,), (0,)), ((), ()))
AXES = ("cell", "blk")
VMEM_LIMIT = 60 * 2**20
ROWS = 256
COST_PART = 50
OFFSETS = (0, -1, -2, -3, -4, 1, 2, 3)


def swappable(mesh):
    return dict(mesh.shape) == {"cell": 16, "blk": 2}


def dot(a, b, dims):
    return lax.dot_general(a, b, dims, preferred_element_type=f32)


def params():
    return pltpu.CompilerParams(vmem_limit_bytes=VMEM_LIMIT)


def cost(flops, nbytes, trans=0):
    return pl.CostEstimate(
        flops=int(flops) // COST_PART,
        bytes_accessed=int(nbytes) // COST_PART,
        transcendentals=int(trans) // COST_PART,
    )


def shape(dims, dtype):
    return jax.ShapeDtypeStruct(dims, dtype)


ANY = pl.BlockSpec(memory_space=pl.ANY)


def fixed(dims):
    return pl.BlockSpec(dims, lambda *_: (0,) * len(dims))


def rowed(rows, width):
    return pl.BlockSpec((rows, width), lambda i, *_: (i, 0))


class Ring:
    def __init__(self, sizes):
        self.cells, self.blks = sizes["cell"], sizes["blk"]
        self.chips = self.cells // 2
        depth = self.chips // 2
        self.order = [2 * z for z in range(depth)] + [2 * z + 1 for z in reversed(range(depth))]
        self.place = [self.order.index(c) for c in range(self.chips)]

    def permute(self, x, target):
        pairs = []
        for cell in range(self.cells):
            for blk in range(self.blks):
                to_cell, to_blk = target(cell, blk)
                pairs.append((cell * self.blks + blk, to_cell * self.blks + to_blk))
        return lax.ppermute(x, AXES, pairs)

    def shift(self, x, by):
        def target(cell, blk):
            chip, core = cell // 2, cell % 2
            way = 1 - 2 * ((core + blk) % 2)
            return self.order[(self.place[chip] + way * by) % self.chips] * 2 + core, blk

        return self.permute(x, target)

    def swap_core(self, x):
        return self.permute(x, lambda cell, blk: (cell ^ 1, blk))

    def swap_blk(self, x):
        return self.permute(x, lambda cell, blk: (cell, 1 - blk))

    def chips_of_slots(self, core):
        chip = lax.axis_index("cell") // 2
        way = 1 - 2 * ((core + lax.axis_index("blk")) % 2)
        place = jnp.array(self.place, jnp.int32)[chip]
        return jnp.array(self.order, jnp.int32)[
            (place + way * jnp.array(OFFSETS, jnp.int32)) % self.chips
        ]

    def gather(self, x, back):
        slots = [x] + [None] * 7
        for k in range(1, 5):
            slots[k] = self.shift(slots[k - 1], 1)
            if k <= back:
                slots[4 + k] = self.shift(slots[3 + k] if k > 1 else slots[0], -1)
            if k > back + 1:
                slots[3 + k] = self.swap_blk(slots[k - 1])
            slots = yield slots

    def reduce(self, parts, back, alone=False):
        def added(terms):
            total = terms[0].astype(f32)
            for t in terms[1:]:
                total = total + t.astype(f32)
            return total.astype(bf16)

        way = {"ahead": self.shift(added(parts[4]), -1)}
        if back:
            way["behind"] = self.shift(added(parts[4 + back]), 1)
        for k in range(3, back, -1):
            way[f"over{k}"] = self.swap_blk(added(parts[4 + k]))
        way = yield way
        for k in (3, 2, 1):
            extra = [way.pop(f"over{k}")] if f"over{k}" in way else []
            way["ahead"] = self.shift(added([way["ahead"]] + parts[k] + extra), -1)
            if k < back and not (alone and k == 1):
                way["behind"] = self.shift(added([way["behind"]] + parts[4 + k]), 1)
            way = yield way
        if alone:
            way["behind"] = self.shift(added([way["behind"]] + parts[5]), 1)
            way = yield way
        ends = [way["ahead"]] + ([way["behind"]] if back else [])
        yield added(ends + parts[0])

    def total(self, x):
        count = self.cells * self.blks
        bits = [1 << i for i in range(count.bit_length() - 1)]
        for bit in [b for b in bits if b >= self.blks] + [b for b in bits if b < self.blks]:
            other = bit
            moved = self.permute(
                x, lambda cell, blk: divmod((cell * self.blks + blk) ^ other, self.blks)
            )
            x, moved = yield x, moved
            x = x + moved
        yield x


def norm_parts(x):
    mean = jnp.mean(x, axis=-1, keepdims=True)
    centered = x - mean
    var = jnp.mean(centered * centered, axis=-1, keepdims=True)
    scale = lax.rsqrt(var + epsilon)
    return centered * scale, scale


def norm_back(xh, scale, gain, grad):
    e = grad * gain
    return scale * (
        e - jnp.mean(e, axis=-1, keepdims=True) - xh * jnp.mean(e * xh, axis=-1, keepdims=True)
    )


def colsum(x):
    return jnp.sum(x, axis=0, keepdims=True)


def place_rows(slots, target, place_ref, sem, first=0, cols=None):
    height = slots[0].shape[0]
    start, wide = cols or (0, slots[0].shape[1])
    return [
        pltpu.make_async_copy(
            slot.at[:, pl.ds(start, wide)],
            target.at[
                pl.ds(pl.multiple_of(place_ref[i] * height, 16), height),
                pl.ds(first + start, wide),
            ],
            sem.at[i],
        )
        for i, slot in enumerate(slots)
    ]


def qkv_kernel(n, place_ref, x_ref, gain_ref, bias_ref, qb_ref, vb_ref, *refs):
    slots, (a_ref, q_ref, k_ref, v_ref, w, sem) = refs[:n], refs[n:]
    width = x_ref.shape[1]
    first = pl.program_id(0) == 0
    copies = [
        place_rows(slots, w, place_ref, sem.at[j], cols=(j * width, width)) for j in range(3)
    ]

    @pl.when(first)
    def _():
        for group in copies:
            for c in group:
                c.start()

    xh, _ = norm_parts(x_ref[...].astype(f32))
    a_ref[...] = (xh * gain_ref[...] + bias_ref[...]).astype(bf16)
    for j, (res_ref, add_ref) in enumerate(((q_ref, qb_ref), (k_ref, None), (v_ref, vb_ref))):

        @pl.when(first)
        def _(group=copies[j]):
            for c in group:
                c.wait()

        res = dot(a_ref[...], w[:, j * width : (j + 1) * width], NN)
        if add_ref is not None:
            res = res + add_ref[...]
        res_ref[...] = res.astype(bf16)


def qkv_call(place, x, gain, bias, qb, vb, slots):
    rows, width = x.shape
    n = len(slots)
    block = rowed(ROWS, width)
    vec = fixed((1, width))
    return pl.pallas_call(
        partial(qkv_kernel, n),
        grid_spec=pltpu.PrefetchScalarGridSpec(
            num_scalar_prefetch=1,
            grid=(rows // ROWS,),
            in_specs=[block, vec, vec, vec, vec] + [ANY] * n,
            out_specs=[block] * 4,
            scratch_shapes=[
                pltpu.VMEM((width, 3 * width), bf16),
                pltpu.SemaphoreType.DMA((3, n)),
            ],
        ),
        out_shape=[shape((rows, width), bf16)] * 4,
        compiler_params=params(),
        cost_estimate=cost(6 * rows * width * width, 2 * width * (5 * rows + 3 * width)),
        name="qkv",
    )(place, x, gain, bias, qb, vb, *slots)


def head_keys(low, k, v, mask, fill):
    res = []
    for half in range(2):
        mine = low if half == 0 else jnp.logical_not(low)
        res.append(
            (
                jnp.where(mine, k.astype(f32), mask).astype(bf16),
                jnp.where(mine, v.astype(f32), fill).astype(bf16),
            )
        )
    return res


def head_query(low, lane, half, q):
    mine = low if half == 0 else jnp.logical_not(low)
    one = lane == (HEAD_DIM if half == 0 else 0)
    q = q.astype(f32) * (1.0 / math.sqrt(HEAD_DIM))
    return jnp.where(mine, q, jnp.where(one, 1.0, 0.0)).astype(bf16)


def attend_kernel(qrows, ahead, mask_ref, keep_ref, q_ref, k_ref, v_ref, o_ref, lse_ref):
    n = q_ref.shape[0]
    lane = lax.broadcasted_iota(jnp.int32, (n, 128), 1)
    pair = head_keys(lane < HEAD_DIM, k_ref[...], v_ref[...], mask_ref[...], 1.0)
    lane = lane[:qrows]
    low = lane < HEAD_DIM
    items = [(i, half) for i in range(n // qrows) for half in range(2)]

    def scores(i, half):
        q = head_query(low, lane, half, q_ref[pl.ds(i * qrows, qrows), :])
        return dot(q, pair[half][0], NT)

    waiting = [scores(*item) for item in items[:ahead]]
    for at, (i, half) in enumerate(items):
        if at + ahead < len(items):
            waiting.append(scores(*items[at + ahead]))
        s = waiting.pop(0)
        rows = pl.ds(i * qrows, qrows)
        top = jnp.max(s, axis=1, keepdims=True)
        mixed = dot(jnp.exp(s - top).astype(bf16), pair[half][1], NN)
        total = pltpu.roll(mixed, HEAD_DIM, 1)
        o, lse = mixed / total, top + jnp.log(total)
        if half == 0:
            o_first, lse_first = o, lse
            continue
        o_ref[rows, :] = (jnp.where(low, o_first, o) * keep_ref[rows, :]).astype(bf16)
        lse = jnp.transpose(jnp.where(low, lse_first, lse))
        lse_ref[0, :, rows] = lse[:1, :]
        lse_ref[1, :, rows] = lse[HEAD_DIM : HEAD_DIM + 1, :]


def attend_call(mask, keep, qkv, first, count, qrows=256, ahead=2):
    n = qkv[0].shape[0]
    block = pl.BlockSpec((n, 128), lambda h: (0, h + first))
    return pl.pallas_call(
        partial(attend_kernel, qrows, ahead),
        grid=(count,),
        in_specs=[fixed((n, 1)), fixed((n, 1)), block, block, block],
        out_specs=[
            pl.BlockSpec((n, 128), lambda h: (0, h)),
            pl.BlockSpec((2, 1, n), lambda h: (h, 0, 0)),
        ],
        out_shape=[shape((n, 128 * count), bf16), shape((2 * count, 1, n), f32)],
        compiler_params=params(),
        cost_estimate=cost(20 * count * n * n * 128, 8 * n * 128 * count, 2 * count * n * n),
        name="attend",
    )(mask, keep, *qkv)


def attend_back_kernel(
    qrows, mask_ref, q_ref, k_ref, v_ref, o_ref, go_ref, lse_ref,
    gq_ref, gk_ref, gv_ref, sq_ref, sv_ref, gk_sum, gv_sum,
):
    n = q_ref.shape[0]
    lane = lax.broadcasted_iota(jnp.int32, (n, 128), 1)
    k = k_ref[...]
    scale = 1.0 / math.sqrt(HEAD_DIM)
    pair = head_keys(lane < HEAD_DIM, k, v_ref[...], mask_ref[...], 0.0)
    k_turned = jnp.transpose(k)
    prod = jnp.transpose(o_ref[...].astype(f32) * go_ref[...].astype(f32))
    delta = [colsum(prod[half * HEAD_DIM : (half + 1) * HEAD_DIM, :]) for half in range(2)]
    top = lane[:qrows]
    for i in range(n // qrows):
        rows = pl.ds(i * qrows, qrows)
        gq = []
        for half in range(2):
            q_raw, go = q_ref[rows, :], go_ref[rows, :]
            q = head_query(top < HEAD_DIM, top, half, q_raw)
            p = jnp.exp(dot(pair[half][0], q, NT) - lse_ref[half, :, rows])
            gp = dot(pair[half][1], go, NT)
            gs = (p * (gp - delta[half][:, i * qrows : (i + 1) * qrows])).astype(bf16)
            gv = dot(p.astype(bf16), go, NN)
            gk = dot(gs, q_raw, NN)
            if i == 0:
                gv_sum[half], gk_sum[half] = gv, gk
            else:
                gv_sum[half] += gv
                gk_sum[half] += gk
            gq.append(dot(k_turned, gs, NN))
        turned = jnp.concatenate([gq[0][:HEAD_DIM], gq[1][HEAD_DIM:]], axis=0)
        gq_ref[rows, :] = jnp.transpose(turned * scale).astype(bf16)
    low = lane < HEAD_DIM
    gk_ref[...] = (jnp.where(low, gk_sum[0], gk_sum[1]) * scale).astype(bf16)
    gv = jnp.where(low, gv_sum[0], gv_sum[1]).astype(bf16)
    gv_ref[...] = gv
    sq_ref[...] = colsum(gq_ref[...].astype(f32))
    sv_ref[...] = colsum(gv.astype(f32))


def attend_back_call(mask, qkv, o, go, lse, count, firsts, qrows=512):
    n = go.shape[0]

    def block(first):
        return pl.BlockSpec((n, 128), lambda h: (0, h + first))

    own, vec = block(0), pl.BlockSpec((1, 128), lambda h: (0, h))
    at_qkv, at_o, at_go = firsts
    return pl.pallas_call(
        partial(attend_back_kernel, qrows),
        grid=(count,),
        in_specs=[fixed((n, 1))]
        + [block(at_qkv)] * 3
        + [block(at_o), block(at_go), pl.BlockSpec((2, 1, n), lambda h: (h + at_o, 0, 0))],
        out_specs=[own, own, own, vec, vec],
        out_shape=[shape((n, 128 * count), bf16)] * 3 + [shape((1, 128 * count), f32)] * 2,
        scratch_shapes=[pltpu.VMEM((2, n, 128), f32)] * 2,
        compiler_params=params(),
        cost_estimate=cost(32 * count * n * n * 128, 16 * n * 128 * count, 2 * count * n * n),
        name="attend_back",
    )(mask, *qkv, o, go, lse)


def load_wout(slots, place_ref, w, sem):
    wide = w.shape[1]
    start = slots[0].shape[1] - wide
    copies = place_rows(slots, w, place_ref, sem, -start, (start, wide))

    @pl.when(pl.program_id(0) == 0)
    def _():
        for c in copies:
            c.start()
        for c in copies:
            c.wait()


def out_kernel(n, place_ref, x_ref, bias_ref, gain_ref, shift_ref, *refs):
    slots, o_refs, (m_ref, b_ref, w, sem) = refs[:n], refs[n:-4], refs[-4:]
    load_wout(slots, place_ref, w, sem)
    m = x_ref[...].astype(f32) + bias_ref[...]
    first = 0
    for o_ref in o_refs:
        m = m + dot(o_ref[...], w[first : first + o_ref.shape[1], :], NN)
        first += o_ref.shape[1]
    m_ref[...] = m
    xh, _ = norm_parts(m)
    b_ref[...] = (xh * gain_ref[...] + shift_ref[...]).astype(bf16)


def out_call(place, x, o_parts, slots, bias, gain, shift):
    rows, width = x.shape
    n = len(slots)
    vec = fixed((1, width))
    block = rowed(ROWS, width)
    return pl.pallas_call(
        partial(out_kernel, n),
        grid_spec=pltpu.PrefetchScalarGridSpec(
            num_scalar_prefetch=1,
            grid=(rows // ROWS,),
            in_specs=[block, vec, vec, vec]
            + [ANY] * n
            + [rowed(ROWS, o.shape[1]) for o in o_parts],
            out_specs=[block, block],
            scratch_shapes=[pltpu.VMEM((width, width), bf16), pltpu.SemaphoreType.DMA((n,))],
        ),
        out_shape=[shape((rows, width), f32), shape((rows, width), bf16)],
        compiler_params=params(),
        cost_estimate=cost(4 * rows * width * width, width * (10 * rows + 2 * width)),
        name="out",
    )(place, x, bias, gain, shift, *slots, *o_parts)


def gelu_both(z, gh):
    t = 1.0 / (1.0 + jnp.abs(z) * (0.3275911 / math.sqrt(2.0)))
    e = jnp.exp(z * z * -0.5)
    half = (0.254829592, -0.284496736, 1.421413741, -1.453152027, 1.061405429)
    tail = half[4] * 0.5
    for c in half[3::-1]:
        tail = tail * t + 0.5 * c
    tail = tail * t * e
    phi = jnp.where(z > 0, 1.0 - tail, tail)
    return z * phi, gh * (phi + z * e * (1.0 / math.sqrt(2.0 * math.pi)))


def ffn_kernel(n, later, *refs):
    b_own, b_sib, g_own, g_sib, ub_ref = refs[:5]
    slots = refs[5 : 5 + n]
    refs = refs[5 + n :]
    if later:
        acc_o, acc_g = refs[:2]
        refs = refs[2:]
        h_ref, gz_ref, sum_ref, oo_ref, go_ref, os_ref, gs_ref, us, ds, sem = refs
    else:
        h_ref, gz_ref, sum_ref, oo_ref, go_ref, us, ds, sem = refs
    units = us.shape[0] // n
    i = pl.program_id(0)
    near = i < pl.num_programs(0) // 2
    copies = []
    for s, slot in enumerate(slots):
        rows = pl.ds(s * units, units)
        copies.append(
            pltpu.make_async_copy(slot.at[pl.ds(0, units), :], us.at[rows, :], sem.at[0, s])
        )
        copies.append(
            pltpu.make_async_copy(slot.at[pl.ds(units, units), :], ds.at[rows, :], sem.at[1, s])
        )

    @pl.when(i == 0)
    def _():
        for c in copies:
            c.start()
        for c in copies:
            c.wait()
        sum_ref[...] = jnp.zeros_like(sum_ref)

    b = jnp.where(near, b_own[...], b_sib[...])
    g = jnp.where(near, g_own[...], g_sib[...])
    h, gz = gelu_both(dot(b, us[...], NT) + ub_ref[...], dot(g, ds[...], NT))
    h, gz = h.astype(bf16), gz.astype(bf16)
    h_ref[...] = h
    gz_ref[...] = gz
    sum_ref[...] += colsum(gz.astype(f32))
    out = dot(h, ds[...], NN)
    back = dot(gz, us[...], NN)
    if not later:
        oo_ref[...] = out
        go_ref[...] = back
        return
    out = out + acc_o[...]
    back = back + acc_g[...]

    @pl.when(near)
    def _():
        oo_ref[...] = out.astype(bf16)
        go_ref[...] = back.astype(bf16)

    @pl.when(jnp.logical_not(near))
    def _():
        os_ref[...] = out.astype(bf16)
        gs_ref[...] = back.astype(bf16)


def ffn_call(b_own, b_sib, g_own, g_sib, ub, slots, acc=None):
    rows, width = b_own.shape
    half = rows // ROWS
    n = len(slots)
    units = ub.shape[1]
    later = acc is not None
    near = pl.BlockSpec((ROWS, width), lambda i: (jnp.minimum(i, half - 1), 0))
    far = pl.BlockSpec((ROWS, width), lambda i: (jnp.maximum(i - half, 0), 0))
    both = rowed(ROWS, width)
    acc = list(acc or ())
    out_specs = [rowed(ROWS, units), rowed(ROWS, units), fixed((1, units))]
    out_shape = [shape((2 * rows, units), bf16)] * 2 + [shape((1, units), f32)]
    if later:
        out_specs += [near, near, far, far]
        out_shape += [shape((rows, width), bf16)] * 4
    else:
        out_specs += [both, both]
        out_shape += [shape((2 * rows, width), f32)] * 2
    return pl.pallas_call(
        partial(ffn_kernel, n, later),
        grid=(2 * half,),
        in_specs=[near, far, near, far, fixed((1, units))] + [ANY] * n + [both] * len(acc),
        out_specs=out_specs,
        out_shape=out_shape,
        scratch_shapes=[
            pltpu.VMEM((units, width), bf16),
            pltpu.VMEM((units, width), bf16),
            pltpu.SemaphoreType.DMA((2, n)),
        ],
        compiler_params=params(),
        cost_estimate=cost(
            24 * rows * width * units, rows * width * (24 + 16 * later), 4 * rows * units
        ),
        name="ffn",
    )(b_own, b_sib, g_own, g_sib, ub, *slots, *acc)


def ffn_weights_kernel(n, gz, h, b_own, b_sib, g_own, g_sib, *refs):
    outs = refs[:n]
    lv, rv, ov, lsem, rsem, osem = refs[n:]
    rows = b_own.shape[0]
    units = outs[0].shape[0] // 2
    loads = []
    for which, (left, parts) in enumerate(((gz, (b_own, b_sib)), (h, (g_own, g_sib)))):
        loads.append(pltpu.make_async_copy(left, lv.at[which], lsem.at[which]))
        for j, part in enumerate(parts):
            loads.append(
                pltpu.make_async_copy(
                    part, rv.at[which, pl.ds(j * rows, rows), :], rsem.at[which, j]
                )
            )
    for c in loads:
        c.start()
    stores = []
    step = 0
    for which in range(2):
        for c in loads[3 * which : 3 * which + 3]:
            c.wait()
        for pair in range(n // 2):
            slot = step % 2
            if step >= 2:
                for c in stores[2 * (step - 2) : 2 * (step - 2) + 2]:
                    c.wait()
            cols = pl.ds(pair * 2 * units, 2 * units)
            ov[slot] = dot(lv[which, :, cols], rv[which], TN).astype(bf16)
            for j in range(2):
                c = pltpu.make_async_copy(
                    ov.at[slot, pl.ds(j * units, units), :],
                    outs[2 * pair + j].at[pl.ds(which * units, units), :],
                    osem.at[slot, j],
                )
                c.start()
                stores.append(c)
            step += 1
    for c in stores[2 * (step - 2) :]:
        c.wait()


def ffn_weights_call(gz, h, b_own, b_sib, g_own, g_sib, n):
    rows, units = gz.shape
    width = b_own.shape[1]
    return pl.pallas_call(
        partial(ffn_weights_kernel, n),
        in_specs=[ANY] * 6,
        out_specs=[ANY] * n,
        out_shape=[shape((2 * units // n, width), bf16)] * n,
        scratch_shapes=[
            pltpu.VMEM((2, rows, units), bf16),
            pltpu.VMEM((2, rows, width), bf16),
            pltpu.VMEM((2, 2 * units // n, width), bf16),
            pltpu.SemaphoreType.DMA((2,)),
            pltpu.SemaphoreType.DMA((2, 2)),
            pltpu.SemaphoreType.DMA((2, 2)),
        ],
        compiler_params=params(),
        cost_estimate=cost(6 * rows * units * width, 4 * rows * (units + width)),
        name="ffn_weights",
    )(gz, h, b_own, b_sib, g_own, g_sib)


def mid_kernel(
    n, place_ref, oo_ref, os_ref, go_ref, gs_ref, m_ref, g_ref, keep_ref, db_ref, gain_ref, *refs
):
    slots, (hid_ref, gr_ref, gatt_ref, sums_ref, w, sem) = refs[:n], refs[n:]
    load_wout(slots, place_ref, w, sem)

    @pl.when(pl.program_id(0) == 0)
    def _():
        sums_ref[...] = jnp.zeros_like(sums_ref)

    m = m_ref[...]
    g = g_ref[...].astype(f32)
    ff = oo_ref[...].astype(f32) + os_ref[...].astype(f32)
    hid_ref[...] = (m + ff + db_ref[...]).astype(bf16)
    gb = go_ref[...].astype(f32) + gs_ref[...].astype(f32)
    xh, scale = norm_parts(m)
    gm = g + norm_back(xh, scale, gain_ref[...], gb)
    gr = gm.astype(bf16)
    gr_ref[...] = gr
    gatt_ref[...] = (dot(gr, w[...], NT) * keep_ref[...]).astype(bf16)
    sums_ref[0:1, :] += colsum(gb * xh)
    sums_ref[1:2, :] += colsum(gb)
    sums_ref[2:3, :] += colsum(gr.astype(f32))
    sums_ref[3:4, :] += colsum(g)


def mid_call(place, oo, os, go, gs, m, g, keep, db, gain, slots):
    rows, width = m.shape
    n = len(slots)
    block = rowed(ROWS, width)
    vec = fixed((1, width))
    return pl.pallas_call(
        partial(mid_kernel, n),
        grid_spec=pltpu.PrefetchScalarGridSpec(
            num_scalar_prefetch=1,
            grid=(rows // ROWS,),
            in_specs=[block] * 6 + [rowed(ROWS, 1), vec, vec] + [ANY] * n,
            out_specs=[block] * 3 + [fixed((8, width))],
            scratch_shapes=[pltpu.VMEM((width, width), bf16), pltpu.SemaphoreType.DMA((n,))],
        ),
        out_shape=[shape((rows, width), bf16)] * 3 + [shape((8, width), f32)],
        compiler_params=params(),
        cost_estimate=cost(4 * rows * width * width, width * (30 * rows + 2 * width)),
        name="mid",
    )(place, oo, os, go, gs, m, g, keep, db, gain, *slots)


def att_weights_kernel(n, counts, blocks, place_ref, *refs):
    lefts, rights = refs[: counts[0]], refs[counts[0] : sum(counts)]
    refs = refs[sum(counts) :]
    outs, (lv, tv, rv, ov, lsem, rsem, osem) = refs[: n + 1], refs[n + 1 :]
    height = outs[0].shape[0]
    loads = [pltpu.make_async_copy(r, lv.at[i], lsem.at[i]) for i, r in enumerate(lefts)]
    ends, right_loads = [], []
    for i, r in enumerate(rights):
        start = ends[-1] if ends else 0
        ends.append(start + r.shape[1])
        right_loads.append(
            pltpu.make_async_copy(r, rv.at[:, pl.ds(start, r.shape[1])], rsem.at[i])
        )
    for c in loads[:1] + right_loads + loads[1:]:
        c.start()
    have, arrived = set(), 0
    stores = []
    for step, (left, start, wide) in enumerate(blocks):
        if left not in have:
            loads[left].wait()
            tv[left] = jnp.transpose(lv[left])
            have.add(left)
        while arrived < len(ends) and (arrived == 0 or ends[arrived - 1] < start + wide):
            right_loads[arrived].wait()
            arrived += 1
        slot = step % 2
        if step >= 2:
            for c in stores[step - 2]:
                c.wait()
        cols = pl.ds(start, wide)
        ov[slot, :, pl.ds(0, wide)] = dot(tv[left], rv[:, cols], NN).astype(bf16)
        stores.append([])
        for i in range(2 * n):
            rows = pl.ds(pl.multiple_of(place_ref[i] * height, 16), height)
            goal = outs[i].at[:, cols] if i < n else outs[n].at[i - n, :, cols]
            c = pltpu.make_async_copy(ov.at[slot, rows, pl.ds(0, wide)], goal, osem.at[slot, i])
            c.start()
            stores[-1].append(c)
    for group in stores[-2:]:
        for c in group:
            c.wait()


def att_weights_call(place, lefts, rights, blocks):
    rows, width = lefts[0].shape
    n = len(OFFSETS)
    total = sum(r.shape[1] for r in rights)
    wide = max(b[2] for b in blocks)
    height = width // (2 * n)
    return pl.pallas_call(
        partial(att_weights_kernel, n, (len(lefts), len(rights)), blocks),
        grid_spec=pltpu.PrefetchScalarGridSpec(
            num_scalar_prefetch=1,
            grid=(1,),
            in_specs=[ANY] * (len(lefts) + len(rights)),
            out_specs=[ANY] * (n + 1),
            scratch_shapes=[
                pltpu.VMEM((len(lefts), rows, width), bf16),
                pltpu.VMEM((len(lefts), width, rows), bf16),
                pltpu.VMEM((rows, total), bf16),
                pltpu.VMEM((2, width, wide), bf16),
                pltpu.SemaphoreType.DMA((len(lefts),)),
                pltpu.SemaphoreType.DMA((len(rights),)),
                pltpu.SemaphoreType.DMA((2, 2 * n)),
            ],
        ),
        out_shape=[shape((height, total), bf16)] * n + [shape((n, height, total), bf16)],
        compiler_params=params(),
        cost_estimate=cost(3 * rows * width * total, 2 * (rows + width) * total),
        name="att_weights",
    )(place, *lefts, *rights)


def in_kernel(n, pieces, place_ref, x_ref, gr_ref, gain_ref, *refs):
    grads, slots = refs[:pieces], refs[pieces : pieces + n]
    res_ref, sums_ref, w, sem = refs[pieces + n :]
    copies = place_rows(slots, w, place_ref, sem, cols=(0, w.shape[1]))

    @pl.when(pl.program_id(0) == 0)
    def _():
        for c in copies:
            c.start()
        for c in copies:
            c.wait()
        sums_ref[...] = jnp.zeros_like(sums_ref)

    ga = None
    col = 0
    for r in grads:
        part = dot(r[...], w[:, col : col + r.shape[1]], NT)
        ga = part if ga is None else ga + part
        col += r.shape[1]
    xh, scale = norm_parts(x_ref[...].astype(f32))
    res = gr_ref[...].astype(f32) + norm_back(xh, scale, gain_ref[...], ga)
    sums_ref[0:1, :] += colsum(ga * xh)
    sums_ref[1:2, :] += colsum(ga)
    res_ref[...] = res.astype(res_ref.dtype)


def in_call(place, x, gr, gain, grads, slots, part, dtype):
    rows, width = x.shape
    n = len(slots)
    half = rows // ROWS // 2

    def piece(w):
        return pl.BlockSpec((ROWS, w), lambda i, *_: (i + part * half, 0))

    return pl.pallas_call(
        partial(in_kernel, n, len(grads)),
        grid_spec=pltpu.PrefetchScalarGridSpec(
            num_scalar_prefetch=1,
            grid=(half,),
            in_specs=[piece(width), piece(width), fixed((1, width))]
            + [piece(g.shape[1]) for g in grads]
            + [ANY] * n,
            out_specs=[rowed(ROWS, width), fixed((8, width))],
            scratch_shapes=[
                pltpu.VMEM((width, 3 * width), bf16),
                pltpu.SemaphoreType.DMA((n,)),
            ],
        ),
        out_shape=[shape((rows // 2, width), dtype), shape((8, width), f32)],
        compiler_params=params(),
        cost_estimate=cost(4 * rows * width * width, width * (7 * rows + 6 * width)),
        name="in",
    )(place, x, gr, gain, *grads, *slots)


def fence(*trees):
    return lax.optimization_barrier(trees)


def side_by_side(vectors):
    total = sum(v.shape[0] for v in vectors)
    res, at = None, 0
    for v in vectors:
        wide = jnp.pad(v, (at, total - at - v.shape[0]))
        at += v.shape[0]
        res = wide if res is None else res + wide
    return res


def local_swapped(
    sizes, hidden_in, lengths, ln1_gain, ln1_bias, w_qkv, q_bias, v_bias, w_out, out_bias, ln2_gain, ln2_bias,
    w_up, up_bias, w_down, down_bias, cotangent,
):
    ring = Ring(sizes)
    blk = lax.axis_index("blk")
    core = lax.axis_index("cell") % 2
    genes, width = hidden_in.shape[1:]
    units = w_up.shape[0]
    shards = ring.cells
    n = len(OFFSETS)

    def vec(v):
        return v.reshape(1, -1)

    def pick(x, which):
        return lax.dynamic_index_in_dim(x, which, 0, keepdims=False)

    chips_own, chips_sib = ring.chips_of_slots(core), ring.chips_of_slots(1 - core)
    shard_own = 2 * chips_own + core
    shard_sib = 2 * chips_sib + 1 - core
    place = jnp.concatenate([shard_own, shard_sib])
    index = jnp.arange(genes, dtype=jnp.int32)
    index = jnp.concatenate([blk * genes + index, (1 - blk) * genes + index])
    keep = (index < pick(lengths, blk)).astype(f32)[:, None]
    mask = jnp.where(keep > 0, 0.0, far_below)

    x_got = ring.swap_blk(pick(hidden_in, 1 - blk))
    steps = ring.gather(jnp.concatenate([w_qkv, w_out], axis=1), 2)
    slots, sib = next(steps), [None] * n
    w_pair = jnp.concatenate([w_up, w_down], axis=0)
    g_send = pick(cotangent, 1 - blk)
    small = [vec(v) for v in (ln1_gain, ln1_bias, q_bias, v_bias, out_bias, ln2_gain, ln2_bias)]
    small += [place, mask, keep]
    slots[1], slots[5] = fence(slots[1], slots[5])
    slots = steps.send(slots)
    slots[2], slots[6], small, x_got, w_pair = fence(slots[2], slots[6], small, x_got, w_pair)
    ln1_gain, ln1_bias, q_bias, v_bias, out_bias, ln2_gain, ln2_bias, place, mask, keep = small
    slots = steps.send(slots)
    for s in (0, 1, 5, 2, 6):
        sib[s] = ring.swap_core(slots[s])
    x = jnp.concatenate([pick(hidden_in, blk), x_got], axis=0)
    slots[3], x, sib, g_send = fence(slots[3], x, sib, g_send)
    slots = steps.send(slots)
    for s in (3, 4, 7):
        sib[s] = ring.swap_core(slots[s])
    slots[4], w_pair = fence(slots[4], w_pair)
    pair = [w_pair, ring.shift(w_pair, 1)] + [None] * 6
    g_send, slots[7] = fence(g_send, slots[7])
    g_send = [g_send[: genes // 2], g_send[genes // 2 :]]
    g_got = [ring.swap_blk(g_send[0])]

    weights = slots + sib
    a, *qkv = qkv_call(place, x, ln1_gain, ln1_bias, q_bias, v_bias, weights)
    qkv, pair[1], g_got, g_send = fence(qkv, pair[1], g_got, g_send)
    g_got.append(ring.swap_blk(g_send[1]))
    pair[2] = ring.shift(pair[1], 1)
    pairs = width // 128
    cut = 6 * pairs // 10
    attended = [attend_call(mask, keep, qkv, 0, cut)]
    attended, qkv, pair[2], g_got = fence(attended, qkv, pair[2], g_got)
    pair[3] = ring.shift(pair[2], 1)
    g = jnp.concatenate([pick(cotangent, blk)] + g_got, axis=0)
    g_sib = ring.swap_core(g)
    attended.append(attend_call(mask, keep, qkv, cut, pairs - cut))
    o_parts = [t[0] for t in attended]
    m, b = out_call(place, x, o_parts, weights, out_bias, ln2_gain, ln2_bias)
    b, g_sib, pair[0], pair[3] = fence(b, g_sib, pair[0], pair[3])
    b_sib = ring.swap_core(b)
    pair[4] = ring.shift(pair[3], 1)
    pair[5] = ring.shift(pair[0], -1)
    pair[7] = ring.swap_blk(pair[3])

    ub = up_bias.reshape(shards, units)[shard_own]
    near, far = (0, 1, 2, 3), (4, 5, 6, 7)
    ub_near, ub_far = [vec(jnp.concatenate([ub[s] for s in group])) for group in (near, far)]
    h_near, gz_near, sum_near, *acc = ffn_call(
        b, b_sib, g, g_sib, ub_near, [pair[s] for s in near]
    )
    h_near, gz_near, acc, pair[5] = fence(h_near, gz_near, acc, pair[5])
    pair[6] = ring.shift(pair[5], -1)
    parts = [None] * n
    made = ffn_weights_call(gz_near, h_near, b, b_sib, g, g_sib, len(near))
    made, acc = fence(made, acc)
    for s, t in zip(near, made, strict=True):
        parts[s] = [t]
    h_far, gz_far, sum_far, oo, gb_own, os_send, gs_send = ffn_call(
        b, b_sib, g, g_sib, ub_far, [pair[s] for s in far], acc
    )
    up_sums = dict(
        zip(near + far, jnp.split(sum_near[0], 4) + jnp.split(sum_far[0], 4), strict=True)
    )
    mine = shard_own[None, :] == jnp.arange(shards, dtype=jnp.int32)[:, None]
    up_rows = jnp.sum(
        jnp.where(mine[:, :, None], jnp.stack([up_sums[s] for s in range(n)])[None], 0.0), axis=1
    )
    made = ffn_weights_call(gz_far, h_far, b, b_sib, g, g_sib, len(far))
    os_got, gs_got = ring.swap_core(os_send), ring.swap_core(gs_send)
    made, oo, os_got, gs_got = fence(made, oo, os_got, gs_got)
    for s, t in zip(far, made, strict=True):
        parts[s] = [t]
    steps = ring.reduce(parts, 1)
    way = next(steps)
    out_hidden, gr, gatt, mid_sums = mid_call(
        place, oo, os_got, gb_own, gs_got, m, g, keep, vec(down_bias), ln2_gain, weights
    )
    hid_send = [out_hidden[genes : genes + genes // 2], out_hidden[genes + genes // 2 :]]

    def back(first, count, gatt):
        o, lse = attended[0 if first < cut else 1]
        at = first if first < cut else first - cut
        return attend_back_call(mask, qkv, o, gatt, lse, count, (first, at, first))

    early, half = 128 * cut, width // 2
    late = width - early
    backs = [back(0, cut, gatt)]
    backs, gatt, way["ahead"], way["over3"], hid_send = fence(
        backs, gatt, way["ahead"], way["over3"], hid_send
    )
    way = steps.send(way)
    first = att_weights_call(
        place, [a, jnp.concatenate(o_parts, axis=1)], list(backs[0][:3]) + [gr],
        [(0, i * early, early) for i in range(3)] + [(1, 3 * early + i * half, half) for i in range(2)],
    )
    first, gatt, way, hid_send = fence(first, gatt, way, hid_send)
    way = steps.send(way)
    hid_got = [ring.swap_blk(hid_send[0])]
    first_sib = ring.swap_core(first[n])
    one = (pairs - cut) // 4
    backs.append(back(cut, one, gatt))
    backs, gatt, first, first_sib, up_rows = fence(backs, gatt, first, first_sib, up_rows)
    steps_first = ring.reduce([[first[s], first_sib[s]] for s in range(n)], 3)
    way_first = next(steps_first)
    backs.append(back(cut + one, pairs - cut - one, gatt))
    backs, way_first, way, hid_got, hid_send = fence(backs, way_first, way, hid_got, hid_send)
    way_first = steps_first.send(way_first)
    hid_got.append(ring.swap_blk(hid_send[1]))
    way = steps.send(way)
    grads = [t[i] for i in range(3) for t in backs]
    in_send, in_sums_send = in_call(place, x, gr, ln1_gain, grads, weights, 1, bf16)
    sums_early = side_by_side(
        [mid_sums[:4].reshape(-1), up_rows.reshape(-1)]
        + [t[i].reshape(-1) for i in (3, 4) for t in backs]
    )
    in_send, backs, way_first, hid_got = fence(in_send, backs, way_first, hid_got)
    way_first = steps_first.send(way_first)
    in_got = ring.swap_blk(in_send)
    second = att_weights_call(
        place, [a], [t[i] for i in range(3) for t in backs[1:]],
        [(0, i * late, late) for i in range(3)],
    )
    second, way, way_first, grads, sums_early = fence(second, way, way_first, grads, sums_early)
    way_first = steps_first.send(way_first)
    ffn_sum = steps.send(way)
    ffn_got = ring.swap_blk(ffn_sum)
    second_sib = ring.swap_core(second[n])
    steps_second = ring.reduce([[second[s], second_sib[s]] for s in range(n)], 3)
    way_second = next(steps_second)
    in_own, in_sums = in_call(place, x, gr, ln1_gain, grads, weights, 0, f32)
    in_own, in_sums, in_sums_send, way_first, way_second = fence(
        in_own, in_sums, in_sums_send, way_first, way_second
    )
    first_sum = steps_first.send(way_first)
    first_got = ring.swap_blk(first_sum)
    way_second = steps_second.send(way_second)
    ln1_sums = (in_sums + in_sums_send)[:2].reshape(-1)
    steps_sums = ring.total(side_by_side([sums_early, ln1_sums]))
    sums = next(steps_sums)
    sums = steps_sums.send(sums)
    way_second, sums = fence(way_second, sums)
    way_second = steps_second.send(way_second)
    sums = steps_sums.send(sums)
    way_second, sums = fence(way_second, sums)
    way_second = steps_second.send(way_second)
    sums = steps_sums.send(sums)
    way_second, sums = fence(way_second, sums)
    second_sum = steps_second.send(way_second)
    second_got = ring.swap_blk(second_sum)
    sums = steps_sums.send(sums)
    sums = steps_sums.send(sums)
    ffn_sum, ffn_got, first_sum, first_got, in_got = fence(
        ffn_sum, ffn_got, first_sum, first_got, in_got
    )
    ffn_rows, first_rows, second_rows = [
        a.astype(f32) + b.astype(f32)
        for a, b in ((ffn_sum, ffn_got), (first_sum, first_got), (second_sum, second_got))
    ]

    def home(own, got):
        got = got.astype(own.dtype)
        return jnp.where(blk == 0, jnp.stack([own, got]), jnp.stack([got, own]))

    hidden = home(out_hidden[:genes], jnp.concatenate(hid_got))
    in_grad = home(in_own, in_got)
    marks = [width] * 4 + [shards * units]
    marks += 2 * [128 * c for c in (cut, one, pairs - cut - one)] + [width] * 2
    pieces, at = [], 0
    for size in marks:
        pieces.append(sums[at : at + size])
        at += size
    ln2_gain_g, ln2_bias_g, out_bias_g, down_bias_g, up_bias_g = pieces[:5]
    q_bias_g, v_bias_g = jnp.concatenate(pieces[5:8]), jnp.concatenate(pieces[8:11])
    ln1_gain_g, ln1_bias_g = pieces[11:]
    w_qkv_grad = jnp.concatenate(
        [
            t
            for i in range(3)
            for t in (
                first_rows[:, i * early : (i + 1) * early],
                second_rows[:, i * late : (i + 1) * late],
            )
        ],
        axis=1,
    )
    return (
        hidden,
        in_grad,
        ln1_gain_g,
        ln1_bias_g,
        w_qkv_grad,
        q_bias_g,
        v_bias_g,
        first_rows[:, 3 * early :],
        out_bias_g,
        ln2_gain_g,
        ln2_bias_g,
        ffn_rows[:units],
        up_bias_g,
        ffn_rows[units:],
        down_bias_g,
    )


def solution(mesh):
    placed = (
        P("cell", "blk", None),
        P("cell"),
        P(),
        P(),
        P("cell", None),
        P(),
        P(),
        P("cell", None),
        P(),
        P(),
        P(),
        P("cell", None),
        P(),
        P("cell", None),
        P(),
        P("cell", "blk", None),
    )
    return jax.shard_map(
        partial(local_swapped, dict(mesh.shape)) if swappable(mesh) else local,
        mesh=mesh,
        in_specs=placed,
        out_specs=(
            P("cell", "blk", None),
            P("cell", "blk", None),
            P(),
            P(),
            P("cell", None),
            P(),
            P(),
            P("cell", None),
            P(),
            P(),
            P(),
            P("cell", None),
            P(),
            P("cell", None),
            P(),
        ),
        check_vma=False,
    )
```

```python
from functools import partial
import math

import jax
import jax.numpy as jnp
from jax import lax
from jax.experimental import pallas as pl
from jax.experimental.pallas import tpu as pltpu
from jax.sharding import PartitionSpec as P

HEAD_DIM = 64


epsilon = 1e-05
far_below = -1e30
row_contract = (((0,), (0,)), ((), ()))
col_contract = (((1,), (1,)), ((), ()))


def passed_along(x, axis, by):
    count = lax.axis_size(axis)
    return lax.ppermute(x, axis, [(i, (i + by) % count) for i in range(count)])


def layer_norm(source, gain_vec, shift_vec):
    row_mean = jnp.mean(source, axis=-1, keepdims=True)
    centered = source - row_mean
    row_var = jnp.mean(centered * centered, axis=-1, keepdims=True)
    return centered * lax.rsqrt(row_var + epsilon) * gain_vec + shift_vec


def local(
    hidden_in,
    lengths,
    ln1_gain,
    ln1_bias,
    w_qkv,
    q_bias,
    v_bias,
    w_out,
    out_bias,
    ln2_gain,
    ln2_bias,
    w_up,
    up_bias,
    w_down,
    down_bias,
    cotangent,
):
    cell_count, local_genes, model_width = hidden_in.shape
    row_count = cell_count * local_genes
    head_count = model_width // HEAD_DIM
    score_scale = 1.0 / math.sqrt(HEAD_DIM)
    cycle_size = lax.axis_size("blk")
    cycle_place = lax.axis_index("blk")
    ratio_ff = up_bias.shape[0] // model_width
    head_shape = (cell_count, local_genes, head_count, HEAD_DIM)
    stat_shape = (cell_count, head_count, local_genes)
    inputs = hidden_in.astype(jnp.float32).reshape(row_count, model_width)
    cot_rows = cotangent.reshape(row_count, model_width)
    gene_index = jnp.arange(local_genes, dtype=jnp.int32)
    query_valid = (cycle_place * local_genes + gene_index)[None, :] < lengths[:, None]
    normed, ln1_pull = jax.vjp(layer_norm, inputs, ln1_gain, ln1_bias)
    normed_low = normed.astype(jnp.bfloat16)
    part_cols = normed_low
    joined = jnp.dot(
        part_cols,
        lax.all_gather(w_qkv, "cell", axis=0, tiled=True),
        preferred_element_type=jnp.float32,
    )
    queries = (joined[:, :model_width] + q_bias).astype(jnp.bfloat16).reshape(head_shape)
    keys_own = joined[:, model_width : 2 * model_width].astype(jnp.bfloat16).reshape(head_shape)
    values_own = (joined[:, 2 * model_width :] + v_bias).astype(jnp.bfloat16).reshape(head_shape)

    def block_scores(key_block, owner_index):
        scores = (
            jnp.einsum("cqhd,ckhd->chqk", queries, key_block, preferred_element_type=jnp.float32)
            * score_scale
        )
        key_valid = (owner_index * local_genes + gene_index)[None, :] < lengths[:, None]
        return (scores, key_valid[:, None, None, :])

    def stats_turn(owner_index, carried, key_block):
        row_top, row_total = carried
        scores, is_valid = block_scores(key_block, owner_index)
        new_top = jnp.maximum(row_top, jnp.max(jnp.where(is_valid, scores, far_below), axis=-1))
        raised = jnp.where(is_valid, jnp.exp(scores - new_top[..., None]), 0.0)
        return (new_top, row_total * jnp.exp(row_top - new_top) + jnp.sum(raised, axis=-1))

    first_stats = stats_turn(
        cycle_place,
        (jnp.full(stat_shape, far_below, jnp.float32), jnp.zeros(stat_shape, jnp.float32)),
        keys_own,
    )

    def stats_step(step_index, carried):
        stats_now, key_block = carried
        key_block = passed_along(key_block, "blk", 1)
        return (
            stats_turn((cycle_place - step_index) % cycle_size, stats_now, key_block),
            key_block,
        )

    final_stats = lax.fori_loop(1, cycle_size, stats_step, (first_stats, keys_own))[0]
    log_total = final_stats[0] + jnp.log(final_stats[1])

    def block_weights(key_block, owner_index):
        scores, is_valid = block_scores(key_block, owner_index)
        return jnp.where(is_valid, jnp.exp(scores - log_total[..., None]), 0.0)

    def mix_turn(owner_index, mixed_sum, key_block, value_block):
        weights = block_weights(key_block, owner_index).astype(jnp.bfloat16)
        return mixed_sum + jnp.einsum(
            "chqk,ckhd->cqhd", weights, value_block, preferred_element_type=jnp.float32
        )

    mixed_start = mix_turn(cycle_place, jnp.zeros(head_shape, jnp.float32), keys_own, values_own)

    def pair_step(step_index, carried):
        inner, key_block, value_block = carried
        key_block, value_block = passed_along((key_block, value_block), "blk", 1)
        return (
            mix_turn((cycle_place - step_index) % cycle_size, inner, key_block, value_block),
            key_block,
            value_block,
        )

    mixed_sum = lax.fori_loop(1, cycle_size, pair_step, (mixed_start, keys_own, values_own))[0]
    mixed_low = (
        jnp.where(query_valid[:, :, None, None], mixed_sum, 0.0)
        .astype(jnp.bfloat16)
        .reshape(row_count, model_width)
    )
    part_cols = mixed_low
    branch = jnp.dot(
        part_cols,
        lax.all_gather(w_out, "cell", axis=0, tiled=True),
        preferred_element_type=jnp.float32,
    )
    middle = inputs + branch + out_bias
    normed2, ln2_pull = jax.vjp(layer_norm, middle, ln2_gain, ln2_bias)
    normed2_low = normed2.astype(jnp.bfloat16)
    gelu_exact = partial(jax.nn.gelu, approximate=False)
    ff_total = up_bias.shape[0]
    out_sum = jnp.zeros((row_count, model_width), jnp.float32)
    ffn_hidden = jnp.zeros((row_count, ff_total), jnp.bfloat16)
    up_piece = lax.all_gather(w_up, "cell", axis=0, tiled=True)
    down_piece = lax.all_gather(w_down, "cell", axis=0, tiled=True)
    pre_gelu = lax.dot_general(
        normed2_low, up_piece, col_contract, preferred_element_type=jnp.float32
    )
    pre_gelu = pre_gelu + up_bias
    activation, gelu_pull = jax.vjp(gelu_exact, pre_gelu)
    active_low = activation.astype(jnp.bfloat16)
    out_sum = out_sum + jnp.dot(active_low, down_piece, preferred_element_type=jnp.float32)
    grad_active = lax.dot_general(
        cot_rows, down_piece, col_contract, preferred_element_type=jnp.float32
    )
    pre_low = gelu_pull(grad_active)[0].astype(jnp.bfloat16)
    back_sum = jnp.dot(pre_low, up_piece, preferred_element_type=jnp.float32)
    ffn_hidden = lax.dynamic_update_slice_in_dim(ffn_hidden, active_low, jnp.int32(0), 1)
    out_sum, back_sum, pre_grads, hidden = (out_sum, back_sum, pre_low, ffn_hidden)
    out_hidden = (middle + out_sum + down_bias).astype(jnp.bfloat16).reshape(hidden_in.shape)
    grad_ln2, ln2_gain_part, ln2_bias_part = ln2_pull(back_sum)
    grad_middle = cot_rows.astype(jnp.float32) + grad_ln2
    branch_grad = grad_middle.astype(jnp.bfloat16)
    grad_mixed = lax.dot_general(
        branch_grad,
        lax.all_gather(w_out, "cell", axis=0, tiled=True),
        col_contract,
        preferred_element_type=jnp.float32,
    )
    grad_out = jnp.where(
        query_valid[:, :, None, None], grad_mixed.astype(jnp.bfloat16).reshape(head_shape), 0.0
    )
    delta = jnp.einsum("cqhd,cqhd->chq", grad_out.astype(jnp.float32), mixed_sum)

    def grad_step(step_index, carried):
        query_grad, key_block, value_block, key_grad, value_grad = carried
        owner_index = (cycle_place - step_index) % cycle_size
        weights = block_weights(key_block, owner_index)
        grad_weights = jnp.einsum(
            "cqhd,ckhd->chqk", grad_out, value_block, preferred_element_type=jnp.float32
        )
        score_grad = (weights * (grad_weights - delta[..., None])).astype(jnp.bfloat16)
        query_grad = (
            query_grad
            + jnp.einsum(
                "chqk,ckhd->cqhd", score_grad, key_block, preferred_element_type=jnp.float32
            )
            * score_scale
        )
        key_grad = (
            key_grad
            + jnp.einsum("chqk,cqhd->ckhd", score_grad, queries, preferred_element_type=jnp.float32)
            * score_scale
        )
        value_grad = value_grad + jnp.einsum(
            "chqk,cqhd->ckhd",
            weights.astype(jnp.bfloat16),
            grad_out,
            preferred_element_type=jnp.float32,
        )
        key_block, value_block, key_grad, value_grad = (
            passed_along(key_block, "blk", 1),
            passed_along(value_block, "blk", 1),
            passed_along(key_grad.astype(jnp.bfloat16), "blk", 1).astype(key_grad.dtype),
            passed_along(value_grad.astype(jnp.bfloat16), "blk", 1).astype(value_grad.dtype),
        )
        return (query_grad, key_block, value_block, key_grad, value_grad)

    zero_heads = jnp.zeros(head_shape, jnp.float32)
    cycle_done = lax.fori_loop(
        0, cycle_size, grad_step, (zero_heads, keys_own, values_own, zero_heads, zero_heads)
    )
    query_low = cycle_done[0].astype(jnp.bfloat16).reshape(row_count, model_width)
    key_low = cycle_done[3].astype(jnp.bfloat16).reshape(row_count, model_width)
    value_low = cycle_done[4].astype(jnp.bfloat16).reshape(row_count, model_width)
    grad_joined = jnp.concatenate([query_low, key_low, value_low], axis=1)
    grad_normed = lax.dot_general(
        grad_joined,
        lax.all_gather(w_qkv, "cell", axis=0, tiled=True),
        col_contract,
        preferred_element_type=jnp.float32,
    )
    grad_ln1, ln1_gain_part, ln1_bias_part = ln1_pull(grad_normed)
    in_grad = (grad_middle + grad_ln1).reshape(hidden_in.shape)
    qkv_term = lax.dot_general(
        normed_low, grad_joined, row_contract, preferred_element_type=jnp.float32
    )
    out_term = lax.dot_general(
        mixed_low, branch_grad, row_contract, preferred_element_type=jnp.float32
    )
    up_term = lax.dot_general(
        pre_grads, normed2_low, row_contract, preferred_element_type=jnp.float32
    )
    down_term = lax.dot_general(hidden, cot_rows, row_contract, preferred_element_type=jnp.float32)
    ffn_term = jnp.concatenate([up_term, down_term], axis=1).reshape(
        lax.axis_size("cell") * (model_width // lax.axis_size("cell")), ratio_ff * 2 * model_width
    )
    summed = lax.psum_scatter(
        jnp.concatenate([qkv_term, out_term, ffn_term], axis=1).astype(jnp.bfloat16),
        "cell",
        scatter_dimension=0,
        tiled=True,
    ).astype(jnp.float32)
    summed = lax.psum(summed.astype(jnp.bfloat16), "blk").astype(jnp.float32)
    own_rows = summed.shape[0]
    w_qkv_grad = summed[:, : 3 * model_width]
    w_out_grad = summed[:, 3 * model_width : 4 * model_width]
    ffn_grads = summed[:, 4 * model_width :].reshape(own_rows * ratio_ff, 2 * model_width)
    w_up_grad = ffn_grads[:, :model_width]
    w_down_grad = ffn_grads[:, model_width:]
    vectors = lax.psum(
        (
            ln1_gain_part,
            ln1_bias_part,
            jnp.sum(query_low, axis=0, dtype=jnp.float32),
            jnp.sum(value_low, axis=0, dtype=jnp.float32),
            jnp.sum(branch_grad, axis=0, dtype=jnp.float32),
            ln2_gain_part,
            ln2_bias_part,
            jnp.sum(pre_grads, axis=0, dtype=jnp.float32),
            jnp.sum(cot_rows, axis=0, dtype=jnp.float32),
        ),
        ("cell", "blk"),
    )
    return (
        out_hidden,
        in_grad,
        vectors[0],
        vectors[1],
        w_qkv_grad,
        vectors[2],
        vectors[3],
        w_out_grad,
        vectors[4],
        vectors[5],
        vectors[6],
        w_up_grad,
        vectors[7],
        w_down_grad,
        vectors[8],
    )


bf16 = jnp.bfloat16
f32 = jnp.float32
NN = (((1,), (0,)), ((), ()))
NT = (((1,), (1,)), ((), ()))
TN = (((0,), (0,)), ((), ()))
AXES = ("cell", "blk")
VMEM_LIMIT = 60 * 2**20
ROWS = 256
COST_PART = 50
OFFSETS = (0, -1, -2, -3, -4, 1, 2, 3)


def swappable(mesh):
    return dict(mesh.shape) == {"cell": 16, "blk": 2}


def dot(a, b, dims):
    return lax.dot_general(a, b, dims, preferred_element_type=f32)


def params():
    return pltpu.CompilerParams(vmem_limit_bytes=VMEM_LIMIT)


def cost(flops, nbytes, trans=0):
    return pl.CostEstimate(
        flops=int(flops) // COST_PART,
        bytes_accessed=int(nbytes) // COST_PART,
        transcendentals=int(trans) // COST_PART,
    )


def shape(dims, dtype):
    return jax.ShapeDtypeStruct(dims, dtype)


ANY = pl.BlockSpec(memory_space=pl.ANY)


def fixed(dims):
    return pl.BlockSpec(dims, lambda *_: (0,) * len(dims))


def rowed(rows, width):
    return pl.BlockSpec((rows, width), lambda i, *_: (i, 0))


class Ring:
    def __init__(self, sizes):
        self.cells, self.blks = sizes["cell"], sizes["blk"]
        self.chips = self.cells // 2
        depth = self.chips // 2
        self.order = [2 * z for z in range(depth)] + [2 * z + 1 for z in reversed(range(depth))]
        self.place = [self.order.index(c) for c in range(self.chips)]

    def permute(self, x, target):
        pairs = []
        for cell in range(self.cells):
            for blk in range(self.blks):
                to_cell, to_blk = target(cell, blk)
                pairs.append((cell * self.blks + blk, to_cell * self.blks + to_blk))
        return lax.ppermute(x, AXES, pairs)

    def shift(self, x, by):
        def target(cell, blk):
            chip, core = cell // 2, cell % 2
            way = 1 - 2 * ((core + blk) % 2)
            return self.order[(self.place[chip] + way * by) % self.chips] * 2 + core, blk

        return self.permute(x, target)

    def swap_core(self, x):
        return self.permute(x, lambda cell, blk: (cell ^ 1, blk))

    def swap_blk(self, x):
        return self.permute(x, lambda cell, blk: (cell, 1 - blk))

    def chips_of_slots(self, core):
        chip = lax.axis_index("cell") // 2
        way = 1 - 2 * ((core + lax.axis_index("blk")) % 2)
        place = jnp.array(self.place, jnp.int32)[chip]
        return jnp.array(self.order, jnp.int32)[
            (place + way * jnp.array(OFFSETS, jnp.int32)) % self.chips
        ]

    def gather(self, x, back):
        slots = [x] + [None] * 7
        for k in range(1, 5):
            slots[k] = self.shift(slots[k - 1], 1)
            if k <= back:
                slots[4 + k] = self.shift(slots[3 + k] if k > 1 else slots[0], -1)
            if k > back + 1:
                slots[3 + k] = self.swap_blk(slots[k - 1])
            slots = yield slots

    def reduce(self, parts, back, alone=False):
        def added(terms):
            total = terms[0].astype(f32)
            for t in terms[1:]:
                total = total + t.astype(f32)
            return total.astype(bf16)

        way = {"ahead": self.shift(added(parts[4]), -1)}
        if back:
            way["behind"] = self.shift(added(parts[4 + back]), 1)
        for k in range(3, back, -1):
            way[f"over{k}"] = self.swap_blk(added(parts[4 + k]))
        way = yield way
        for k in (3, 2, 1):
            extra = [way.pop(f"over{k}")] if f"over{k}" in way else []
            way["ahead"] = self.shift(added([way["ahead"]] + parts[k] + extra), -1)
            if k < back and not (alone and k == 1):
                way["behind"] = self.shift(added([way["behind"]] + parts[4 + k]), 1)
            way = yield way
        if alone:
            way["behind"] = self.shift(added([way["behind"]] + parts[5]), 1)
            way = yield way
        ends = [way["ahead"]] + ([way["behind"]] if back else [])
        yield added(ends + parts[0])

    def total(self, x):
        count = self.cells * self.blks
        bits = [1 << i for i in range(count.bit_length() - 1)]
        for bit in [b for b in bits if b >= self.blks] + [b for b in bits if b < self.blks]:
            other = bit
            moved = self.permute(
                x, lambda cell, blk: divmod((cell * self.blks + blk) ^ other, self.blks)
            )
            x, moved = yield x, moved
            x = x + moved
        yield x


def norm_parts(x):
    mean = jnp.mean(x, axis=-1, keepdims=True)
    centered = x - mean
    var = jnp.mean(centered * centered, axis=-1, keepdims=True)
    scale = lax.rsqrt(var + epsilon)
    return centered * scale, scale


def norm_back(xh, scale, gain, grad):
    e = grad * gain
    return scale * (
        e - jnp.mean(e, axis=-1, keepdims=True) - xh * jnp.mean(e * xh, axis=-1, keepdims=True)
    )


def colsum(x):
    return jnp.sum(x, axis=0, keepdims=True)


def place_rows(slots, target, place_ref, sem, first=0, cols=None):
    height = slots[0].shape[0]
    start, wide = cols or (0, slots[0].shape[1])
    return [
        pltpu.make_async_copy(
            slot.at[:, pl.ds(start, wide)],
            target.at[
                pl.ds(pl.multiple_of(place_ref[i] * height, 16), height),
                pl.ds(first + start, wide),
            ],
            sem.at[i],
        )
        for i, slot in enumerate(slots)
    ]


def qkv_kernel(n, place_ref, x_ref, gain_ref, bias_ref, qb_ref, vb_ref, *refs):
    slots, (a_ref, q_ref, k_ref, v_ref, w, sem) = refs[:n], refs[n:]
    width = x_ref.shape[1]
    first = pl.program_id(0) == 0
    copies = [
        place_rows(slots, w, place_ref, sem.at[j], cols=(j * width, width)) for j in range(3)
    ]

    @pl.when(first)
    def _():
        for group in copies:
            for c in group:
                c.start()

    xh, _ = norm_parts(x_ref[...].astype(f32))
    a_ref[...] = (xh * gain_ref[...] + bias_ref[...]).astype(bf16)
    for j, (res_ref, add_ref) in enumerate(((q_ref, qb_ref), (k_ref, None), (v_ref, vb_ref))):

        @pl.when(first)
        def _(group=copies[j]):
            for c in group:
                c.wait()

        res = dot(a_ref[...], w[:, j * width : (j + 1) * width], NN)
        if add_ref is not None:
            res = res + add_ref[...]
        res_ref[...] = res.astype(bf16)


def qkv_call(place, x, gain, bias, qb, vb, slots):
    rows, width = x.shape
    n = len(slots)
    block = rowed(ROWS, width)
    vec = fixed((1, width))
    return pl.pallas_call(
        partial(qkv_kernel, n),
        grid_spec=pltpu.PrefetchScalarGridSpec(
            num_scalar_prefetch=1,
            grid=(rows // ROWS,),
            in_specs=[block, vec, vec, vec, vec] + [ANY] * n,
            out_specs=[block] * 4,
            scratch_shapes=[
                pltpu.VMEM((width, 3 * width), bf16),
                pltpu.SemaphoreType.DMA((3, n)),
            ],
        ),
        out_shape=[shape((rows, width), bf16)] * 4,
        compiler_params=params(),
        cost_estimate=cost(6 * rows * width * width, 2 * width * (5 * rows + 3 * width)),
        name="qkv",
    )(place, x, gain, bias, qb, vb, *slots)


def head_keys(low, k, v, mask, fill):
    res = []
    for half in range(2):
        mine = low if half == 0 else jnp.logical_not(low)
        res.append(
            (
                jnp.where(mine, k.astype(f32), mask).astype(bf16),
                jnp.where(mine, v.astype(f32), fill).astype(bf16),
            )
        )
    return res


def head_query(low, lane, half, q):
    mine = low if half == 0 else jnp.logical_not(low)
    one = lane == (HEAD_DIM if half == 0 else 0)
    q = q.astype(f32) * (1.0 / math.sqrt(HEAD_DIM))
    return jnp.where(mine, q, jnp.where(one, 1.0, 0.0)).astype(bf16)


def attend_kernel(qrows, ahead, mask_ref, keep_ref, q_ref, k_ref, v_ref, o_ref, lse_ref):
    n = q_ref.shape[0]
    lane = lax.broadcasted_iota(jnp.int32, (n, 128), 1)
    pair = head_keys(lane < HEAD_DIM, k_ref[...], v_ref[...], mask_ref[...], 1.0)
    lane = lane[:qrows]
    low = lane < HEAD_DIM
    items = [(i, half) for i in range(n // qrows) for half in range(2)]

    def scores(i, half):
        q = head_query(low, lane, half, q_ref[pl.ds(i * qrows, qrows), :])
        return dot(q, pair[half][0], NT)

    waiting = [scores(*item) for item in items[:ahead]]
    for at, (i, half) in enumerate(items):
        if at + ahead < len(items):
            waiting.append(scores(*items[at + ahead]))
        s = waiting.pop(0)
        rows = pl.ds(i * qrows, qrows)
        top = jnp.max(s, axis=1, keepdims=True)
        mixed = dot(jnp.exp(s - top).astype(bf16), pair[half][1], NN)
        total = pltpu.roll(mixed, HEAD_DIM, 1)
        o, lse = mixed / total, top + jnp.log(total)
        if half == 0:
            o_first, lse_first = o, lse
            continue
        o_ref[rows, :] = (jnp.where(low, o_first, o) * keep_ref[rows, :]).astype(bf16)
        lse = jnp.transpose(jnp.where(low, lse_first, lse))
        lse_ref[0, :, rows] = lse[:1, :]
        lse_ref[1, :, rows] = lse[HEAD_DIM : HEAD_DIM + 1, :]


def attend_call(mask, keep, qkv, first, count, qrows=256, ahead=2):
    n = qkv[0].shape[0]
    block = pl.BlockSpec((n, 128), lambda h: (0, h + first))
    return pl.pallas_call(
        partial(attend_kernel, qrows, ahead),
        grid=(count,),
        in_specs=[fixed((n, 1)), fixed((n, 1)), block, block, block],
        out_specs=[
            pl.BlockSpec((n, 128), lambda h: (0, h)),
            pl.BlockSpec((2, 1, n), lambda h: (h, 0, 0)),
        ],
        out_shape=[shape((n, 128 * count), bf16), shape((2 * count, 1, n), f32)],
        compiler_params=params(),
        cost_estimate=cost(20 * count * n * n * 128, 8 * n * 128 * count, 2 * count * n * n),
        name="attend",
    )(mask, keep, *qkv)


def attend_back_kernel(
    qrows, mask_ref, q_ref, k_ref, v_ref, o_ref, go_ref, lse_ref,
    gq_ref, gk_ref, gv_ref, sq_ref, sv_ref, gk_sum, gv_sum,
):
    n = q_ref.shape[0]
    lane = lax.broadcasted_iota(jnp.int32, (n, 128), 1)
    k = k_ref[...]
    scale = 1.0 / math.sqrt(HEAD_DIM)
    pair = head_keys(lane < HEAD_DIM, k, v_ref[...], mask_ref[...], 0.0)
    k_turned = jnp.transpose(k)
    prod = jnp.transpose(o_ref[...].astype(f32) * go_ref[...].astype(f32))
    delta = [colsum(prod[half * HEAD_DIM : (half + 1) * HEAD_DIM, :]) for half in range(2)]
    top = lane[:qrows]
    for i in range(n // qrows):
        rows = pl.ds(i * qrows, qrows)
        gq = []
        for half in range(2):
            q_raw, go = q_ref[rows, :], go_ref[rows, :]
            q = head_query(top < HEAD_DIM, top, half, q_raw)
            p = jnp.exp(dot(pair[half][0], q, NT) - lse_ref[half, :, rows])
            gp = dot(pair[half][1], go, NT)
            gs = (p * (gp - delta[half][:, i * qrows : (i + 1) * qrows])).astype(bf16)
            gv = dot(p.astype(bf16), go, NN)
            gk = dot(gs, q_raw, NN)
            if i == 0:
                gv_sum[half], gk_sum[half] = gv, gk
            else:
                gv_sum[half] += gv
                gk_sum[half] += gk
            gq.append(dot(k_turned, gs, NN))
        turned = jnp.concatenate([gq[0][:HEAD_DIM], gq[1][HEAD_DIM:]], axis=0)
        gq_ref[rows, :] = jnp.transpose(turned * scale).astype(bf16)
    low = lane < HEAD_DIM
    gk_ref[...] = (jnp.where(low, gk_sum[0], gk_sum[1]) * scale).astype(bf16)
    gv = jnp.where(low, gv_sum[0], gv_sum[1]).astype(bf16)
    gv_ref[...] = gv
    sq_ref[...] = colsum(gq_ref[...].astype(f32))
    sv_ref[...] = colsum(gv.astype(f32))


def attend_back_call(mask, qkv, o, go, lse, count, firsts, qrows=512):
    n = go.shape[0]

    def block(first):
        return pl.BlockSpec((n, 128), lambda h: (0, h + first))

    own, vec = block(0), pl.BlockSpec((1, 128), lambda h: (0, h))
    at_qkv, at_o, at_go = firsts
    return pl.pallas_call(
        partial(attend_back_kernel, qrows),
        grid=(count,),
        in_specs=[fixed((n, 1))]
        + [block(at_qkv)] * 3
        + [block(at_o), block(at_go), pl.BlockSpec((2, 1, n), lambda h: (h + at_o, 0, 0))],
        out_specs=[own, own, own, vec, vec],
        out_shape=[shape((n, 128 * count), bf16)] * 3 + [shape((1, 128 * count), f32)] * 2,
        scratch_shapes=[pltpu.VMEM((2, n, 128), f32)] * 2,
        compiler_params=params(),
        cost_estimate=cost(32 * count * n * n * 128, 16 * n * 128 * count, 2 * count * n * n),
        name="attend_back",
    )(mask, *qkv, o, go, lse)


def load_wout(slots, place_ref, w, sem):
    wide = w.shape[1]
    start = slots[0].shape[1] - wide
    copies = place_rows(slots, w, place_ref, sem, -start, (start, wide))

    @pl.when(pl.program_id(0) == 0)
    def _():
        for c in copies:
            c.start()
        for c in copies:
            c.wait()


def out_kernel(n, place_ref, x_ref, bias_ref, gain_ref, shift_ref, *refs):
    slots, o_refs, (m_ref, b_ref, w, sem) = refs[:n], refs[n:-4], refs[-4:]
    load_wout(slots, place_ref, w, sem)
    m = x_ref[...].astype(f32) + bias_ref[...]
    first = 0
    for o_ref in o_refs:
        m = m + dot(o_ref[...], w[first : first + o_ref.shape[1], :], NN)
        first += o_ref.shape[1]
    m_ref[...] = m
    xh, _ = norm_parts(m)
    b_ref[...] = (xh * gain_ref[...] + shift_ref[...]).astype(bf16)


def out_call(place, x, o_parts, slots, bias, gain, shift):
    rows, width = x.shape
    n = len(slots)
    vec = fixed((1, width))
    block = rowed(ROWS, width)
    return pl.pallas_call(
        partial(out_kernel, n),
        grid_spec=pltpu.PrefetchScalarGridSpec(
            num_scalar_prefetch=1,
            grid=(rows // ROWS,),
            in_specs=[block, vec, vec, vec]
            + [ANY] * n
            + [rowed(ROWS, o.shape[1]) for o in o_parts],
            out_specs=[block, block],
            scratch_shapes=[pltpu.VMEM((width, width), bf16), pltpu.SemaphoreType.DMA((n,))],
        ),
        out_shape=[shape((rows, width), f32), shape((rows, width), bf16)],
        compiler_params=params(),
        cost_estimate=cost(4 * rows * width * width, width * (10 * rows + 2 * width)),
        name="out",
    )(place, x, bias, gain, shift, *slots, *o_parts)


def gelu_both(z, gh):
    t = 1.0 / (1.0 + jnp.abs(z) * (0.3275911 / math.sqrt(2.0)))
    e = jnp.exp(z * z * -0.5)
    half = (0.254829592, -0.284496736, 1.421413741, -1.453152027, 1.061405429)
    tail = half[4] * 0.5
    for c in half[3::-1]:
        tail = tail * t + 0.5 * c
    tail = tail * t * e
    phi = jnp.where(z > 0, 1.0 - tail, tail)
    return z * phi, gh * (phi + z * e * (1.0 / math.sqrt(2.0 * math.pi)))


def ffn_kernel(n, later, *refs):
    b_own, b_sib, g_own, g_sib, ub_ref = refs[:5]
    slots = refs[5 : 5 + n]
    refs = refs[5 + n :]
    if later:
        acc_o, acc_g = refs[:2]
        refs = refs[2:]
        h_ref, gz_ref, sum_ref, oo_ref, go_ref, os_ref, gs_ref, us, ds, sem = refs
    else:
        h_ref, gz_ref, sum_ref, oo_ref, go_ref, us, ds, sem = refs
    units = us.shape[0] // n
    i = pl.program_id(0)
    near = i < pl.num_programs(0) // 2
    copies = []
    for s, slot in enumerate(slots):
        rows = pl.ds(s * units, units)
        copies.append(
            pltpu.make_async_copy(slot.at[pl.ds(0, units), :], us.at[rows, :], sem.at[0, s])
        )
        copies.append(
            pltpu.make_async_copy(slot.at[pl.ds(units, units), :], ds.at[rows, :], sem.at[1, s])
        )

    @pl.when(i == 0)
    def _():
        for c in copies:
            c.start()
        for c in copies:
            c.wait()
        sum_ref[...] = jnp.zeros_like(sum_ref)

    b = jnp.where(near, b_own[...], b_sib[...])
    g = jnp.where(near, g_own[...], g_sib[...])
    h, gz = gelu_both(dot(b, us[...], NT) + ub_ref[...], dot(g, ds[...], NT))
    h, gz = h.astype(bf16), gz.astype(bf16)
    h_ref[...] = h
    gz_ref[...] = gz
    sum_ref[...] += colsum(gz.astype(f32))
    out = dot(h, ds[...], NN)
    back = dot(gz, us[...], NN)
    if not later:
        oo_ref[...] = out
        go_ref[...] = back
        return
    out = out + acc_o[...]
    back = back + acc_g[...]

    @pl.when(near)
    def _():
        oo_ref[...] = out.astype(bf16)
        go_ref[...] = back.astype(bf16)

    @pl.when(jnp.logical_not(near))
    def _():
        os_ref[...] = out.astype(bf16)
        gs_ref[...] = back.astype(bf16)


def ffn_call(b_own, b_sib, g_own, g_sib, ub, slots, acc=None):
    rows, width = b_own.shape
    half = rows // ROWS
    n = len(slots)
    units = ub.shape[1]
    later = acc is not None
    near = pl.BlockSpec((ROWS, width), lambda i: (jnp.minimum(i, half - 1), 0))
    far = pl.BlockSpec((ROWS, width), lambda i: (jnp.maximum(i - half, 0), 0))
    both = rowed(ROWS, width)
    acc = list(acc or ())
    out_specs = [rowed(ROWS, units), rowed(ROWS, units), fixed((1, units))]
    out_shape = [shape((2 * rows, units), bf16)] * 2 + [shape((1, units), f32)]
    if later:
        out_specs += [near, near, far, far]
        out_shape += [shape((rows, width), bf16)] * 4
    else:
        out_specs += [both, both]
        out_shape += [shape((2 * rows, width), f32)] * 2
    return pl.pallas_call(
        partial(ffn_kernel, n, later),
        grid=(2 * half,),
        in_specs=[near, far, near, far, fixed((1, units))] + [ANY] * n + [both] * len(acc),
        out_specs=out_specs,
        out_shape=out_shape,
        scratch_shapes=[
            pltpu.VMEM((units, width), bf16),
            pltpu.VMEM((units, width), bf16),
            pltpu.SemaphoreType.DMA((2, n)),
        ],
        compiler_params=params(),
        cost_estimate=cost(
            24 * rows * width * units, rows * width * (24 + 16 * later), 4 * rows * units
        ),
        name="ffn",
    )(b_own, b_sib, g_own, g_sib, ub, *slots, *acc)


def ffn_weights_kernel(n, gz, h, b_own, b_sib, g_own, g_sib, *refs):
    outs = refs[:n]
    lv, rv, ov, lsem, rsem, osem = refs[n:]
    rows = b_own.shape[0]
    units = outs[0].shape[0] // 2
    loads = []
    for which, (left, parts) in enumerate(((gz, (b_own, b_sib)), (h, (g_own, g_sib)))):
        loads.append(pltpu.make_async_copy(left, lv.at[which], lsem.at[which]))
        for j, part in enumerate(parts):
            loads.append(
                pltpu.make_async_copy(
                    part, rv.at[which, pl.ds(j * rows, rows), :], rsem.at[which, j]
                )
            )
    for c in loads:
        c.start()
    stores = []
    step = 0
    for which in range(2):
        for c in loads[3 * which : 3 * which + 3]:
            c.wait()
        for pair in range(n // 2):
            slot = step % 2
            if step >= 2:
                for c in stores[2 * (step - 2) : 2 * (step - 2) + 2]:
                    c.wait()
            cols = pl.ds(pair * 2 * units, 2 * units)
            ov[slot] = dot(lv[which, :, cols], rv[which], TN).astype(bf16)
            for j in range(2):
                c = pltpu.make_async_copy(
                    ov.at[slot, pl.ds(j * units, units), :],
                    outs[2 * pair + j].at[pl.ds(which * units, units), :],
                    osem.at[slot, j],
                )
                c.start()
                stores.append(c)
            step += 1
    for c in stores[2 * (step - 2) :]:
        c.wait()


def ffn_weights_call(gz, h, b_own, b_sib, g_own, g_sib, n):
    rows, units = gz.shape
    width = b_own.shape[1]
    return pl.pallas_call(
        partial(ffn_weights_kernel, n),
        in_specs=[ANY] * 6,
        out_specs=[ANY] * n,
        out_shape=[shape((2 * units // n, width), bf16)] * n,
        scratch_shapes=[
            pltpu.VMEM((2, rows, units), bf16),
            pltpu.VMEM((2, rows, width), bf16),
            pltpu.VMEM((2, 2 * units // n, width), bf16),
            pltpu.SemaphoreType.DMA((2,)),
            pltpu.SemaphoreType.DMA((2, 2)),
            pltpu.SemaphoreType.DMA((2, 2)),
        ],
        compiler_params=params(),
        cost_estimate=cost(6 * rows * units * width, 4 * rows * (units + width)),
        name="ffn_weights",
    )(gz, h, b_own, b_sib, g_own, g_sib)


def mid_kernel(
    n, place_ref, oo_ref, os_ref, go_ref, gs_ref, m_ref, g_ref, keep_ref, db_ref, gain_ref, *refs
):
    slots, (hid_ref, gr_ref, gatt_ref, sums_ref, w, sem) = refs[:n], refs[n:]
    load_wout(slots, place_ref, w, sem)

    @pl.when(pl.program_id(0) == 0)
    def _():
        sums_ref[...] = jnp.zeros_like(sums_ref)

    m = m_ref[...]
    g = g_ref[...].astype(f32)
    ff = oo_ref[...].astype(f32) + os_ref[...].astype(f32)
    hid_ref[...] = (m + ff + db_ref[...]).astype(bf16)
    gb = go_ref[...].astype(f32) + gs_ref[...].astype(f32)
    xh, scale = norm_parts(m)
    gm = g + norm_back(xh, scale, gain_ref[...], gb)
    gr = gm.astype(bf16)
    gr_ref[...] = gr
    gatt_ref[...] = (dot(gr, w[...], NT) * keep_ref[...]).astype(bf16)
    sums_ref[0:1, :] += colsum(gb * xh)
    sums_ref[1:2, :] += colsum(gb)
    sums_ref[2:3, :] += colsum(gr.astype(f32))
    sums_ref[3:4, :] += colsum(g)


def mid_call(place, oo, os, go, gs, m, g, keep, db, gain, slots):
    rows, width = m.shape
    n = len(slots)
    block = rowed(ROWS, width)
    vec = fixed((1, width))
    return pl.pallas_call(
        partial(mid_kernel, n),
        grid_spec=pltpu.PrefetchScalarGridSpec(
            num_scalar_prefetch=1,
            grid=(rows // ROWS,),
            in_specs=[block] * 6 + [rowed(ROWS, 1), vec, vec] + [ANY] * n,
            out_specs=[block] * 3 + [fixed((8, width))],
            scratch_shapes=[pltpu.VMEM((width, width), bf16), pltpu.SemaphoreType.DMA((n,))],
        ),
        out_shape=[shape((rows, width), bf16)] * 3 + [shape((8, width), f32)],
        compiler_params=params(),
        cost_estimate=cost(4 * rows * width * width, width * (30 * rows + 2 * width)),
        name="mid",
    )(place, oo, os, go, gs, m, g, keep, db, gain, *slots)


def att_weights_kernel(n, counts, blocks, place_ref, *refs):
    lefts, at = [], 0
    for count in counts[:-1]:
        lefts.append(refs[at : at + count])
        at += count
    rights, refs = refs[at : at + counts[-1]], refs[at + counts[-1] :]
    outs, (lv, tv, rv, ov, lsem, rsem, osem) = refs[: n + 1], refs[n + 1 :]
    height = outs[0].shape[0]
    loads = []
    for i, pieces in enumerate(lefts):
        loads.append([])
        at = 0
        for j, r in enumerate(pieces):
            wide = r.shape[1]
            loads[-1].append(
                pltpu.make_async_copy(r, lv.at[i, :, pl.ds(at, wide)], lsem.at[i, j])
            )
            at += wide
    ends, right_loads = [], []
    for i, r in enumerate(rights):
        start = ends[-1] if ends else 0
        ends.append(start + r.shape[1])
        right_loads.append(
            pltpu.make_async_copy(r, rv.at[:, pl.ds(start, r.shape[1])], rsem.at[i])
        )
    for c in loads[0] + right_loads + [c for group in loads[1:] for c in group]:
        c.start()
    have, arrived = set(), 0
    stores = []
    for step, (left, start, wide) in enumerate(blocks):
        if left not in have:
            for c in loads[left]:
                c.wait()
            tv[left] = jnp.transpose(lv[left])
            have.add(left)
        while arrived < len(ends) and (arrived == 0 or ends[arrived - 1] < start + wide):
            right_loads[arrived].wait()
            arrived += 1
        slot = step % 2
        if step >= 2:
            for c in stores[step - 2]:
                c.wait()
        cols = pl.ds(start, wide)
        ov[slot, :, pl.ds(0, wide)] = dot(tv[left], rv[:, cols], NN).astype(bf16)
        stores.append([])
        for i in range(2 * n):
            rows = pl.ds(pl.multiple_of(place_ref[i] * height, 16), height)
            goal = outs[i].at[:, cols] if i < n else outs[n].at[i - n, :, cols]
            c = pltpu.make_async_copy(ov.at[slot, rows, pl.ds(0, wide)], goal, osem.at[slot, i])
            c.start()
            stores[-1].append(c)
    for group in stores[-2:]:
        for c in group:
            c.wait()


def att_weights_call(place, lefts, rights, blocks):
    rows, width = lefts[0][0].shape[0], sum(l.shape[1] for l in lefts[0])
    n = len(OFFSETS)
    total = sum(r.shape[1] for r in rights)
    wide = max(b[2] for b in blocks)
    height = width // (2 * n)
    return pl.pallas_call(
        partial(att_weights_kernel, n, [len(l) for l in lefts] + [len(rights)], blocks),
        grid_spec=pltpu.PrefetchScalarGridSpec(
            num_scalar_prefetch=1,
            grid=(1,),
            in_specs=[ANY] * (sum(len(l) for l in lefts) + len(rights)),
            out_specs=[ANY] * (n + 1),
            scratch_shapes=[
                pltpu.VMEM((len(lefts), rows, width), bf16),
                pltpu.VMEM((len(lefts), width, rows), bf16),
                pltpu.VMEM((rows, total), bf16),
                pltpu.VMEM((2, width, wide), bf16),
                pltpu.SemaphoreType.DMA((len(lefts), max(len(l) for l in lefts))),
                pltpu.SemaphoreType.DMA((len(rights),)),
                pltpu.SemaphoreType.DMA((2, 2 * n)),
            ],
        ),
        out_shape=[shape((height, total), bf16)] * n + [shape((n, height, total), bf16)],
        compiler_params=params(),
        cost_estimate=cost(3 * rows * width * total, 2 * (rows + width) * total),
        name="att_weights",
    )(place, *[a for l in lefts for a in l], *rights)


def in_kernel(n, pieces, place_ref, x_ref, gr_ref, gain_ref, *refs):
    grads, slots = refs[:pieces], refs[pieces : pieces + n]
    res_ref, sums_ref, w, sem = refs[pieces + n :]
    copies = place_rows(slots, w, place_ref, sem, cols=(0, w.shape[1]))

    @pl.when(pl.program_id(0) == 0)
    def _():
        for c in copies:
            c.start()
        for c in copies:
            c.wait()
        sums_ref[...] = jnp.zeros_like(sums_ref)

    ga = None
    col = 0
    for r in grads:
        part = dot(r[...], w[:, col : col + r.shape[1]], NT)
        ga = part if ga is None else ga + part
        col += r.shape[1]
    xh, scale = norm_parts(x_ref[...].astype(f32))
    res = gr_ref[...].astype(f32) + norm_back(xh, scale, gain_ref[...], ga)
    sums_ref[0:1, :] += colsum(ga * xh)
    sums_ref[1:2, :] += colsum(ga)
    res_ref[...] = res.astype(res_ref.dtype)


def in_call(place, x, gr, gain, grads, slots, part, dtype):
    rows, width = x.shape
    n = len(slots)
    half = rows // ROWS // 2

    def piece(w):
        return pl.BlockSpec((ROWS, w), lambda i, *_: (i + part * half, 0))

    return pl.pallas_call(
        partial(in_kernel, n, len(grads)),
        grid_spec=pltpu.PrefetchScalarGridSpec(
            num_scalar_prefetch=1,
            grid=(half,),
            in_specs=[piece(width), piece(width), fixed((1, width))]
            + [piece(g.shape[1]) for g in grads]
            + [ANY] * n,
            out_specs=[rowed(ROWS, width), fixed((8, width))],
            scratch_shapes=[
                pltpu.VMEM((width, 3 * width), bf16),
                pltpu.SemaphoreType.DMA((n,)),
            ],
        ),
        out_shape=[shape((rows // 2, width), dtype), shape((8, width), f32)],
        compiler_params=params(),
        cost_estimate=cost(4 * rows * width * width, width * (7 * rows + 6 * width)),
        name="in",
    )(place, x, gr, gain, *grads, *slots)


def fence(*trees):
    return lax.optimization_barrier(trees)


def side_by_side(vectors):
    total = sum(v.shape[0] for v in vectors)
    res, at = None, 0
    for v in vectors:
        wide = jnp.pad(v, (at, total - at - v.shape[0]))
        at += v.shape[0]
        res = wide if res is None else res + wide
    return res


def local_swapped(
    sizes, hidden_in, lengths, ln1_gain, ln1_bias, w_qkv, q_bias, v_bias, w_out, out_bias, ln2_gain, ln2_bias,
    w_up, up_bias, w_down, down_bias, cotangent,
):
    ring = Ring(sizes)
    blk = lax.axis_index("blk")
    core = lax.axis_index("cell") % 2
    genes, width = hidden_in.shape[1:]
    units = w_up.shape[0]
    shards = ring.cells
    n = len(OFFSETS)

    def vec(v):
        return v.reshape(1, -1)

    def pick(x, which):
        return lax.dynamic_index_in_dim(x, which, 0, keepdims=False)

    chips_own, chips_sib = ring.chips_of_slots(core), ring.chips_of_slots(1 - core)
    shard_own = 2 * chips_own + core
    shard_sib = 2 * chips_sib + 1 - core
    place = jnp.concatenate([shard_own, shard_sib])
    index = jnp.arange(genes, dtype=jnp.int32)
    index = jnp.concatenate([blk * genes + index, (1 - blk) * genes + index])
    keep = (index < pick(lengths, blk)).astype(f32)[:, None]
    mask = jnp.where(keep > 0, 0.0, far_below)

    x_got = ring.swap_blk(pick(hidden_in, 1 - blk))
    steps = ring.gather(jnp.concatenate([w_qkv, w_out], axis=1), 2)
    slots, sib = next(steps), [None] * n
    w_pair = jnp.concatenate([w_up, w_down], axis=0)
    g_send = pick(cotangent, 1 - blk)
    small = [vec(v) for v in (ln1_gain, ln1_bias, q_bias, v_bias, out_bias, ln2_gain, ln2_bias)]
    small += [place, mask, keep]
    slots[1], slots[5] = fence(slots[1], slots[5])
    slots = steps.send(slots)
    slots[2], slots[6], small, x_got, w_pair = fence(slots[2], slots[6], small, x_got, w_pair)
    ln1_gain, ln1_bias, q_bias, v_bias, out_bias, ln2_gain, ln2_bias, place, mask, keep = small
    slots = steps.send(slots)
    for s in (0, 1, 5, 2, 6):
        sib[s] = ring.swap_core(slots[s])
    x = jnp.concatenate([pick(hidden_in, blk), x_got], axis=0)
    slots[3], x, sib, g_send = fence(slots[3], x, sib, g_send)
    slots = steps.send(slots)
    for s in (3, 4, 7):
        sib[s] = ring.swap_core(slots[s])
    slots[4], w_pair = fence(slots[4], w_pair)
    pair = [w_pair, ring.shift(w_pair, 1)] + [None] * 6
    g_send, slots[7] = fence(g_send, slots[7])
    g_send = [g_send[: genes // 2], g_send[genes // 2 :]]
    g_got = [ring.swap_blk(g_send[0])]

    weights = slots + sib
    a, *qkv = qkv_call(place, x, ln1_gain, ln1_bias, q_bias, v_bias, weights)
    qkv, pair[1], g_got, g_send = fence(qkv, pair[1], g_got, g_send)
    g_got.append(ring.swap_blk(g_send[1]))
    pair[2] = ring.shift(pair[1], 1)
    pairs = width // 128
    cut = 6 * pairs // 10
    attended = [attend_call(mask, keep, qkv, 0, cut)]
    attended, qkv, pair[2], g_got = fence(attended, qkv, pair[2], g_got)
    pair[3] = ring.shift(pair[2], 1)
    g = jnp.concatenate([pick(cotangent, blk)] + g_got, axis=0)
    g_sib = ring.swap_core(g)
    attended.append(attend_call(mask, keep, qkv, cut, pairs - cut))
    o_parts = [t[0] for t in attended]
    m, b = out_call(place, x, o_parts, weights, out_bias, ln2_gain, ln2_bias)
    b, g_sib, pair[0], pair[3] = fence(b, g_sib, pair[0], pair[3])
    b_sib = ring.swap_core(b)
    pair[4] = ring.shift(pair[3], 1)
    pair[5] = ring.shift(pair[0], -1)
    pair[7] = ring.swap_blk(pair[3])

    ub = up_bias.reshape(shards, units)[shard_own]
    near, far = (0, 1, 2, 3), (4, 5, 6, 7)
    ub_near, ub_far = [vec(jnp.concatenate([ub[s] for s in group])) for group in (near, far)]
    h_near, gz_near, sum_near, *acc = ffn_call(
        b, b_sib, g, g_sib, ub_near, [pair[s] for s in near]
    )
    h_near, gz_near, acc, pair[5] = fence(h_near, gz_near, acc, pair[5])
    pair[6] = ring.shift(pair[5], -1)
    parts = [None] * n
    made = ffn_weights_call(gz_near, h_near, b, b_sib, g, g_sib, len(near))
    made, acc = fence(made, acc)
    for s, t in zip(near, made, strict=True):
        parts[s] = [t]
    h_far, gz_far, sum_far, oo, gb_own, os_send, gs_send = ffn_call(
        b, b_sib, g, g_sib, ub_far, [pair[s] for s in far], acc
    )
    up_sums = dict(
        zip(near + far, jnp.split(sum_near[0], 4) + jnp.split(sum_far[0], 4), strict=True)
    )
    mine = shard_own[None, :] == jnp.arange(shards, dtype=jnp.int32)[:, None]
    up_rows = jnp.sum(
        jnp.where(mine[:, :, None], jnp.stack([up_sums[s] for s in range(n)])[None], 0.0), axis=1
    )
    made = ffn_weights_call(gz_far, h_far, b, b_sib, g, g_sib, len(far))
    os_got, gs_got = ring.swap_core(os_send), ring.swap_core(gs_send)
    made, oo, os_got, gs_got = fence(made, oo, os_got, gs_got)
    for s, t in zip(far, made, strict=True):
        parts[s] = [t]
    steps = ring.reduce(parts, 1)
    way = next(steps)
    out_hidden, gr, gatt, mid_sums = mid_call(
        place, oo, os_got, gb_own, gs_got, m, g, keep, vec(down_bias), ln2_gain, weights
    )
    hid_send = [out_hidden[genes : genes + genes // 2], out_hidden[genes + genes // 2 :]]

    def back(first, count, gatt):
        o, lse = attended[0 if first < cut else 1]
        at = first if first < cut else first - cut
        return attend_back_call(mask, qkv, o, gatt, lse, count, (first, at, first))

    early, half = 128 * cut, width // 2
    late = width - early
    backs = [back(0, cut, gatt)]
    backs, gatt, way["ahead"], way["over3"], hid_send = fence(
        backs, gatt, way["ahead"], way["over3"], hid_send
    )
    way = steps.send(way)
    first = att_weights_call(
        place, [[a], o_parts], list(backs[0][:3]) + [gr],
        [(0, i * early, early) for i in range(3)] + [(1, 3 * early + i * half, half) for i in range(2)],
    )
    first, gatt, way, hid_send = fence(first, gatt, way, hid_send)
    way = steps.send(way)
    hid_got = [ring.swap_blk(hid_send[0])]
    first_sib = ring.swap_core(first[n])
    one = (pairs - cut) // 4
    backs.append(back(cut, one, gatt))
    backs, gatt, first, first_sib, up_rows = fence(backs, gatt, first, first_sib, up_rows)
    steps_first = ring.reduce([[first[s], first_sib[s]] for s in range(n)], 3)
    way_first = next(steps_first)
    backs.append(back(cut + one, pairs - cut - one, gatt))
    backs, way_first, way, hid_got, hid_send = fence(backs, way_first, way, hid_got, hid_send)
    way_first = steps_first.send(way_first)
    hid_got.append(ring.swap_blk(hid_send[1]))
    way = steps.send(way)
    grads = [t[i] for i in range(3) for t in backs]
    in_send, in_sums_send = in_call(place, x, gr, ln1_gain, grads, weights, 1, bf16)
    sums_early = side_by_side(
        [mid_sums[:4].reshape(-1), up_rows.reshape(-1)]
        + [t[i].reshape(-1) for i in (3, 4) for t in backs]
    )
    in_send, backs, way_first, hid_got, way = fence(in_send, backs, way_first, hid_got, way)
    ffn_sum = steps.send(way)
    ffn_sum = [ffn_sum[:units], ffn_sum[units:]]
    ffn_got = [ring.swap_blk(ffn_sum[0])]
    way_first = steps_first.send(way_first)
    in_got = ring.swap_blk(in_send)
    second = att_weights_call(
        place, [[a]], [t[i] for i in range(3) for t in backs[1:]],
        [(0, i * late, late) for i in range(3)],
    )
    second, way_first, grads, sums_early, ffn_got, ffn_sum = fence(
        second, way_first, grads, sums_early, ffn_got, ffn_sum
    )
    ffn_got.append(ring.swap_blk(ffn_sum[1]))
    way_first = steps_first.send(way_first)
    second_sib = ring.swap_core(second[n])
    steps_second = ring.reduce([[second[s], second_sib[s]] for s in range(n)], 3)
    way_second = next(steps_second)
    in_own, in_sums = in_call(place, x, gr, ln1_gain, grads, weights, 0, f32)
    in_own, in_sums, in_sums_send, way_first, way_second = fence(
        in_own, in_sums, in_sums_send, way_first, way_second
    )
    first_sum = steps_first.send(way_first)
    first_got = ring.swap_blk(first_sum)
    way_second = steps_second.send(way_second)
    ln1_sums = (in_sums + in_sums_send)[:2].reshape(-1)
    steps_sums = ring.total(side_by_side([sums_early, ln1_sums]))
    sums = next(steps_sums)
    sums = steps_sums.send(sums)
    way_second, sums = fence(way_second, sums)
    way_second = steps_second.send(way_second)
    sums = steps_sums.send(sums)
    way_second, sums = fence(way_second, sums)
    way_second = steps_second.send(way_second)
    sums = steps_sums.send(sums)
    way_second, sums = fence(way_second, sums)
    second_sum = steps_second.send(way_second)
    second_got = ring.swap_blk(second_sum)
    sums = steps_sums.send(sums)
    sums = steps_sums.send(sums)
    ffn_sum, ffn_got, first_sum, first_got, in_got = fence(
        ffn_sum, ffn_got, first_sum, first_got, in_got
    )
    sums_own, sums_got = ffn_sum + [first_sum, second_sum], ffn_got + [first_got, second_got]
    w_up_grad, w_down_grad, first_rows, second_rows = [
        a.astype(f32) + b.astype(f32) for a, b in zip(sums_own, sums_got, strict=True)
    ]

    def home(own, got):
        got = got.astype(own.dtype)
        return jnp.where(blk == 0, jnp.stack([own, got]), jnp.stack([got, own]))

    hidden = home(out_hidden[:genes], jnp.concatenate(hid_got))
    in_grad = home(in_own, in_got)
    marks = [width] * 4 + [shards * units]
    marks += 2 * [128 * c for c in (cut, one, pairs - cut - one)] + [width] * 2
    pieces, at = [], 0
    for size in marks:
        pieces.append(sums[at : at + size])
        at += size
    ln2_gain_g, ln2_bias_g, out_bias_g, down_bias_g, up_bias_g = pieces[:5]
    q_bias_g, v_bias_g = jnp.concatenate(pieces[5:8]), jnp.concatenate(pieces[8:11])
    ln1_gain_g, ln1_bias_g = pieces[11:]
    w_qkv_grad = jnp.concatenate(
        [
            t
            for i in range(3)
            for t in (
                first_rows[:, i * early : (i + 1) * early],
                second_rows[:, i * late : (i + 1) * late],
            )
        ],
        axis=1,
    )
    return (
        hidden,
        in_grad,
        ln1_gain_g,
        ln1_bias_g,
        w_qkv_grad,
        q_bias_g,
        v_bias_g,
        first_rows[:, 3 * early :],
        out_bias_g,
        ln2_gain_g,
        ln2_bias_g,
        w_up_grad,
        up_bias_g,
        w_down_grad,
        down_bias_g,
    )


def solution(mesh):
    placed = (
        P("cell", "blk", None),
        P("cell"),
        P(),
        P(),
        P("cell", None),
        P(),
        P(),
        P("cell", None),
        P(),
        P(),
        P(),
        P("cell", None),
        P(),
        P("cell", None),
        P(),
        P("cell", "blk", None),
    )
    return jax.shard_map(
        partial(local_swapped, dict(mesh.shape)) if swappable(mesh) else local,
        mesh=mesh,
        in_specs=placed,
        out_specs=(
            P("cell", "blk", None),
            P("cell", "blk", None),
            P(),
            P(),
            P("cell", None),
            P(),
            P(),
            P("cell", None),
            P(),
            P(),
            P(),
            P("cell", None),
            P(),
            P("cell", None),
            P(),
        ),
        check_vma=False,
    )
```

```python
from functools import partial
import math

import jax
import jax.numpy as jnp
from jax import lax
from jax.experimental import pallas as pl
from jax.experimental.pallas import tpu as pltpu
from jax.sharding import PartitionSpec as P

HEAD_DIM = 64


epsilon = 1e-05
far_below = -1e30
row_contract = (((0,), (0,)), ((), ()))
col_contract = (((1,), (1,)), ((), ()))


def passed_along(x, axis, by):
    count = lax.axis_size(axis)
    return lax.ppermute(x, axis, [(i, (i + by) % count) for i in range(count)])


def layer_norm(source, gain_vec, shift_vec):
    row_mean = jnp.mean(source, axis=-1, keepdims=True)
    centered = source - row_mean
    row_var = jnp.mean(centered * centered, axis=-1, keepdims=True)
    return centered * lax.rsqrt(row_var + epsilon) * gain_vec + shift_vec


def local(
    hidden_in,
    lengths,
    ln1_gain,
    ln1_bias,
    w_qkv,
    q_bias,
    v_bias,
    w_out,
    out_bias,
    ln2_gain,
    ln2_bias,
    w_up,
    up_bias,
    w_down,
    down_bias,
    cotangent,
):
    cell_count, local_genes, model_width = hidden_in.shape
    row_count = cell_count * local_genes
    head_count = model_width // HEAD_DIM
    score_scale = 1.0 / math.sqrt(HEAD_DIM)
    cycle_size = lax.axis_size("blk")
    cycle_place = lax.axis_index("blk")
    ratio_ff = up_bias.shape[0] // model_width
    head_shape = (cell_count, local_genes, head_count, HEAD_DIM)
    stat_shape = (cell_count, head_count, local_genes)
    inputs = hidden_in.astype(jnp.float32).reshape(row_count, model_width)
    cot_rows = cotangent.reshape(row_count, model_width)
    gene_index = jnp.arange(local_genes, dtype=jnp.int32)
    query_valid = (cycle_place * local_genes + gene_index)[None, :] < lengths[:, None]
    normed, ln1_pull = jax.vjp(layer_norm, inputs, ln1_gain, ln1_bias)
    normed_low = normed.astype(jnp.bfloat16)
    part_cols = normed_low
    joined = jnp.dot(
        part_cols,
        lax.all_gather(w_qkv, "cell", axis=0, tiled=True),
        preferred_element_type=jnp.float32,
    )
    queries = (joined[:, :model_width] + q_bias).astype(jnp.bfloat16).reshape(head_shape)
    keys_own = joined[:, model_width : 2 * model_width].astype(jnp.bfloat16).reshape(head_shape)
    values_own = (joined[:, 2 * model_width :] + v_bias).astype(jnp.bfloat16).reshape(head_shape)

    def block_scores(key_block, owner_index):
        scores = (
            jnp.einsum("cqhd,ckhd->chqk", queries, key_block, preferred_element_type=jnp.float32)
            * score_scale
        )
        key_valid = (owner_index * local_genes + gene_index)[None, :] < lengths[:, None]
        return (scores, key_valid[:, None, None, :])

    def stats_turn(owner_index, carried, key_block):
        row_top, row_total = carried
        scores, is_valid = block_scores(key_block, owner_index)
        new_top = jnp.maximum(row_top, jnp.max(jnp.where(is_valid, scores, far_below), axis=-1))
        raised = jnp.where(is_valid, jnp.exp(scores - new_top[..., None]), 0.0)
        return (new_top, row_total * jnp.exp(row_top - new_top) + jnp.sum(raised, axis=-1))

    first_stats = stats_turn(
        cycle_place,
        (jnp.full(stat_shape, far_below, jnp.float32), jnp.zeros(stat_shape, jnp.float32)),
        keys_own,
    )

    def stats_step(step_index, carried):
        stats_now, key_block = carried
        key_block = passed_along(key_block, "blk", 1)
        return (
            stats_turn((cycle_place - step_index) % cycle_size, stats_now, key_block),
            key_block,
        )

    final_stats = lax.fori_loop(1, cycle_size, stats_step, (first_stats, keys_own))[0]
    log_total = final_stats[0] + jnp.log(final_stats[1])

    def block_weights(key_block, owner_index):
        scores, is_valid = block_scores(key_block, owner_index)
        return jnp.where(is_valid, jnp.exp(scores - log_total[..., None]), 0.0)

    def mix_turn(owner_index, mixed_sum, key_block, value_block):
        weights = block_weights(key_block, owner_index).astype(jnp.bfloat16)
        return mixed_sum + jnp.einsum(
            "chqk,ckhd->cqhd", weights, value_block, preferred_element_type=jnp.float32
        )

    mixed_start = mix_turn(cycle_place, jnp.zeros(head_shape, jnp.float32), keys_own, values_own)

    def pair_step(step_index, carried):
        inner, key_block, value_block = carried
        key_block, value_block = passed_along((key_block, value_block), "blk", 1)
        return (
            mix_turn((cycle_place - step_index) % cycle_size, inner, key_block, value_block),
            key_block,
            value_block,
        )

    mixed_sum = lax.fori_loop(1, cycle_size, pair_step, (mixed_start, keys_own, values_own))[0]
    mixed_low = (
        jnp.where(query_valid[:, :, None, None], mixed_sum, 0.0)
        .astype(jnp.bfloat16)
        .reshape(row_count, model_width)
    )
    part_cols = mixed_low
    branch = jnp.dot(
        part_cols,
        lax.all_gather(w_out, "cell", axis=0, tiled=True),
        preferred_element_type=jnp.float32,
    )
    middle = inputs + branch + out_bias
    normed2, ln2_pull = jax.vjp(layer_norm, middle, ln2_gain, ln2_bias)
    normed2_low = normed2.astype(jnp.bfloat16)
    gelu_exact = partial(jax.nn.gelu, approximate=False)
    ff_total = up_bias.shape[0]
    out_sum = jnp.zeros((row_count, model_width), jnp.float32)
    ffn_hidden = jnp.zeros((row_count, ff_total), jnp.bfloat16)
    up_piece = lax.all_gather(w_up, "cell", axis=0, tiled=True)
    down_piece = lax.all_gather(w_down, "cell", axis=0, tiled=True)
    pre_gelu = lax.dot_general(
        normed2_low, up_piece, col_contract, preferred_element_type=jnp.float32
    )
    pre_gelu = pre_gelu + up_bias
    activation, gelu_pull = jax.vjp(gelu_exact, pre_gelu)
    active_low = activation.astype(jnp.bfloat16)
    out_sum = out_sum + jnp.dot(active_low, down_piece, preferred_element_type=jnp.float32)
    grad_active = lax.dot_general(
        cot_rows, down_piece, col_contract, preferred_element_type=jnp.float32
    )
    pre_low = gelu_pull(grad_active)[0].astype(jnp.bfloat16)
    back_sum = jnp.dot(pre_low, up_piece, preferred_element_type=jnp.float32)
    ffn_hidden = lax.dynamic_update_slice_in_dim(ffn_hidden, active_low, jnp.int32(0), 1)
    out_sum, back_sum, pre_grads, hidden = (out_sum, back_sum, pre_low, ffn_hidden)
    out_hidden = (middle + out_sum + down_bias).astype(jnp.bfloat16).reshape(hidden_in.shape)
    grad_ln2, ln2_gain_part, ln2_bias_part = ln2_pull(back_sum)
    grad_middle = cot_rows.astype(jnp.float32) + grad_ln2
    branch_grad = grad_middle.astype(jnp.bfloat16)
    grad_mixed = lax.dot_general(
        branch_grad,
        lax.all_gather(w_out, "cell", axis=0, tiled=True),
        col_contract,
        preferred_element_type=jnp.float32,
    )
    grad_out = jnp.where(
        query_valid[:, :, None, None], grad_mixed.astype(jnp.bfloat16).reshape(head_shape), 0.0
    )
    delta = jnp.einsum("cqhd,cqhd->chq", grad_out.astype(jnp.float32), mixed_sum)

    def grad_step(step_index, carried):
        query_grad, key_block, value_block, key_grad, value_grad = carried
        owner_index = (cycle_place - step_index) % cycle_size
        weights = block_weights(key_block, owner_index)
        grad_weights = jnp.einsum(
            "cqhd,ckhd->chqk", grad_out, value_block, preferred_element_type=jnp.float32
        )
        score_grad = (weights * (grad_weights - delta[..., None])).astype(jnp.bfloat16)
        query_grad = (
            query_grad
            + jnp.einsum(
                "chqk,ckhd->cqhd", score_grad, key_block, preferred_element_type=jnp.float32
            )
            * score_scale
        )
        key_grad = (
            key_grad
            + jnp.einsum("chqk,cqhd->ckhd", score_grad, queries, preferred_element_type=jnp.float32)
            * score_scale
        )
        value_grad = value_grad + jnp.einsum(
            "chqk,cqhd->ckhd",
            weights.astype(jnp.bfloat16),
            grad_out,
            preferred_element_type=jnp.float32,
        )
        key_block, value_block, key_grad, value_grad = (
            passed_along(key_block, "blk", 1),
            passed_along(value_block, "blk", 1),
            passed_along(key_grad.astype(jnp.bfloat16), "blk", 1).astype(key_grad.dtype),
            passed_along(value_grad.astype(jnp.bfloat16), "blk", 1).astype(value_grad.dtype),
        )
        return (query_grad, key_block, value_block, key_grad, value_grad)

    zero_heads = jnp.zeros(head_shape, jnp.float32)
    cycle_done = lax.fori_loop(
        0, cycle_size, grad_step, (zero_heads, keys_own, values_own, zero_heads, zero_heads)
    )
    query_low = cycle_done[0].astype(jnp.bfloat16).reshape(row_count, model_width)
    key_low = cycle_done[3].astype(jnp.bfloat16).reshape(row_count, model_width)
    value_low = cycle_done[4].astype(jnp.bfloat16).reshape(row_count, model_width)
    grad_joined = jnp.concatenate([query_low, key_low, value_low], axis=1)
    grad_normed = lax.dot_general(
        grad_joined,
        lax.all_gather(w_qkv, "cell", axis=0, tiled=True),
        col_contract,
        preferred_element_type=jnp.float32,
    )
    grad_ln1, ln1_gain_part, ln1_bias_part = ln1_pull(grad_normed)
    in_grad = (grad_middle + grad_ln1).reshape(hidden_in.shape)
    qkv_term = lax.dot_general(
        normed_low, grad_joined, row_contract, preferred_element_type=jnp.float32
    )
    out_term = lax.dot_general(
        mixed_low, branch_grad, row_contract, preferred_element_type=jnp.float32
    )
    up_term = lax.dot_general(
        pre_grads, normed2_low, row_contract, preferred_element_type=jnp.float32
    )
    down_term = lax.dot_general(hidden, cot_rows, row_contract, preferred_element_type=jnp.float32)
    ffn_term = jnp.concatenate([up_term, down_term], axis=1).reshape(
        lax.axis_size("cell") * (model_width // lax.axis_size("cell")), ratio_ff * 2 * model_width
    )
    summed = lax.psum_scatter(
        jnp.concatenate([qkv_term, out_term, ffn_term], axis=1).astype(jnp.bfloat16),
        "cell",
        scatter_dimension=0,
        tiled=True,
    ).astype(jnp.float32)
    summed = lax.psum(summed.astype(jnp.bfloat16), "blk").astype(jnp.float32)
    own_rows = summed.shape[0]
    w_qkv_grad = summed[:, : 3 * model_width]
    w_out_grad = summed[:, 3 * model_width : 4 * model_width]
    ffn_grads = summed[:, 4 * model_width :].reshape(own_rows * ratio_ff, 2 * model_width)
    w_up_grad = ffn_grads[:, :model_width]
    w_down_grad = ffn_grads[:, model_width:]
    vectors = lax.psum(
        (
            ln1_gain_part,
            ln1_bias_part,
            jnp.sum(query_low, axis=0, dtype=jnp.float32),
            jnp.sum(value_low, axis=0, dtype=jnp.float32),
            jnp.sum(branch_grad, axis=0, dtype=jnp.float32),
            ln2_gain_part,
            ln2_bias_part,
            jnp.sum(pre_grads, axis=0, dtype=jnp.float32),
            jnp.sum(cot_rows, axis=0, dtype=jnp.float32),
        ),
        ("cell", "blk"),
    )
    return (
        out_hidden,
        in_grad,
        vectors[0],
        vectors[1],
        w_qkv_grad,
        vectors[2],
        vectors[3],
        w_out_grad,
        vectors[4],
        vectors[5],
        vectors[6],
        w_up_grad,
        vectors[7],
        w_down_grad,
        vectors[8],
    )


bf16 = jnp.bfloat16
f32 = jnp.float32
NN = (((1,), (0,)), ((), ()))
NT = (((1,), (1,)), ((), ()))
TN = (((0,), (0,)), ((), ()))
AXES = ("cell", "blk")
VMEM_LIMIT = 60 * 2**20
ROWS = 256
COST_PART = 50
OFFSETS = (0, -1, -2, -3, -4, 1, 2, 3)


def swappable(mesh):
    return dict(mesh.shape) == {"cell": 16, "blk": 2}


def dot(a, b, dims):
    return lax.dot_general(a, b, dims, preferred_element_type=f32)


def params():
    return pltpu.CompilerParams(vmem_limit_bytes=VMEM_LIMIT)


def cost(flops, nbytes, trans=0):
    return pl.CostEstimate(
        flops=int(flops) // COST_PART,
        bytes_accessed=int(nbytes) // COST_PART,
        transcendentals=int(trans) // COST_PART,
    )


def shape(dims, dtype):
    return jax.ShapeDtypeStruct(dims, dtype)


ANY = pl.BlockSpec(memory_space=pl.ANY)


def fixed(dims):
    return pl.BlockSpec(dims, lambda *_: (0,) * len(dims))


def rowed(rows, width):
    return pl.BlockSpec((rows, width), lambda i, *_: (i, 0))


class Ring:
    def __init__(self, sizes):
        self.cells, self.blks = sizes["cell"], sizes["blk"]
        self.chips = self.cells // 2
        depth = self.chips // 2
        self.order = [2 * z for z in range(depth)] + [2 * z + 1 for z in reversed(range(depth))]
        self.place = [self.order.index(c) for c in range(self.chips)]

    def permute(self, x, target):
        pairs = []
        for cell in range(self.cells):
            for blk in range(self.blks):
                to_cell, to_blk = target(cell, blk)
                pairs.append((cell * self.blks + blk, to_cell * self.blks + to_blk))
        return lax.ppermute(x, AXES, pairs)

    def shift(self, x, by):
        def target(cell, blk):
            chip, core = cell // 2, cell % 2
            way = 1 - 2 * ((core + blk) % 2)
            return self.order[(self.place[chip] + way * by) % self.chips] * 2 + core, blk

        return self.permute(x, target)

    def swap_core(self, x):
        return self.permute(x, lambda cell, blk: (cell ^ 1, blk))

    def swap_blk(self, x):
        return self.permute(x, lambda cell, blk: (cell, 1 - blk))

    def chips_of_slots(self, core):
        chip = lax.axis_index("cell") // 2
        way = 1 - 2 * ((core + lax.axis_index("blk")) % 2)
        place = jnp.array(self.place, jnp.int32)[chip]
        return jnp.array(self.order, jnp.int32)[
            (place + way * jnp.array(OFFSETS, jnp.int32)) % self.chips
        ]

    def gather(self, x, back):
        slots = [x] + [None] * 7
        for k in range(1, 5):
            slots[k] = self.shift(slots[k - 1], 1)
            if k <= back:
                slots[4 + k] = self.shift(slots[3 + k] if k > 1 else slots[0], -1)
            if k > back + 1:
                slots[3 + k] = self.swap_blk(slots[k - 1])
            slots = yield slots

    def reduce(self, parts, back, alone=False):
        def added(terms):
            total = terms[0].astype(f32)
            for t in terms[1:]:
                total = total + t.astype(f32)
            return total.astype(bf16)

        way = {"ahead": self.shift(added(parts[4]), -1)}
        if back:
            way["behind"] = self.shift(added(parts[4 + back]), 1)
        for k in range(3, back, -1):
            way[f"over{k}"] = self.swap_blk(added(parts[4 + k]))
        way = yield way
        for k in (3, 2, 1):
            extra = [way.pop(f"over{k}")] if f"over{k}" in way else []
            way["ahead"] = self.shift(added([way["ahead"]] + parts[k] + extra), -1)
            if k < back and not (alone and k == 1):
                way["behind"] = self.shift(added([way["behind"]] + parts[4 + k]), 1)
            way = yield way
        if alone:
            way["behind"] = self.shift(added([way["behind"]] + parts[5]), 1)
            way = yield way
        ends = [way["ahead"]] + ([way["behind"]] if back else [])
        yield added(ends + parts[0])

    def total(self, x):
        count = self.cells * self.blks
        bits = [1 << i for i in range(count.bit_length() - 1)]
        for bit in [b for b in bits if b >= self.blks] + [b for b in bits if b < self.blks]:
            other = bit
            moved = self.permute(
                x, lambda cell, blk: divmod((cell * self.blks + blk) ^ other, self.blks)
            )
            x, moved = yield x, moved
            x = x + moved
        yield x


def norm_parts(x):
    mean = jnp.mean(x, axis=-1, keepdims=True)
    centered = x - mean
    var = jnp.mean(centered * centered, axis=-1, keepdims=True)
    scale = lax.rsqrt(var + epsilon)
    return centered * scale, scale


def norm_back(xh, scale, gain, grad):
    e = grad * gain
    return scale * (
        e - jnp.mean(e, axis=-1, keepdims=True) - xh * jnp.mean(e * xh, axis=-1, keepdims=True)
    )


def colsum(x):
    return jnp.sum(x, axis=0, keepdims=True)


def place_rows(slots, target, place_ref, sem, first=0, cols=None):
    height = slots[0].shape[0]
    start, wide = cols or (0, slots[0].shape[1])
    return [
        pltpu.make_async_copy(
            slot.at[:, pl.ds(start, wide)],
            target.at[
                pl.ds(pl.multiple_of(place_ref[i] * height, 16), height),
                pl.ds(first + start, wide),
            ],
            sem.at[i],
        )
        for i, slot in enumerate(slots)
    ]


def qkv_kernel(n, place_ref, x_ref, gain_ref, bias_ref, qb_ref, vb_ref, *refs):
    slots, (a_ref, q_ref, k_ref, v_ref, w, sem) = refs[:n], refs[n:]
    width = x_ref.shape[1]
    first = pl.program_id(0) == 0
    copies = [
        place_rows(slots, w, place_ref, sem.at[j], cols=(j * width, width)) for j in range(3)
    ]

    @pl.when(first)
    def _():
        for group in copies:
            for c in group:
                c.start()

    xh, _ = norm_parts(x_ref[...].astype(f32))
    a_ref[...] = (xh * gain_ref[...] + bias_ref[...]).astype(bf16)
    for j, (res_ref, add_ref) in enumerate(((q_ref, qb_ref), (k_ref, None), (v_ref, vb_ref))):

        @pl.when(first)
        def _(group=copies[j]):
            for c in group:
                c.wait()

        res = dot(a_ref[...], w[:, j * width : (j + 1) * width], NN)
        if add_ref is not None:
            res = res + add_ref[...]
        res_ref[...] = res.astype(bf16)


def qkv_call(place, x, gain, bias, qb, vb, slots):
    rows, width = x.shape
    n = len(slots)
    block = rowed(ROWS, width)
    vec = fixed((1, width))
    return pl.pallas_call(
        partial(qkv_kernel, n),
        grid_spec=pltpu.PrefetchScalarGridSpec(
            num_scalar_prefetch=1,
            grid=(rows // ROWS,),
            in_specs=[block, vec, vec, vec, vec] + [ANY] * n,
            out_specs=[block] * 4,
            scratch_shapes=[
                pltpu.VMEM((width, 3 * width), bf16),
                pltpu.SemaphoreType.DMA((3, n)),
            ],
        ),
        out_shape=[shape((rows, width), bf16)] * 4,
        compiler_params=params(),
        cost_estimate=cost(6 * rows * width * width, 2 * width * (5 * rows + 3 * width)),
        name="qkv",
    )(place, x, gain, bias, qb, vb, *slots)


def head_keys(low, k, v, mask, fill):
    res = []
    for half in range(2):
        mine = low if half == 0 else jnp.logical_not(low)
        res.append(
            (
                jnp.where(mine, k.astype(f32), mask).astype(bf16),
                jnp.where(mine, v.astype(f32), fill).astype(bf16),
            )
        )
    return res


def head_query(low, lane, half, q):
    mine = low if half == 0 else jnp.logical_not(low)
    one = lane == (HEAD_DIM if half == 0 else 0)
    q = q.astype(f32) * (1.0 / math.sqrt(HEAD_DIM))
    return jnp.where(mine, q, jnp.where(one, 1.0, 0.0)).astype(bf16)


def attend_kernel(qrows, ahead, mask_ref, keep_ref, q_ref, k_ref, v_ref, o_ref, lse_ref):
    n = q_ref.shape[0]
    lane = lax.broadcasted_iota(jnp.int32, (n, 128), 1)
    pair = head_keys(lane < HEAD_DIM, k_ref[...], v_ref[...], mask_ref[...], 1.0)
    lane = lane[:qrows]
    low = lane < HEAD_DIM
    items = [(i, half) for i in range(n // qrows) for half in range(2)]

    def scores(i, half):
        q = head_query(low, lane, half, q_ref[pl.ds(i * qrows, qrows), :])
        return dot(q, pair[half][0], NT)

    waiting = [scores(*item) for item in items[:ahead]]
    for at, (i, half) in enumerate(items):
        if at + ahead < len(items):
            waiting.append(scores(*items[at + ahead]))
        s = waiting.pop(0)
        rows = pl.ds(i * qrows, qrows)
        top = jnp.max(s, axis=1, keepdims=True)
        mixed = dot(jnp.exp(s - top).astype(bf16), pair[half][1], NN)
        total = pltpu.roll(mixed, HEAD_DIM, 1)
        o, lse = mixed / total, top + jnp.log(total)
        if half == 0:
            o_first, lse_first = o, lse
            continue
        o_ref[rows, :] = (jnp.where(low, o_first, o) * keep_ref[rows, :]).astype(bf16)
        lse = jnp.transpose(jnp.where(low, lse_first, lse))
        lse_ref[0, :, rows] = lse[:1, :]
        lse_ref[1, :, rows] = lse[HEAD_DIM : HEAD_DIM + 1, :]


def attend_call(mask, keep, qkv, first, count, qrows=256, ahead=2):
    n = qkv[0].shape[0]
    block = pl.BlockSpec((n, 128), lambda h: (0, h + first))
    return pl.pallas_call(
        partial(attend_kernel, qrows, ahead),
        grid=(count,),
        in_specs=[fixed((n, 1)), fixed((n, 1)), block, block, block],
        out_specs=[
            pl.BlockSpec((n, 128), lambda h: (0, h)),
            pl.BlockSpec((2, 1, n), lambda h: (h, 0, 0)),
        ],
        out_shape=[shape((n, 128 * count), bf16), shape((2 * count, 1, n), f32)],
        compiler_params=params(),
        cost_estimate=cost(20 * count * n * n * 128, 8 * n * 128 * count, 2 * count * n * n),
        name="attend",
    )(mask, keep, *qkv)


def attend_back_kernel(
    qrows, mask_ref, q_ref, k_ref, v_ref, o_ref, go_ref, lse_ref,
    gq_ref, gk_ref, gv_ref, sq_ref, sv_ref, gk_sum, gv_sum,
):
    n = q_ref.shape[0]
    lane = lax.broadcasted_iota(jnp.int32, (n, 128), 1)
    k = k_ref[...]
    scale = 1.0 / math.sqrt(HEAD_DIM)
    pair = head_keys(lane < HEAD_DIM, k, v_ref[...], mask_ref[...], 0.0)
    k_turned = jnp.transpose(k)
    prod = jnp.transpose(o_ref[...].astype(f32) * go_ref[...].astype(f32))
    delta = [colsum(prod[half * HEAD_DIM : (half + 1) * HEAD_DIM, :]) for half in range(2)]
    top = lane[:qrows]
    for i in range(n // qrows):
        rows = pl.ds(i * qrows, qrows)
        gq = []
        for half in range(2):
            q_raw, go = q_ref[rows, :], go_ref[rows, :]
            q = head_query(top < HEAD_DIM, top, half, q_raw)
            p = jnp.exp(dot(pair[half][0], q, NT) - lse_ref[half, :, rows])
            gp = dot(pair[half][1], go, NT)
            gs = (p * (gp - delta[half][:, i * qrows : (i + 1) * qrows])).astype(bf16)
            gv = dot(p.astype(bf16), go, NN)
            gk = dot(gs, q_raw, NN)
            if i == 0:
                gv_sum[half], gk_sum[half] = gv, gk
            else:
                gv_sum[half] += gv
                gk_sum[half] += gk
            gq.append(dot(k_turned, gs, NN))
        turned = jnp.concatenate([gq[0][:HEAD_DIM], gq[1][HEAD_DIM:]], axis=0)
        gq_ref[rows, :] = jnp.transpose(turned * scale).astype(bf16)
    low = lane < HEAD_DIM
    gk_ref[...] = (jnp.where(low, gk_sum[0], gk_sum[1]) * scale).astype(bf16)
    gv = jnp.where(low, gv_sum[0], gv_sum[1]).astype(bf16)
    gv_ref[...] = gv
    sq_ref[...] = colsum(gq_ref[...].astype(f32))
    sv_ref[...] = colsum(gv.astype(f32))


def attend_back_call(mask, qkv, o, go, lse, count, firsts, qrows=512):
    n = go.shape[0]

    def block(first):
        return pl.BlockSpec((n, 128), lambda h: (0, h + first))

    own, vec = block(0), pl.BlockSpec((1, 128), lambda h: (0, h))
    at_qkv, at_o, at_go = firsts
    return pl.pallas_call(
        partial(attend_back_kernel, qrows),
        grid=(count,),
        in_specs=[fixed((n, 1))]
        + [block(at_qkv)] * 3
        + [block(at_o), block(at_go), pl.BlockSpec((2, 1, n), lambda h: (h + at_o, 0, 0))],
        out_specs=[own, own, own, vec, vec],
        out_shape=[shape((n, 128 * count), bf16)] * 3 + [shape((1, 128 * count), f32)] * 2,
        scratch_shapes=[pltpu.VMEM((2, n, 128), f32)] * 2,
        compiler_params=params(),
        cost_estimate=cost(32 * count * n * n * 128, 16 * n * 128 * count, 2 * count * n * n),
        name="attend_back",
    )(mask, *qkv, o, go, lse)


def load_wout(slots, place_ref, w, sem):
    wide = w.shape[1]
    start = slots[0].shape[1] - wide
    copies = place_rows(slots, w, place_ref, sem, -start, (start, wide))

    @pl.when(pl.program_id(0) == 0)
    def _():
        for c in copies:
            c.start()
        for c in copies:
            c.wait()


def out_kernel(n, place_ref, x_ref, bias_ref, gain_ref, shift_ref, *refs):
    slots, o_refs, (m_ref, b_ref, w, sem) = refs[:n], refs[n:-4], refs[-4:]
    load_wout(slots, place_ref, w, sem)
    m = x_ref[...].astype(f32) + bias_ref[...]
    first = 0
    for o_ref in o_refs:
        m = m + dot(o_ref[...], w[first : first + o_ref.shape[1], :], NN)
        first += o_ref.shape[1]
    m_ref[...] = m
    xh, _ = norm_parts(m)
    b_ref[...] = (xh * gain_ref[...] + shift_ref[...]).astype(bf16)


def out_call(place, x, o_parts, slots, bias, gain, shift):
    rows, width = x.shape
    n = len(slots)
    vec = fixed((1, width))
    block = rowed(ROWS, width)
    return pl.pallas_call(
        partial(out_kernel, n),
        grid_spec=pltpu.PrefetchScalarGridSpec(
            num_scalar_prefetch=1,
            grid=(rows // ROWS,),
            in_specs=[block, vec, vec, vec]
            + [ANY] * n
            + [rowed(ROWS, o.shape[1]) for o in o_parts],
            out_specs=[block, block],
            scratch_shapes=[pltpu.VMEM((width, width), bf16), pltpu.SemaphoreType.DMA((n,))],
        ),
        out_shape=[shape((rows, width), f32), shape((rows, width), bf16)],
        compiler_params=params(),
        cost_estimate=cost(4 * rows * width * width, width * (10 * rows + 2 * width)),
        name="out",
    )(place, x, bias, gain, shift, *slots, *o_parts)


def gelu_both(z, gh):
    t = 1.0 / (1.0 + jnp.abs(z) * (0.3275911 / math.sqrt(2.0)))
    e = jnp.exp(z * z * -0.5)
    half = (0.254829592, -0.284496736, 1.421413741, -1.453152027, 1.061405429)
    tail = half[4] * 0.5
    for c in half[3::-1]:
        tail = tail * t + 0.5 * c
    tail = tail * t * e
    phi = jnp.where(z > 0, 1.0 - tail, tail)
    return z * phi, gh * (phi + z * e * (1.0 / math.sqrt(2.0 * math.pi)))


def ffn_kernel(n, later, *refs):
    b_own, b_sib, g_own, g_sib, ub_ref = refs[:5]
    slots = refs[5 : 5 + n]
    refs = refs[5 + n :]
    if later:
        acc_o, acc_g = refs[:2]
        refs = refs[2:]
        h_ref, gz_ref, sum_ref, oo_ref, go_ref, os_ref, gs_ref, us, ds, sem = refs
    else:
        h_ref, gz_ref, sum_ref, oo_ref, go_ref, us, ds, sem = refs
    units = us.shape[0] // n
    i = pl.program_id(0)
    near = i < pl.num_programs(0) // 2
    copies = []
    for s, slot in enumerate(slots):
        rows = pl.ds(s * units, units)
        copies.append(
            pltpu.make_async_copy(slot.at[pl.ds(0, units), :], us.at[rows, :], sem.at[0, s])
        )
        copies.append(
            pltpu.make_async_copy(slot.at[pl.ds(units, units), :], ds.at[rows, :], sem.at[1, s])
        )

    @pl.when(i == 0)
    def _():
        for c in copies:
            c.start()
        for c in copies:
            c.wait()
        sum_ref[...] = jnp.zeros_like(sum_ref)

    b = jnp.where(near, b_own[...], b_sib[...])
    g = jnp.where(near, g_own[...], g_sib[...])
    h, gz = gelu_both(dot(b, us[...], NT) + ub_ref[...], dot(g, ds[...], NT))
    h, gz = h.astype(bf16), gz.astype(bf16)
    h_ref[...] = h
    gz_ref[...] = gz
    sum_ref[...] += colsum(gz.astype(f32))
    out = dot(h, ds[...], NN)
    back = dot(gz, us[...], NN)
    if not later:
        oo_ref[...] = out
        go_ref[...] = back
        return
    out = out + acc_o[...]
    back = back + acc_g[...]

    @pl.when(near)
    def _():
        oo_ref[...] = out.astype(bf16)
        go_ref[...] = back.astype(bf16)

    @pl.when(jnp.logical_not(near))
    def _():
        os_ref[...] = out.astype(bf16)
        gs_ref[...] = back.astype(bf16)


def ffn_call(b_own, b_sib, g_own, g_sib, ub, slots, acc=None):
    rows, width = b_own.shape
    half = rows // ROWS
    n = len(slots)
    units = ub.shape[1]
    later = acc is not None
    near = pl.BlockSpec((ROWS, width), lambda i: (jnp.minimum(i, half - 1), 0))
    far = pl.BlockSpec((ROWS, width), lambda i: (jnp.maximum(i - half, 0), 0))
    both = rowed(ROWS, width)
    acc = list(acc or ())
    out_specs = [rowed(ROWS, units), rowed(ROWS, units), fixed((1, units))]
    out_shape = [shape((2 * rows, units), bf16)] * 2 + [shape((1, units), f32)]
    if later:
        out_specs += [near, near, far, far]
        out_shape += [shape((rows, width), bf16)] * 4
    else:
        out_specs += [both, both]
        out_shape += [shape((2 * rows, width), f32)] * 2
    return pl.pallas_call(
        partial(ffn_kernel, n, later),
        grid=(2 * half,),
        in_specs=[near, far, near, far, fixed((1, units))] + [ANY] * n + [both] * len(acc),
        out_specs=out_specs,
        out_shape=out_shape,
        scratch_shapes=[
            pltpu.VMEM((units, width), bf16),
            pltpu.VMEM((units, width), bf16),
            pltpu.SemaphoreType.DMA((2, n)),
        ],
        compiler_params=params(),
        cost_estimate=cost(
            24 * rows * width * units, rows * width * (24 + 16 * later), 4 * rows * units
        ),
        name="ffn",
    )(b_own, b_sib, g_own, g_sib, ub, *slots, *acc)


def ffn_weights_kernel(n, gz, h, b_own, b_sib, g_own, g_sib, *refs):
    outs = refs[:n]
    lv, rv, ov, lsem, rsem, osem = refs[n:]
    rows = b_own.shape[0]
    units = outs[0].shape[0] // 2
    loads = []
    for which, (left, parts) in enumerate(((gz, (b_own, b_sib)), (h, (g_own, g_sib)))):
        loads.append(pltpu.make_async_copy(left, lv.at[which], lsem.at[which]))
        for j, part in enumerate(parts):
            loads.append(
                pltpu.make_async_copy(
                    part, rv.at[which, pl.ds(j * rows, rows), :], rsem.at[which, j]
                )
            )
    for c in loads:
        c.start()
    stores = []
    step = 0
    for which in range(2):
        for c in loads[3 * which : 3 * which + 3]:
            c.wait()
        for pair in range(n // 2):
            slot = step % 2
            if step >= 2:
                for c in stores[2 * (step - 2) : 2 * (step - 2) + 2]:
                    c.wait()
            cols = pl.ds(pair * 2 * units, 2 * units)
            ov[slot] = dot(lv[which, :, cols], rv[which], TN).astype(bf16)
            for j in range(2):
                c = pltpu.make_async_copy(
                    ov.at[slot, pl.ds(j * units, units), :],
                    outs[2 * pair + j].at[pl.ds(which * units, units), :],
                    osem.at[slot, j],
                )
                c.start()
                stores.append(c)
            step += 1
    for c in stores[2 * (step - 2) :]:
        c.wait()


def ffn_weights_call(gz, h, b_own, b_sib, g_own, g_sib, n):
    rows, units = gz.shape
    width = b_own.shape[1]
    return pl.pallas_call(
        partial(ffn_weights_kernel, n),
        in_specs=[ANY] * 6,
        out_specs=[ANY] * n,
        out_shape=[shape((2 * units // n, width), bf16)] * n,
        scratch_shapes=[
            pltpu.VMEM((2, rows, units), bf16),
            pltpu.VMEM((2, rows, width), bf16),
            pltpu.VMEM((2, 2 * units // n, width), bf16),
            pltpu.SemaphoreType.DMA((2,)),
            pltpu.SemaphoreType.DMA((2, 2)),
            pltpu.SemaphoreType.DMA((2, 2)),
        ],
        compiler_params=params(),
        cost_estimate=cost(6 * rows * units * width, 4 * rows * (units + width)),
        name="ffn_weights",
    )(gz, h, b_own, b_sib, g_own, g_sib)


def mid_kernel(
    n, place_ref, oo_ref, os_ref, go_ref, gs_ref, m_ref, g_ref, keep_ref, db_ref, gain_ref, *refs
):
    slots, (hid_ref, gr_ref, gatt_ref, sums_ref, w, sem) = refs[:n], refs[n:]
    load_wout(slots, place_ref, w, sem)

    @pl.when(pl.program_id(0) == 0)
    def _():
        sums_ref[...] = jnp.zeros_like(sums_ref)

    m = m_ref[...]
    g = g_ref[...].astype(f32)
    ff = oo_ref[...].astype(f32) + os_ref[...].astype(f32)
    hid_ref[...] = (m + ff + db_ref[...]).astype(bf16)
    gb = go_ref[...].astype(f32) + gs_ref[...].astype(f32)
    xh, scale = norm_parts(m)
    gm = g + norm_back(xh, scale, gain_ref[...], gb)
    gr = gm.astype(bf16)
    gr_ref[...] = gr
    gatt_ref[...] = (dot(gr, w[...], NT) * keep_ref[...]).astype(bf16)
    sums_ref[0:1, :] += colsum(gb * xh)
    sums_ref[1:2, :] += colsum(gb)
    sums_ref[2:3, :] += colsum(gr.astype(f32))
    sums_ref[3:4, :] += colsum(g)


def mid_call(place, oo, os, go, gs, m, g, keep, db, gain, slots):
    rows, width = m.shape
    n = len(slots)
    block = rowed(ROWS, width)
    vec = fixed((1, width))
    return pl.pallas_call(
        partial(mid_kernel, n),
        grid_spec=pltpu.PrefetchScalarGridSpec(
            num_scalar_prefetch=1,
            grid=(rows // ROWS,),
            in_specs=[block] * 6 + [rowed(ROWS, 1), vec, vec] + [ANY] * n,
            out_specs=[block] * 3 + [fixed((8, width))],
            scratch_shapes=[pltpu.VMEM((width, width), bf16), pltpu.SemaphoreType.DMA((n,))],
        ),
        out_shape=[shape((rows, width), bf16)] * 3 + [shape((8, width), f32)],
        compiler_params=params(),
        cost_estimate=cost(4 * rows * width * width, width * (30 * rows + 2 * width)),
        name="mid",
    )(place, oo, os, go, gs, m, g, keep, db, gain, *slots)


def att_weights_kernel(n, counts, blocks, place_ref, *refs):
    lefts, at = [], 0
    for count in counts[:-1]:
        lefts.append(refs[at : at + count])
        at += count
    rights, refs = refs[at : at + counts[-1]], refs[at + counts[-1] :]
    outs, (lv, tv, rv, ov, lsem, rsem, osem) = refs[: n + 1], refs[n + 1 :]
    height = outs[0].shape[0]
    loads = []
    for i, pieces in enumerate(lefts):
        loads.append([])
        at = 0
        for j, r in enumerate(pieces):
            wide = r.shape[1]
            loads[-1].append(
                pltpu.make_async_copy(r, lv.at[i, :, pl.ds(at, wide)], lsem.at[i, j])
            )
            at += wide
    ends, right_loads = [], []
    for i, r in enumerate(rights):
        start = ends[-1] if ends else 0
        ends.append(start + r.shape[1])
        right_loads.append(
            pltpu.make_async_copy(r, rv.at[:, pl.ds(start, r.shape[1])], rsem.at[i])
        )
    for c in loads[0] + right_loads + [c for group in loads[1:] for c in group]:
        c.start()
    have, arrived = set(), 0
    stores = []
    for step, (left, start, wide) in enumerate(blocks):
        if left not in have:
            for c in loads[left]:
                c.wait()
            tv[left] = jnp.transpose(lv[left])
            have.add(left)
        while arrived < len(ends) and (arrived == 0 or ends[arrived - 1] < start + wide):
            right_loads[arrived].wait()
            arrived += 1
        slot = step % 2
        if step >= 2:
            for c in stores[step - 2]:
                c.wait()
        cols = pl.ds(start, wide)
        ov[slot, :, pl.ds(0, wide)] = dot(tv[left], rv[:, cols], NN).astype(bf16)
        stores.append([])
        for i in range(2 * n):
            rows = pl.ds(pl.multiple_of(place_ref[i] * height, 16), height)
            goal = outs[i].at[:, cols] if i < n else outs[n].at[i - n, :, cols]
            c = pltpu.make_async_copy(ov.at[slot, rows, pl.ds(0, wide)], goal, osem.at[slot, i])
            c.start()
            stores[-1].append(c)
    for group in stores[-2:]:
        for c in group:
            c.wait()


def att_weights_call(place, lefts, rights, blocks):
    rows, width = lefts[0][0].shape[0], sum(l.shape[1] for l in lefts[0])
    n = len(OFFSETS)
    total = sum(r.shape[1] for r in rights)
    wide = max(b[2] for b in blocks)
    height = width // (2 * n)
    return pl.pallas_call(
        partial(att_weights_kernel, n, [len(l) for l in lefts] + [len(rights)], blocks),
        grid_spec=pltpu.PrefetchScalarGridSpec(
            num_scalar_prefetch=1,
            grid=(1,),
            in_specs=[ANY] * (sum(len(l) for l in lefts) + len(rights)),
            out_specs=[ANY] * (n + 1),
            scratch_shapes=[
                pltpu.VMEM((len(lefts), rows, width), bf16),
                pltpu.VMEM((len(lefts), width, rows), bf16),
                pltpu.VMEM((rows, total), bf16),
                pltpu.VMEM((2, width, wide), bf16),
                pltpu.SemaphoreType.DMA((len(lefts), max(len(l) for l in lefts))),
                pltpu.SemaphoreType.DMA((len(rights),)),
                pltpu.SemaphoreType.DMA((2, 2 * n)),
            ],
        ),
        out_shape=[shape((height, total), bf16)] * n + [shape((n, height, total), bf16)],
        compiler_params=params(),
        cost_estimate=cost(3 * rows * width * total, 2 * (rows + width) * total),
        name="att_weights",
    )(place, *[a for l in lefts for a in l], *rights)


def in_kernel(n, pieces, place_ref, x_ref, gr_ref, gain_ref, *refs):
    grads, slots = refs[:pieces], refs[pieces : pieces + n]
    res_ref, sums_ref, w, sem = refs[pieces + n :]
    copies = place_rows(slots, w, place_ref, sem, cols=(0, w.shape[1]))

    @pl.when(pl.program_id(0) == 0)
    def _():
        for c in copies:
            c.start()
        for c in copies:
            c.wait()
        sums_ref[...] = jnp.zeros_like(sums_ref)

    ga = None
    col = 0
    for r in grads:
        part = dot(r[...], w[:, col : col + r.shape[1]], NT)
        ga = part if ga is None else ga + part
        col += r.shape[1]
    xh, scale = norm_parts(x_ref[...].astype(f32))
    res = gr_ref[...].astype(f32) + norm_back(xh, scale, gain_ref[...], ga)
    sums_ref[0:1, :] += colsum(ga * xh)
    sums_ref[1:2, :] += colsum(ga)
    res_ref[...] = res.astype(res_ref.dtype)


def in_call(place, x, gr, gain, grads, slots, part, dtype):
    rows, width = x.shape
    n = len(slots)
    half = rows // ROWS // 2

    def piece(w):
        return pl.BlockSpec((ROWS, w), lambda i, *_: (i + part * half, 0))

    return pl.pallas_call(
        partial(in_kernel, n, len(grads)),
        grid_spec=pltpu.PrefetchScalarGridSpec(
            num_scalar_prefetch=1,
            grid=(half,),
            in_specs=[piece(width), piece(width), fixed((1, width))]
            + [piece(g.shape[1]) for g in grads]
            + [ANY] * n,
            out_specs=[rowed(ROWS, width), fixed((8, width))],
            scratch_shapes=[
                pltpu.VMEM((width, 3 * width), bf16),
                pltpu.SemaphoreType.DMA((n,)),
            ],
        ),
        out_shape=[shape((rows // 2, width), dtype), shape((8, width), f32)],
        compiler_params=params(),
        cost_estimate=cost(4 * rows * width * width, width * (7 * rows + 6 * width)),
        name="in",
    )(place, x, gr, gain, *grads, *slots)


def fence(*trees):
    return lax.optimization_barrier(trees)


def side_by_side(vectors):
    total = sum(v.shape[0] for v in vectors)
    res, at = None, 0
    for v in vectors:
        wide = jnp.pad(v, (at, total - at - v.shape[0]))
        at += v.shape[0]
        res = wide if res is None else res + wide
    return res


def local_swapped(
    sizes, hidden_in, lengths, ln1_gain, ln1_bias, w_qkv, q_bias, v_bias, w_out, out_bias, ln2_gain, ln2_bias,
    w_up, up_bias, w_down, down_bias, cotangent,
):
    ring = Ring(sizes)
    blk = lax.axis_index("blk")
    core = lax.axis_index("cell") % 2
    genes, width = hidden_in.shape[1:]
    units = w_up.shape[0]
    shards = ring.cells
    n = len(OFFSETS)

    def vec(v):
        return v.reshape(1, -1)

    def pick(x, which):
        return lax.dynamic_index_in_dim(x, which, 0, keepdims=False)

    chips_own, chips_sib = ring.chips_of_slots(core), ring.chips_of_slots(1 - core)
    shard_own = 2 * chips_own + core
    shard_sib = 2 * chips_sib + 1 - core
    place = jnp.concatenate([shard_own, shard_sib])
    index = jnp.arange(genes, dtype=jnp.int32)
    index = jnp.concatenate([blk * genes + index, (1 - blk) * genes + index])
    keep = (index < pick(lengths, blk)).astype(f32)[:, None]
    mask = jnp.where(keep > 0, 0.0, far_below)

    x_got = ring.swap_blk(pick(hidden_in, 1 - blk))
    steps = ring.gather(jnp.concatenate([w_qkv, w_out], axis=1), 2)
    slots, sib = next(steps), [None] * n
    w_pair = jnp.concatenate([w_up, w_down], axis=0)
    g_send = pick(cotangent, 1 - blk)
    small = [vec(v) for v in (ln1_gain, ln1_bias, q_bias, v_bias, out_bias, ln2_gain, ln2_bias)]
    small += [place, mask, keep]
    slots[1], slots[5] = fence(slots[1], slots[5])
    slots = steps.send(slots)
    slots[2], slots[6], small, x_got, w_pair = fence(slots[2], slots[6], small, x_got, w_pair)
    ln1_gain, ln1_bias, q_bias, v_bias, out_bias, ln2_gain, ln2_bias, place, mask, keep = small
    slots = steps.send(slots)
    for s in (0, 1, 5, 2, 6):
        sib[s] = ring.swap_core(slots[s])
    x = jnp.concatenate([pick(hidden_in, blk), x_got], axis=0)
    slots[3], x, sib, g_send = fence(slots[3], x, sib, g_send)
    slots = steps.send(slots)
    for s in (3, 4, 7):
        sib[s] = ring.swap_core(slots[s])
    slots[4], w_pair = fence(slots[4], w_pair)
    pair = [w_pair, ring.shift(w_pair, 1)] + [None] * 6
    g_send, slots[7] = fence(g_send, slots[7])
    g_send = [g_send[: genes // 2], g_send[genes // 2 :]]
    g_got = [ring.swap_blk(g_send[0])]

    weights = slots + sib
    a, *qkv = qkv_call(place, x, ln1_gain, ln1_bias, q_bias, v_bias, weights)
    qkv, pair[1], g_got, g_send = fence(qkv, pair[1], g_got, g_send)
    g_got.append(ring.swap_blk(g_send[1]))
    pair[2] = ring.shift(pair[1], 1)
    pairs = width // 128
    cut = 6 * pairs // 10
    attended = [attend_call(mask, keep, qkv, 0, cut)]
    attended, qkv, pair[2], g_got = fence(attended, qkv, pair[2], g_got)
    pair[3] = ring.shift(pair[2], 1)
    g = jnp.concatenate([pick(cotangent, blk)] + g_got, axis=0)
    g_sib = ring.swap_core(g)
    attended.append(attend_call(mask, keep, qkv, cut, pairs - cut))
    o_parts = [t[0] for t in attended]
    m, b = out_call(place, x, o_parts, weights, out_bias, ln2_gain, ln2_bias)
    b, g_sib, pair[0], pair[3] = fence(b, g_sib, pair[0], pair[3])
    b_sib = ring.swap_core(b)
    pair[4] = ring.shift(pair[3], 1)
    pair[5] = ring.shift(pair[0], -1)
    pair[7] = ring.swap_blk(pair[3])

    ub = up_bias.reshape(shards, units)[shard_own]
    near, far = (0, 1, 2, 3), (4, 5, 6, 7)
    ub_near, ub_far = [vec(jnp.concatenate([ub[s] for s in group])) for group in (near, far)]
    h_near, gz_near, sum_near, *acc = ffn_call(
        b, b_sib, g, g_sib, ub_near, [pair[s] for s in near]
    )
    h_near, gz_near, acc, pair[5] = fence(h_near, gz_near, acc, pair[5])
    pair[6] = ring.shift(pair[5], -1)
    parts = [None] * n
    made = ffn_weights_call(gz_near, h_near, b, b_sib, g, g_sib, len(near))
    made, acc = fence(made, acc)
    for s, t in zip(near, made, strict=True):
        parts[s] = [t]
    h_far, gz_far, sum_far, oo, gb_own, os_send, gs_send = ffn_call(
        b, b_sib, g, g_sib, ub_far, [pair[s] for s in far], acc
    )
    up_sums = dict(
        zip(near + far, jnp.split(sum_near[0], 4) + jnp.split(sum_far[0], 4), strict=True)
    )
    mine = shard_own[None, :] == jnp.arange(shards, dtype=jnp.int32)[:, None]
    up_rows = jnp.sum(
        jnp.where(mine[:, :, None], jnp.stack([up_sums[s] for s in range(n)])[None], 0.0), axis=1
    )
    made = ffn_weights_call(gz_far, h_far, b, b_sib, g, g_sib, len(far))
    os_got, gs_got = ring.swap_core(os_send), ring.swap_core(gs_send)
    made, oo, os_got, gs_got = fence(made, oo, os_got, gs_got)
    for s, t in zip(far, made, strict=True):
        parts[s] = [t]
    steps = ring.reduce(parts, 1)
    way = next(steps)
    out_hidden, gr, gatt, mid_sums = mid_call(
        place, oo, os_got, gb_own, gs_got, m, g, keep, vec(down_bias), ln2_gain, weights
    )
    hid_send = [out_hidden[genes : genes + genes // 2], out_hidden[genes + genes // 2 :]]

    def back(first, count, gatt):
        o, lse = attended[0 if first < cut else 1]
        at = first if first < cut else first - cut
        return attend_back_call(mask, qkv, o, gatt, lse, count, (first, at, first))

    early, half = 128 * cut, width // 2
    late = width - early
    backs = [back(0, cut, gatt)]
    backs, gatt, way["ahead"], way["over3"], hid_send = fence(
        backs, gatt, way["ahead"], way["over3"], hid_send
    )
    way = steps.send(way)
    first = att_weights_call(
        place, [[a], o_parts], list(backs[0][:3]) + [gr],
        [(0, i * early, early) for i in range(3)] + [(1, 3 * early + i * half, half) for i in range(2)],
    )
    first, gatt, way, hid_send = fence(first, gatt, way, hid_send)
    way = steps.send(way)
    hid_got = [ring.swap_blk(hid_send[0])]
    first_sib = ring.swap_core(first[n])
    one = (pairs - cut) // 4
    backs.append(back(cut, one, gatt))
    backs, gatt, first, first_sib, up_rows = fence(backs, gatt, first, first_sib, up_rows)
    steps_first = ring.reduce([[first[s], first_sib[s]] for s in range(n)], 3)
    way_first = next(steps_first)
    backs.append(back(cut + one, pairs - cut - one, gatt))
    backs, way_first, way, hid_got, hid_send = fence(backs, way_first, way, hid_got, hid_send)
    way_first = steps_first.send(way_first)
    hid_got.append(ring.swap_blk(hid_send[1]))
    way = steps.send(way)
    grads = [t[i] for i in range(3) for t in backs]
    in_send, in_sums_send = in_call(place, x, gr, ln1_gain, grads, weights, 1, bf16)
    sums_early = side_by_side(
        [mid_sums[:4].reshape(-1), up_rows.reshape(-1)]
        + [t[i].reshape(-1) for i in (3, 4) for t in backs]
    )
    in_send, backs, way_first, hid_got, way = fence(in_send, backs, way_first, hid_got, way)
    ffn_sum = steps.send(way)
    ffn_sum = [ffn_sum[:units], ffn_sum[units:]]
    ffn_got = [ring.swap_blk(ffn_sum[0])]
    way_first = steps_first.send(way_first)
    in_got = ring.swap_blk(in_send)
    second = att_weights_call(
        place, [[a]], [t[i] for i in range(3) for t in backs[1:]],
        [(0, i * late, late) for i in range(3)],
    )
    second, way_first, grads, sums_early, ffn_got, ffn_sum = fence(
        second, way_first, grads, sums_early, ffn_got, ffn_sum
    )
    ffn_got.append(ring.swap_blk(ffn_sum[1]))
    way_first = steps_first.send(way_first)
    second_sib = ring.swap_core(second[n])
    steps_second = ring.reduce([[second[s], second_sib[s]] for s in range(n)], 3)
    way_second = next(steps_second)
    in_own, in_sums = in_call(place, x, gr, ln1_gain, grads, weights, 0, f32)
    w_up_grad = ffn_sum[0].astype(f32) + ffn_got[0].astype(f32)
    in_own, in_sums, in_sums_send, way_first, way_second, w_up_grad = fence(
        in_own, in_sums, in_sums_send, way_first, way_second, w_up_grad
    )
    first_sum = steps_first.send(way_first)
    first_got = ring.swap_blk(first_sum)
    way_second = steps_second.send(way_second)
    ln1_sums = (in_sums + in_sums_send)[:2].reshape(-1)
    steps_sums = ring.total(side_by_side([sums_early, ln1_sums]))
    sums = next(steps_sums)
    sums = steps_sums.send(sums)
    way_second, sums = fence(way_second, sums)
    way_second = steps_second.send(way_second)
    sums = steps_sums.send(sums)
    way_second, sums = fence(way_second, sums)
    way_second = steps_second.send(way_second)
    sums = steps_sums.send(sums)
    way_second, sums = fence(way_second, sums)
    second_sum = steps_second.send(way_second)
    second_got = ring.swap_blk(second_sum)
    sums = steps_sums.send(sums)
    down_sum, down_got, first_sum, first_got, in_got, second_sum, _ = fence(
        ffn_sum[1], ffn_got[1], first_sum, first_got, in_got, second_sum, sums[0]
    )
    sums = steps_sums.send(sums)
    w_down_grad, first_rows, second_rows = [
        a.astype(f32) + b.astype(f32)
        for a, b in ((down_sum, down_got), (first_sum, first_got), (second_sum, second_got))
    ]

    def home(own, got):
        got = got.astype(own.dtype)
        return jnp.where(blk == 0, jnp.stack([own, got]), jnp.stack([got, own]))

    hidden = home(out_hidden[:genes], jnp.concatenate(hid_got))
    in_grad = home(in_own, in_got)
    marks = [width] * 4 + [shards * units]
    marks += 2 * [128 * c for c in (cut, one, pairs - cut - one)] + [width] * 2
    pieces, at = [], 0
    for size in marks:
        pieces.append(sums[at : at + size])
        at += size
    ln2_gain_g, ln2_bias_g, out_bias_g, down_bias_g, up_bias_g = pieces[:5]
    q_bias_g, v_bias_g = jnp.concatenate(pieces[5:8]), jnp.concatenate(pieces[8:11])
    ln1_gain_g, ln1_bias_g = pieces[11:]
    w_qkv_grad = jnp.concatenate(
        [
            t
            for i in range(3)
            for t in (
                first_rows[:, i * early : (i + 1) * early],
                second_rows[:, i * late : (i + 1) * late],
            )
        ],
        axis=1,
    )
    return (
        hidden,
        in_grad,
        ln1_gain_g,
        ln1_bias_g,
        w_qkv_grad,
        q_bias_g,
        v_bias_g,
        first_rows[:, 3 * early :],
        out_bias_g,
        ln2_gain_g,
        ln2_bias_g,
        w_up_grad,
        up_bias_g,
        w_down_grad,
        down_bias_g,
    )


def solution(mesh):
    placed = (
        P("cell", "blk", None),
        P("cell"),
        P(),
        P(),
        P("cell", None),
        P(),
        P(),
        P("cell", None),
        P(),
        P(),
        P(),
        P("cell", None),
        P(),
        P("cell", None),
        P(),
        P("cell", "blk", None),
    )
    return jax.shard_map(
        partial(local_swapped, dict(mesh.shape)) if swappable(mesh) else local,
        mesh=mesh,
        in_specs=placed,
        out_specs=(
            P("cell", "blk", None),
            P("cell", "blk", None),
            P(),
            P(),
            P("cell", None),
            P(),
            P(),
            P("cell", None),
            P(),
            P(),
            P(),
            P("cell", None),
            P(),
            P("cell", None),
            P(),
        ),
        check_vma=False,
    )
```

```python
from functools import partial
import math

import jax
import jax.numpy as jnp
from jax import lax
from jax.experimental import pallas as pl
from jax.experimental.pallas import tpu as pltpu
from jax.sharding import PartitionSpec as P

HEAD_DIM = 64


epsilon = 1e-05
far_below = -1e30
row_contract = (((0,), (0,)), ((), ()))
col_contract = (((1,), (1,)), ((), ()))


def passed_along(x, axis, by):
    count = lax.axis_size(axis)
    return lax.ppermute(x, axis, [(i, (i + by) % count) for i in range(count)])


def layer_norm(source, gain_vec, shift_vec):
    row_mean = jnp.mean(source, axis=-1, keepdims=True)
    centered = source - row_mean
    row_var = jnp.mean(centered * centered, axis=-1, keepdims=True)
    return centered * lax.rsqrt(row_var + epsilon) * gain_vec + shift_vec


def local(
    hidden_in,
    lengths,
    ln1_gain,
    ln1_bias,
    w_qkv,
    q_bias,
    v_bias,
    w_out,
    out_bias,
    ln2_gain,
    ln2_bias,
    w_up,
    up_bias,
    w_down,
    down_bias,
    cotangent,
):
    cell_count, local_genes, model_width = hidden_in.shape
    row_count = cell_count * local_genes
    head_count = model_width // HEAD_DIM
    score_scale = 1.0 / math.sqrt(HEAD_DIM)
    cycle_size = lax.axis_size("blk")
    cycle_place = lax.axis_index("blk")
    ratio_ff = up_bias.shape[0] // model_width
    head_shape = (cell_count, local_genes, head_count, HEAD_DIM)
    stat_shape = (cell_count, head_count, local_genes)
    inputs = hidden_in.astype(jnp.float32).reshape(row_count, model_width)
    cot_rows = cotangent.reshape(row_count, model_width)
    gene_index = jnp.arange(local_genes, dtype=jnp.int32)
    query_valid = (cycle_place * local_genes + gene_index)[None, :] < lengths[:, None]
    normed, ln1_pull = jax.vjp(layer_norm, inputs, ln1_gain, ln1_bias)
    normed_low = normed.astype(jnp.bfloat16)
    part_cols = normed_low
    joined = jnp.dot(
        part_cols,
        lax.all_gather(w_qkv, "cell", axis=0, tiled=True),
        preferred_element_type=jnp.float32,
    )
    queries = (joined[:, :model_width] + q_bias).astype(jnp.bfloat16).reshape(head_shape)
    keys_own = joined[:, model_width : 2 * model_width].astype(jnp.bfloat16).reshape(head_shape)
    values_own = (joined[:, 2 * model_width :] + v_bias).astype(jnp.bfloat16).reshape(head_shape)

    def block_scores(key_block, owner_index):
        scores = (
            jnp.einsum("cqhd,ckhd->chqk", queries, key_block, preferred_element_type=jnp.float32)
            * score_scale
        )
        key_valid = (owner_index * local_genes + gene_index)[None, :] < lengths[:, None]
        return (scores, key_valid[:, None, None, :])

    def stats_turn(owner_index, carried, key_block):
        row_top, row_total = carried
        scores, is_valid = block_scores(key_block, owner_index)
        new_top = jnp.maximum(row_top, jnp.max(jnp.where(is_valid, scores, far_below), axis=-1))
        raised = jnp.where(is_valid, jnp.exp(scores - new_top[..., None]), 0.0)
        return (new_top, row_total * jnp.exp(row_top - new_top) + jnp.sum(raised, axis=-1))

    first_stats = stats_turn(
        cycle_place,
        (jnp.full(stat_shape, far_below, jnp.float32), jnp.zeros(stat_shape, jnp.float32)),
        keys_own,
    )

    def stats_step(step_index, carried):
        stats_now, key_block = carried
        key_block = passed_along(key_block, "blk", 1)
        return (
            stats_turn((cycle_place - step_index) % cycle_size, stats_now, key_block),
            key_block,
        )

    final_stats = lax.fori_loop(1, cycle_size, stats_step, (first_stats, keys_own))[0]
    log_total = final_stats[0] + jnp.log(final_stats[1])

    def block_weights(key_block, owner_index):
        scores, is_valid = block_scores(key_block, owner_index)
        return jnp.where(is_valid, jnp.exp(scores - log_total[..., None]), 0.0)

    def mix_turn(owner_index, mixed_sum, key_block, value_block):
        weights = block_weights(key_block, owner_index).astype(jnp.bfloat16)
        return mixed_sum + jnp.einsum(
            "chqk,ckhd->cqhd", weights, value_block, preferred_element_type=jnp.float32
        )

    mixed_start = mix_turn(cycle_place, jnp.zeros(head_shape, jnp.float32), keys_own, values_own)

    def pair_step(step_index, carried):
        inner, key_block, value_block = carried
        key_block, value_block = passed_along((key_block, value_block), "blk", 1)
        return (
            mix_turn((cycle_place - step_index) % cycle_size, inner, key_block, value_block),
            key_block,
            value_block,
        )

    mixed_sum = lax.fori_loop(1, cycle_size, pair_step, (mixed_start, keys_own, values_own))[0]
    mixed_low = (
        jnp.where(query_valid[:, :, None, None], mixed_sum, 0.0)
        .astype(jnp.bfloat16)
        .reshape(row_count, model_width)
    )
    part_cols = mixed_low
    branch = jnp.dot(
        part_cols,
        lax.all_gather(w_out, "cell", axis=0, tiled=True),
        preferred_element_type=jnp.float32,
    )
    middle = inputs + branch + out_bias
    normed2, ln2_pull = jax.vjp(layer_norm, middle, ln2_gain, ln2_bias)
    normed2_low = normed2.astype(jnp.bfloat16)
    gelu_exact = partial(jax.nn.gelu, approximate=False)
    ff_total = up_bias.shape[0]
    out_sum = jnp.zeros((row_count, model_width), jnp.float32)
    ffn_hidden = jnp.zeros((row_count, ff_total), jnp.bfloat16)
    up_piece = lax.all_gather(w_up, "cell", axis=0, tiled=True)
    down_piece = lax.all_gather(w_down, "cell", axis=0, tiled=True)
    pre_gelu = lax.dot_general(
        normed2_low, up_piece, col_contract, preferred_element_type=jnp.float32
    )
    pre_gelu = pre_gelu + up_bias
    activation, gelu_pull = jax.vjp(gelu_exact, pre_gelu)
    active_low = activation.astype(jnp.bfloat16)
    out_sum = out_sum + jnp.dot(active_low, down_piece, preferred_element_type=jnp.float32)
    grad_active = lax.dot_general(
        cot_rows, down_piece, col_contract, preferred_element_type=jnp.float32
    )
    pre_low = gelu_pull(grad_active)[0].astype(jnp.bfloat16)
    back_sum = jnp.dot(pre_low, up_piece, preferred_element_type=jnp.float32)
    ffn_hidden = lax.dynamic_update_slice_in_dim(ffn_hidden, active_low, jnp.int32(0), 1)
    out_sum, back_sum, pre_grads, hidden = (out_sum, back_sum, pre_low, ffn_hidden)
    out_hidden = (middle + out_sum + down_bias).astype(jnp.bfloat16).reshape(hidden_in.shape)
    grad_ln2, ln2_gain_part, ln2_bias_part = ln2_pull(back_sum)
    grad_middle = cot_rows.astype(jnp.float32) + grad_ln2
    branch_grad = grad_middle.astype(jnp.bfloat16)
    grad_mixed = lax.dot_general(
        branch_grad,
        lax.all_gather(w_out, "cell", axis=0, tiled=True),
        col_contract,
        preferred_element_type=jnp.float32,
    )
    grad_out = jnp.where(
        query_valid[:, :, None, None], grad_mixed.astype(jnp.bfloat16).reshape(head_shape), 0.0
    )
    delta = jnp.einsum("cqhd,cqhd->chq", grad_out.astype(jnp.float32), mixed_sum)

    def grad_step(step_index, carried):
        query_grad, key_block, value_block, key_grad, value_grad = carried
        owner_index = (cycle_place - step_index) % cycle_size
        weights = block_weights(key_block, owner_index)
        grad_weights = jnp.einsum(
            "cqhd,ckhd->chqk", grad_out, value_block, preferred_element_type=jnp.float32
        )
        score_grad = (weights * (grad_weights - delta[..., None])).astype(jnp.bfloat16)
        query_grad = (
            query_grad
            + jnp.einsum(
                "chqk,ckhd->cqhd", score_grad, key_block, preferred_element_type=jnp.float32
            )
            * score_scale
        )
        key_grad = (
            key_grad
            + jnp.einsum("chqk,cqhd->ckhd", score_grad, queries, preferred_element_type=jnp.float32)
            * score_scale
        )
        value_grad = value_grad + jnp.einsum(
            "chqk,cqhd->ckhd",
            weights.astype(jnp.bfloat16),
            grad_out,
            preferred_element_type=jnp.float32,
        )
        key_block, value_block, key_grad, value_grad = (
            passed_along(key_block, "blk", 1),
            passed_along(value_block, "blk", 1),
            passed_along(key_grad.astype(jnp.bfloat16), "blk", 1).astype(key_grad.dtype),
            passed_along(value_grad.astype(jnp.bfloat16), "blk", 1).astype(value_grad.dtype),
        )
        return (query_grad, key_block, value_block, key_grad, value_grad)

    zero_heads = jnp.zeros(head_shape, jnp.float32)
    cycle_done = lax.fori_loop(
        0, cycle_size, grad_step, (zero_heads, keys_own, values_own, zero_heads, zero_heads)
    )
    query_low = cycle_done[0].astype(jnp.bfloat16).reshape(row_count, model_width)
    key_low = cycle_done[3].astype(jnp.bfloat16).reshape(row_count, model_width)
    value_low = cycle_done[4].astype(jnp.bfloat16).reshape(row_count, model_width)
    grad_joined = jnp.concatenate([query_low, key_low, value_low], axis=1)
    grad_normed = lax.dot_general(
        grad_joined,
        lax.all_gather(w_qkv, "cell", axis=0, tiled=True),
        col_contract,
        preferred_element_type=jnp.float32,
    )
    grad_ln1, ln1_gain_part, ln1_bias_part = ln1_pull(grad_normed)
    in_grad = (grad_middle + grad_ln1).reshape(hidden_in.shape)
    qkv_term = lax.dot_general(
        normed_low, grad_joined, row_contract, preferred_element_type=jnp.float32
    )
    out_term = lax.dot_general(
        mixed_low, branch_grad, row_contract, preferred_element_type=jnp.float32
    )
    up_term = lax.dot_general(
        pre_grads, normed2_low, row_contract, preferred_element_type=jnp.float32
    )
    down_term = lax.dot_general(hidden, cot_rows, row_contract, preferred_element_type=jnp.float32)
    ffn_term = jnp.concatenate([up_term, down_term], axis=1).reshape(
        lax.axis_size("cell") * (model_width // lax.axis_size("cell")), ratio_ff * 2 * model_width
    )
    summed = lax.psum_scatter(
        jnp.concatenate([qkv_term, out_term, ffn_term], axis=1).astype(jnp.bfloat16),
        "cell",
        scatter_dimension=0,
        tiled=True,
    ).astype(jnp.float32)
    summed = lax.psum(summed.astype(jnp.bfloat16), "blk").astype(jnp.float32)
    own_rows = summed.shape[0]
    w_qkv_grad = summed[:, : 3 * model_width]
    w_out_grad = summed[:, 3 * model_width : 4 * model_width]
    ffn_grads = summed[:, 4 * model_width :].reshape(own_rows * ratio_ff, 2 * model_width)
    w_up_grad = ffn_grads[:, :model_width]
    w_down_grad = ffn_grads[:, model_width:]
    vectors = lax.psum(
        (
            ln1_gain_part,
            ln1_bias_part,
            jnp.sum(query_low, axis=0, dtype=jnp.float32),
            jnp.sum(value_low, axis=0, dtype=jnp.float32),
            jnp.sum(branch_grad, axis=0, dtype=jnp.float32),
            ln2_gain_part,
            ln2_bias_part,
            jnp.sum(pre_grads, axis=0, dtype=jnp.float32),
            jnp.sum(cot_rows, axis=0, dtype=jnp.float32),
        ),
        ("cell", "blk"),
    )
    return (
        out_hidden,
        in_grad,
        vectors[0],
        vectors[1],
        w_qkv_grad,
        vectors[2],
        vectors[3],
        w_out_grad,
        vectors[4],
        vectors[5],
        vectors[6],
        w_up_grad,
        vectors[7],
        w_down_grad,
        vectors[8],
    )


bf16 = jnp.bfloat16
f32 = jnp.float32
NN = (((1,), (0,)), ((), ()))
NT = (((1,), (1,)), ((), ()))
TN = (((0,), (0,)), ((), ()))
AXES = ("cell", "blk")
VMEM_LIMIT = 60 * 2**20
ROWS = 256
COST_PART = 50
OFFSETS = (0, -1, -2, -3, -4, 1, 2, 3)


def swappable(mesh):
    return dict(mesh.shape) == {"cell": 16, "blk": 2}


def dot(a, b, dims):
    return lax.dot_general(a, b, dims, preferred_element_type=f32)


def params():
    return pltpu.CompilerParams(vmem_limit_bytes=VMEM_LIMIT)


def cost(flops, nbytes, trans=0):
    return pl.CostEstimate(
        flops=int(flops) // COST_PART,
        bytes_accessed=int(nbytes) // COST_PART,
        transcendentals=int(trans) // COST_PART,
    )


def shape(dims, dtype):
    return jax.ShapeDtypeStruct(dims, dtype)


ANY = pl.BlockSpec(memory_space=pl.ANY)


def fixed(dims):
    return pl.BlockSpec(dims, lambda *_: (0,) * len(dims))


def rowed(rows, width):
    return pl.BlockSpec((rows, width), lambda i, *_: (i, 0))


class Ring:
    def __init__(self, sizes):
        self.cells, self.blks = sizes["cell"], sizes["blk"]
        self.chips = self.cells // 2
        depth = self.chips // 2
        self.order = [2 * z for z in range(depth)] + [2 * z + 1 for z in reversed(range(depth))]
        self.place = [self.order.index(c) for c in range(self.chips)]

    def permute(self, x, target):
        pairs = []
        for cell in range(self.cells):
            for blk in range(self.blks):
                to_cell, to_blk = target(cell, blk)
                pairs.append((cell * self.blks + blk, to_cell * self.blks + to_blk))
        return lax.ppermute(x, AXES, pairs)

    def shift(self, x, by):
        def target(cell, blk):
            chip, core = cell // 2, cell % 2
            way = 1 - 2 * ((core + blk) % 2)
            return self.order[(self.place[chip] + way * by) % self.chips] * 2 + core, blk

        return self.permute(x, target)

    def swap_core(self, x):
        return self.permute(x, lambda cell, blk: (cell ^ 1, blk))

    def swap_blk(self, x):
        return self.permute(x, lambda cell, blk: (cell, 1 - blk))

    def chips_of_slots(self, core):
        chip = lax.axis_index("cell") // 2
        way = 1 - 2 * ((core + lax.axis_index("blk")) % 2)
        place = jnp.array(self.place, jnp.int32)[chip]
        return jnp.array(self.order, jnp.int32)[
            (place + way * jnp.array(OFFSETS, jnp.int32)) % self.chips
        ]

    def gather(self, x, back):
        slots = [x] + [None] * 7
        for k in range(1, 5):
            slots[k] = self.shift(slots[k - 1], 1)
            if k <= back:
                slots[4 + k] = self.shift(slots[3 + k] if k > 1 else slots[0], -1)
            if k > back + 1:
                slots[3 + k] = self.swap_blk(slots[k - 1])
            slots = yield slots

    def reduce(self, parts, back, alone=False):
        def added(terms):
            total = terms[0].astype(f32)
            for t in terms[1:]:
                total = total + t.astype(f32)
            return total.astype(bf16)

        way = {"ahead": self.shift(added(parts[4]), -1)}
        if back:
            way["behind"] = self.shift(added(parts[4 + back]), 1)
        for k in range(3, back, -1):
            way[f"over{k}"] = self.swap_blk(added(parts[4 + k]))
        way = yield way
        for k in (3, 2, 1):
            extra = [way.pop(f"over{k}")] if f"over{k}" in way else []
            way["ahead"] = self.shift(added([way["ahead"]] + parts[k] + extra), -1)
            if k < back and not (alone and k == 1):
                way["behind"] = self.shift(added([way["behind"]] + parts[4 + k]), 1)
            way = yield way
        if alone:
            way["behind"] = self.shift(added([way["behind"]] + parts[5]), 1)
            way = yield way
        ends = [way["ahead"]] + ([way["behind"]] if back else [])
        yield added(ends + parts[0])

    def total(self, x):
        count = self.cells * self.blks
        bits = [1 << i for i in range(count.bit_length() - 1)]
        for bit in [b for b in bits if b >= self.blks] + [b for b in bits if b < self.blks]:
            other = bit
            moved = self.permute(
                x, lambda cell, blk: divmod((cell * self.blks + blk) ^ other, self.blks)
            )
            x, moved = yield x, moved
            x = x + moved
        yield x


def norm_parts(x):
    mean = jnp.mean(x, axis=-1, keepdims=True)
    centered = x - mean
    var = jnp.mean(centered * centered, axis=-1, keepdims=True)
    scale = lax.rsqrt(var + epsilon)
    return centered * scale, scale


def norm_back(xh, scale, gain, grad):
    e = grad * gain
    return scale * (
        e - jnp.mean(e, axis=-1, keepdims=True) - xh * jnp.mean(e * xh, axis=-1, keepdims=True)
    )


def colsum(x):
    return jnp.sum(x, axis=0, keepdims=True)


def place_rows(slots, target, place_ref, sem, first=0, cols=None):
    height = slots[0].shape[0]
    start, wide = cols or (0, slots[0].shape[1])
    return [
        pltpu.make_async_copy(
            slot.at[:, pl.ds(start, wide)],
            target.at[
                pl.ds(pl.multiple_of(place_ref[i] * height, 16), height),
                pl.ds(first + start, wide),
            ],
            sem.at[i],
        )
        for i, slot in enumerate(slots)
    ]


def qkv_kernel(n, place_ref, x_ref, gain_ref, bias_ref, qb_ref, vb_ref, *refs):
    slots, (a_ref, q_ref, k_ref, v_ref, w, sem) = refs[:n], refs[n:]
    width = x_ref.shape[1]
    first = pl.program_id(0) == 0
    copies = [
        place_rows(slots, w, place_ref, sem.at[j], cols=(j * width, width)) for j in range(3)
    ]

    @pl.when(first)
    def _():
        for group in copies:
            for c in group:
                c.start()

    xh, _ = norm_parts(x_ref[...].astype(f32))
    a_ref[...] = (xh * gain_ref[...] + bias_ref[...]).astype(bf16)
    for j, (res_ref, add_ref) in enumerate(((q_ref, qb_ref), (k_ref, None), (v_ref, vb_ref))):

        @pl.when(first)
        def _(group=copies[j]):
            for c in group:
                c.wait()

        res = dot(a_ref[...], w[:, j * width : (j + 1) * width], NN)
        if add_ref is not None:
            res = res + add_ref[...]
        res_ref[...] = res.astype(bf16)


def qkv_call(place, x, gain, bias, qb, vb, slots):
    rows, width = x.shape
    n = len(slots)
    block = rowed(ROWS, width)
    vec = fixed((1, width))
    return pl.pallas_call(
        partial(qkv_kernel, n),
        grid_spec=pltpu.PrefetchScalarGridSpec(
            num_scalar_prefetch=1,
            grid=(rows // ROWS,),
            in_specs=[block, vec, vec, vec, vec] + [ANY] * n,
            out_specs=[block] * 4,
            scratch_shapes=[
                pltpu.VMEM((width, 3 * width), bf16),
                pltpu.SemaphoreType.DMA((3, n)),
            ],
        ),
        out_shape=[shape((rows, width), bf16)] * 4,
        compiler_params=params(),
        cost_estimate=cost(6 * rows * width * width, 2 * width * (5 * rows + 3 * width)),
        name="qkv",
    )(place, x, gain, bias, qb, vb, *slots)


def head_keys(low, k, v, mask, fill):
    res = []
    for half in range(2):
        mine = low if half == 0 else jnp.logical_not(low)
        res.append(
            (
                jnp.where(mine, k.astype(f32), mask).astype(bf16),
                jnp.where(mine, v.astype(f32), fill).astype(bf16),
            )
        )
    return res


def head_query(low, lane, half, q):
    mine = low if half == 0 else jnp.logical_not(low)
    one = lane == (HEAD_DIM if half == 0 else 0)
    q = q.astype(f32) * (1.0 / math.sqrt(HEAD_DIM))
    return jnp.where(mine, q, jnp.where(one, 1.0, 0.0)).astype(bf16)


def attend_kernel(qrows, ahead, mask_ref, keep_ref, q_ref, k_ref, v_ref, o_ref, lse_ref):
    n = q_ref.shape[0]
    lane = lax.broadcasted_iota(jnp.int32, (n, 128), 1)
    pair = head_keys(lane < HEAD_DIM, k_ref[...], v_ref[...], mask_ref[...], 1.0)
    lane = lane[:qrows]
    low = lane < HEAD_DIM
    items = [(i, half) for i in range(n // qrows) for half in range(2)]

    def scores(i, half):
        q = head_query(low, lane, half, q_ref[pl.ds(i * qrows, qrows), :])
        return dot(q, pair[half][0], NT)

    waiting = [scores(*item) for item in items[:ahead]]
    for at, (i, half) in enumerate(items):
        if at + ahead < len(items):
            waiting.append(scores(*items[at + ahead]))
        s = waiting.pop(0)
        rows = pl.ds(i * qrows, qrows)
        top = jnp.max(s, axis=1, keepdims=True)
        mixed = dot(jnp.exp(s - top).astype(bf16), pair[half][1], NN)
        total = pltpu.roll(mixed, HEAD_DIM, 1)
        o, lse = mixed / total, top + jnp.log(total)
        if half == 0:
            o_first, lse_first = o, lse
            continue
        o_ref[rows, :] = (jnp.where(low, o_first, o) * keep_ref[rows, :]).astype(bf16)
        lse = jnp.transpose(jnp.where(low, lse_first, lse))
        lse_ref[0, :, rows] = lse[:1, :]
        lse_ref[1, :, rows] = lse[HEAD_DIM : HEAD_DIM + 1, :]


def attend_call(mask, keep, qkv, first, count, qrows=256, ahead=2):
    n = qkv[0].shape[0]
    block = pl.BlockSpec((n, 128), lambda h: (0, h + first))
    return pl.pallas_call(
        partial(attend_kernel, qrows, ahead),
        grid=(count,),
        in_specs=[fixed((n, 1)), fixed((n, 1)), block, block, block],
        out_specs=[
            pl.BlockSpec((n, 128), lambda h: (0, h)),
            pl.BlockSpec((2, 1, n), lambda h: (h, 0, 0)),
        ],
        out_shape=[shape((n, 128 * count), bf16), shape((2 * count, 1, n), f32)],
        compiler_params=params(),
        cost_estimate=cost(20 * count * n * n * 128, 8 * n * 128 * count, 2 * count * n * n),
        name="attend",
    )(mask, keep, *qkv)


def attend_back_kernel(
    qrows, mask_ref, q_ref, k_ref, v_ref, o_ref, go_ref, lse_ref,
    gq_ref, gk_ref, gv_ref, sq_ref, sv_ref, gk_sum, gv_sum,
):
    n = q_ref.shape[0]
    lane = lax.broadcasted_iota(jnp.int32, (n, 128), 1)
    k = k_ref[...]
    scale = 1.0 / math.sqrt(HEAD_DIM)
    pair = head_keys(lane < HEAD_DIM, k, v_ref[...], mask_ref[...], 0.0)
    k_turned = jnp.transpose(k)
    prod = jnp.transpose(o_ref[...].astype(f32) * go_ref[...].astype(f32))
    delta = [colsum(prod[half * HEAD_DIM : (half + 1) * HEAD_DIM, :]) for half in range(2)]
    top = lane[:qrows]
    for i in range(n // qrows):
        rows = pl.ds(i * qrows, qrows)
        gq = []
        for half in range(2):
            q_raw, go = q_ref[rows, :], go_ref[rows, :]
            q = head_query(top < HEAD_DIM, top, half, q_raw)
            p = jnp.exp(dot(pair[half][0], q, NT) - lse_ref[half, :, rows])
            gp = dot(pair[half][1], go, NT)
            gs = (p * (gp - delta[half][:, i * qrows : (i + 1) * qrows])).astype(bf16)
            gv = dot(p.astype(bf16), go, NN)
            gk = dot(gs, q_raw, NN)
            if i == 0:
                gv_sum[half], gk_sum[half] = gv, gk
            else:
                gv_sum[half] += gv
                gk_sum[half] += gk
            gq.append(dot(k_turned, gs, NN))
        turned = jnp.concatenate([gq[0][:HEAD_DIM], gq[1][HEAD_DIM:]], axis=0)
        gq_ref[rows, :] = jnp.transpose(turned * scale).astype(bf16)
    low = lane < HEAD_DIM
    gk_ref[...] = (jnp.where(low, gk_sum[0], gk_sum[1]) * scale).astype(bf16)
    gv = jnp.where(low, gv_sum[0], gv_sum[1]).astype(bf16)
    gv_ref[...] = gv
    sq_ref[...] = colsum(gq_ref[...].astype(f32))
    sv_ref[...] = colsum(gv.astype(f32))


def attend_back_call(mask, qkv, o, go, lse, count, firsts, qrows=512):
    n = go.shape[0]

    def block(first):
        return pl.BlockSpec((n, 128), lambda h: (0, h + first))

    own, vec = block(0), pl.BlockSpec((1, 128), lambda h: (0, h))
    at_qkv, at_o, at_go = firsts
    return pl.pallas_call(
        partial(attend_back_kernel, qrows),
        grid=(count,),
        in_specs=[fixed((n, 1))]
        + [block(at_qkv)] * 3
        + [block(at_o), block(at_go), pl.BlockSpec((2, 1, n), lambda h: (h + at_o, 0, 0))],
        out_specs=[own, own, own, vec, vec],
        out_shape=[shape((n, 128 * count), bf16)] * 3 + [shape((1, 128 * count), f32)] * 2,
        scratch_shapes=[pltpu.VMEM((2, n, 128), f32)] * 2,
        compiler_params=params(),
        cost_estimate=cost(32 * count * n * n * 128, 16 * n * 128 * count, 2 * count * n * n),
        name="attend_back",
    )(mask, *qkv, o, go, lse)


def load_wout(slots, place_ref, w, sem):
    wide = w.shape[1]
    start = slots[0].shape[1] - wide
    copies = place_rows(slots, w, place_ref, sem, -start, (start, wide))

    @pl.when(pl.program_id(0) == 0)
    def _():
        for c in copies:
            c.start()
        for c in copies:
            c.wait()


def out_kernel(n, place_ref, x_ref, bias_ref, gain_ref, shift_ref, *refs):
    slots, o_refs, (m_ref, b_ref, w, sem) = refs[:n], refs[n:-4], refs[-4:]
    load_wout(slots, place_ref, w, sem)
    m = x_ref[...].astype(f32) + bias_ref[...]
    first = 0
    for o_ref in o_refs:
        m = m + dot(o_ref[...], w[first : first + o_ref.shape[1], :], NN)
        first += o_ref.shape[1]
    m_ref[...] = m
    xh, _ = norm_parts(m)
    b_ref[...] = (xh * gain_ref[...] + shift_ref[...]).astype(bf16)


def out_call(place, x, o_parts, slots, bias, gain, shift):
    rows, width = x.shape
    n = len(slots)
    vec = fixed((1, width))
    block = rowed(ROWS, width)
    return pl.pallas_call(
        partial(out_kernel, n),
        grid_spec=pltpu.PrefetchScalarGridSpec(
            num_scalar_prefetch=1,
            grid=(rows // ROWS,),
            in_specs=[block, vec, vec, vec]
            + [ANY] * n
            + [rowed(ROWS, o.shape[1]) for o in o_parts],
            out_specs=[block, block],
            scratch_shapes=[pltpu.VMEM((width, width), bf16), pltpu.SemaphoreType.DMA((n,))],
        ),
        out_shape=[shape((rows, width), f32), shape((rows, width), bf16)],
        compiler_params=params(),
        cost_estimate=cost(4 * rows * width * width, width * (10 * rows + 2 * width)),
        name="out",
    )(place, x, bias, gain, shift, *slots, *o_parts)


def gelu_both(z, gh):
    t = 1.0 / (1.0 + jnp.abs(z) * (0.3275911 / math.sqrt(2.0)))
    e = jnp.exp(z * z * -0.5)
    half = (0.254829592, -0.284496736, 1.421413741, -1.453152027, 1.061405429)
    tail = half[4] * 0.5
    for c in half[3::-1]:
        tail = tail * t + 0.5 * c
    tail = tail * t * e
    phi = jnp.where(z > 0, 1.0 - tail, tail)
    return z * phi, gh * (phi + z * e * (1.0 / math.sqrt(2.0 * math.pi)))


def ffn_kernel(n, later, *refs):
    b_own, b_sib, g_own, g_sib, ub_ref = refs[:5]
    slots = refs[5 : 5 + n]
    refs = refs[5 + n :]
    if later:
        acc_o, acc_g = refs[:2]
        refs = refs[2:]
        h_ref, gz_ref, sum_ref, oo_ref, go_ref, os_ref, gs_ref, us, ds, sem = refs
    else:
        h_ref, gz_ref, sum_ref, oo_ref, go_ref, us, ds, sem = refs
    units = us.shape[0] // n
    i = pl.program_id(0)
    near = i < pl.num_programs(0) // 2
    copies = []
    for s, slot in enumerate(slots):
        rows = pl.ds(s * units, units)
        copies.append(
            pltpu.make_async_copy(slot.at[pl.ds(0, units), :], us.at[rows, :], sem.at[0, s])
        )
        copies.append(
            pltpu.make_async_copy(slot.at[pl.ds(units, units), :], ds.at[rows, :], sem.at[1, s])
        )

    @pl.when(i == 0)
    def _():
        for c in copies:
            c.start()
        for c in copies:
            c.wait()
        sum_ref[...] = jnp.zeros_like(sum_ref)

    b = jnp.where(near, b_own[...], b_sib[...])
    g = jnp.where(near, g_own[...], g_sib[...])
    h, gz = gelu_both(dot(b, us[...], NT) + ub_ref[...], dot(g, ds[...], NT))
    h, gz = h.astype(bf16), gz.astype(bf16)
    h_ref[...] = h
    gz_ref[...] = gz
    sum_ref[...] += colsum(gz.astype(f32))
    out = dot(h, ds[...], NN)
    back = dot(gz, us[...], NN)
    if not later:
        oo_ref[...] = out
        go_ref[...] = back
        return
    out = out + acc_o[...]
    back = back + acc_g[...]

    @pl.when(near)
    def _():
        oo_ref[...] = out.astype(bf16)
        go_ref[...] = back.astype(bf16)

    @pl.when(jnp.logical_not(near))
    def _():
        os_ref[...] = out.astype(bf16)
        gs_ref[...] = back.astype(bf16)


def ffn_call(b_own, b_sib, g_own, g_sib, ub, slots, acc=None):
    rows, width = b_own.shape
    half = rows // ROWS
    n = len(slots)
    units = ub.shape[1]
    later = acc is not None
    near = pl.BlockSpec((ROWS, width), lambda i: (jnp.minimum(i, half - 1), 0))
    far = pl.BlockSpec((ROWS, width), lambda i: (jnp.maximum(i - half, 0), 0))
    both = rowed(ROWS, width)
    acc = list(acc or ())
    out_specs = [rowed(ROWS, units), rowed(ROWS, units), fixed((1, units))]
    out_shape = [shape((2 * rows, units), bf16)] * 2 + [shape((1, units), f32)]
    if later:
        out_specs += [near, near, far, far]
        out_shape += [shape((rows, width), bf16)] * 4
    else:
        out_specs += [both, both]
        out_shape += [shape((2 * rows, width), f32)] * 2
    return pl.pallas_call(
        partial(ffn_kernel, n, later),
        grid=(2 * half,),
        in_specs=[near, far, near, far, fixed((1, units))] + [ANY] * n + [both] * len(acc),
        out_specs=out_specs,
        out_shape=out_shape,
        scratch_shapes=[
            pltpu.VMEM((units, width), bf16),
            pltpu.VMEM((units, width), bf16),
            pltpu.SemaphoreType.DMA((2, n)),
        ],
        compiler_params=params(),
        cost_estimate=cost(
            24 * rows * width * units, rows * width * (24 + 16 * later), 4 * rows * units
        ),
        name="ffn",
    )(b_own, b_sib, g_own, g_sib, ub, *slots, *acc)


def ffn_weights_kernel(n, gz, h, b_own, b_sib, g_own, g_sib, *refs):
    outs = refs[:n]
    lv, rv, ov, lsem, rsem, osem = refs[n:]
    rows = b_own.shape[0]
    units = outs[0].shape[0] // 2
    loads = []
    for which, (left, parts) in enumerate(((gz, (b_own, b_sib)), (h, (g_own, g_sib)))):
        loads.append(pltpu.make_async_copy(left, lv.at[which], lsem.at[which]))
        for j, part in enumerate(parts):
            loads.append(
                pltpu.make_async_copy(
                    part, rv.at[which, pl.ds(j * rows, rows), :], rsem.at[which, j]
                )
            )
    for c in loads:
        c.start()
    stores = []
    step = 0
    for which in range(2):
        for c in loads[3 * which : 3 * which + 3]:
            c.wait()
        for pair in range(n // 2):
            slot = step % 2
            if step >= 2:
                for c in stores[2 * (step - 2) : 2 * (step - 2) + 2]:
                    c.wait()
            cols = pl.ds(pair * 2 * units, 2 * units)
            ov[slot] = dot(lv[which, :, cols], rv[which], TN).astype(bf16)
            for j in range(2):
                c = pltpu.make_async_copy(
                    ov.at[slot, pl.ds(j * units, units), :],
                    outs[2 * pair + j].at[pl.ds(which * units, units), :],
                    osem.at[slot, j],
                )
                c.start()
                stores.append(c)
            step += 1
    for c in stores[2 * (step - 2) :]:
        c.wait()


def ffn_weights_call(gz, h, b_own, b_sib, g_own, g_sib, n):
    rows, units = gz.shape
    width = b_own.shape[1]
    return pl.pallas_call(
        partial(ffn_weights_kernel, n),
        in_specs=[ANY] * 6,
        out_specs=[ANY] * n,
        out_shape=[shape((2 * units // n, width), bf16)] * n,
        scratch_shapes=[
            pltpu.VMEM((2, rows, units), bf16),
            pltpu.VMEM((2, rows, width), bf16),
            pltpu.VMEM((2, 2 * units // n, width), bf16),
            pltpu.SemaphoreType.DMA((2,)),
            pltpu.SemaphoreType.DMA((2, 2)),
            pltpu.SemaphoreType.DMA((2, 2)),
        ],
        compiler_params=params(),
        cost_estimate=cost(6 * rows * units * width, 4 * rows * (units + width)),
        name="ffn_weights",
    )(gz, h, b_own, b_sib, g_own, g_sib)


def mid_kernel(
    n, place_ref, oo_ref, os_ref, go_ref, gs_ref, m_ref, g_ref, keep_ref, db_ref, gain_ref, *refs
):
    slots, (hid_ref, gr_ref, gatt_ref, sums_ref, w, sem) = refs[:n], refs[n:]
    load_wout(slots, place_ref, w, sem)

    @pl.when(pl.program_id(0) == 0)
    def _():
        sums_ref[...] = jnp.zeros_like(sums_ref)

    m = m_ref[...]
    g = g_ref[...].astype(f32)
    ff = oo_ref[...].astype(f32) + os_ref[...].astype(f32)
    hid_ref[...] = (m + ff + db_ref[...]).astype(bf16)
    gb = go_ref[...].astype(f32) + gs_ref[...].astype(f32)
    xh, scale = norm_parts(m)
    gm = g + norm_back(xh, scale, gain_ref[...], gb)
    gr = gm.astype(bf16)
    gr_ref[...] = gr
    gatt_ref[...] = (dot(gr, w[...], NT) * keep_ref[...]).astype(bf16)
    sums_ref[0:1, :] += colsum(gb * xh)
    sums_ref[1:2, :] += colsum(gb)
    sums_ref[2:3, :] += colsum(gr.astype(f32))
    sums_ref[3:4, :] += colsum(g)


def mid_call(place, oo, os, go, gs, m, g, keep, db, gain, slots):
    rows, width = m.shape
    n = len(slots)
    block = rowed(ROWS, width)
    vec = fixed((1, width))
    return pl.pallas_call(
        partial(mid_kernel, n),
        grid_spec=pltpu.PrefetchScalarGridSpec(
            num_scalar_prefetch=1,
            grid=(rows // ROWS,),
            in_specs=[block] * 6 + [rowed(ROWS, 1), vec, vec] + [ANY] * n,
            out_specs=[block] * 3 + [fixed((8, width))],
            scratch_shapes=[pltpu.VMEM((width, width), bf16), pltpu.SemaphoreType.DMA((n,))],
        ),
        out_shape=[shape((rows, width), bf16)] * 3 + [shape((8, width), f32)],
        compiler_params=params(),
        cost_estimate=cost(4 * rows * width * width, width * (30 * rows + 2 * width)),
        name="mid",
    )(place, oo, os, go, gs, m, g, keep, db, gain, *slots)


def att_weights_kernel(n, counts, blocks, place_ref, *refs):
    lefts, at = [], 0
    for count in counts[:-1]:
        lefts.append(refs[at : at + count])
        at += count
    rights, refs = refs[at : at + counts[-1]], refs[at + counts[-1] :]
    outs, (lv, tv, rv, ov, lsem, rsem, osem) = refs[: n + 1], refs[n + 1 :]
    height = outs[0].shape[0]
    loads = []
    for i, pieces in enumerate(lefts):
        loads.append([])
        at = 0
        for j, r in enumerate(pieces):
            wide = r.shape[1]
            loads[-1].append(
                pltpu.make_async_copy(r, lv.at[i, :, pl.ds(at, wide)], lsem.at[i, j])
            )
            at += wide
    ends, right_loads = [], []
    for i, r in enumerate(rights):
        start = ends[-1] if ends else 0
        ends.append(start + r.shape[1])
        right_loads.append(
            pltpu.make_async_copy(r, rv.at[:, pl.ds(start, r.shape[1])], rsem.at[i])
        )
    for c in loads[0] + right_loads + [c for group in loads[1:] for c in group]:
        c.start()
    have, arrived = set(), 0
    stores = []
    for step, (left, start, wide) in enumerate(blocks):
        if left not in have:
            for c in loads[left]:
                c.wait()
            tv[left] = jnp.transpose(lv[left])
            have.add(left)
        while arrived < len(ends) and (arrived == 0 or ends[arrived - 1] < start + wide):
            right_loads[arrived].wait()
            arrived += 1
        slot = step % 2
        if step >= 2:
            for c in stores[step - 2]:
                c.wait()
        cols = pl.ds(start, wide)
        ov[slot, :, pl.ds(0, wide)] = dot(tv[left], rv[:, cols], NN).astype(bf16)
        stores.append([])
        for i in range(2 * n):
            rows = pl.ds(pl.multiple_of(place_ref[i] * height, 16), height)
            goal = outs[i].at[:, cols] if i < n else outs[n].at[i - n, :, cols]
            c = pltpu.make_async_copy(ov.at[slot, rows, pl.ds(0, wide)], goal, osem.at[slot, i])
            c.start()
            stores[-1].append(c)
    for group in stores[-2:]:
        for c in group:
            c.wait()


def att_weights_call(place, lefts, rights, blocks):
    rows, width = lefts[0][0].shape[0], sum(l.shape[1] for l in lefts[0])
    n = len(OFFSETS)
    total = sum(r.shape[1] for r in rights)
    wide = max(b[2] for b in blocks)
    height = width // (2 * n)
    return pl.pallas_call(
        partial(att_weights_kernel, n, [len(l) for l in lefts] + [len(rights)], blocks),
        grid_spec=pltpu.PrefetchScalarGridSpec(
            num_scalar_prefetch=1,
            grid=(1,),
            in_specs=[ANY] * (sum(len(l) for l in lefts) + len(rights)),
            out_specs=[ANY] * (n + 1),
            scratch_shapes=[
                pltpu.VMEM((len(lefts), rows, width), bf16),
                pltpu.VMEM((len(lefts), width, rows), bf16),
                pltpu.VMEM((rows, total), bf16),
                pltpu.VMEM((2, width, wide), bf16),
                pltpu.SemaphoreType.DMA((len(lefts), max(len(l) for l in lefts))),
                pltpu.SemaphoreType.DMA((len(rights),)),
                pltpu.SemaphoreType.DMA((2, 2 * n)),
            ],
        ),
        out_shape=[shape((height, total), bf16)] * n + [shape((n, height, total), bf16)],
        compiler_params=params(),
        cost_estimate=cost(3 * rows * width * total, 2 * (rows + width) * total),
        name="att_weights",
    )(place, *[a for l in lefts for a in l], *rights)


def in_kernel(n, pieces, place_ref, x_ref, gr_ref, gain_ref, *refs):
    grads, slots = refs[:pieces], refs[pieces : pieces + n]
    res_ref, sums_ref, w, sem = refs[pieces + n :]
    copies = place_rows(slots, w, place_ref, sem, cols=(0, w.shape[1]))

    @pl.when(pl.program_id(0) == 0)
    def _():
        for c in copies:
            c.start()
        for c in copies:
            c.wait()
        sums_ref[...] = jnp.zeros_like(sums_ref)

    ga = None
    col = 0
    for r in grads:
        part = dot(r[...], w[:, col : col + r.shape[1]], NT)
        ga = part if ga is None else ga + part
        col += r.shape[1]
    xh, scale = norm_parts(x_ref[...].astype(f32))
    res = gr_ref[...].astype(f32) + norm_back(xh, scale, gain_ref[...], ga)
    sums_ref[0:1, :] += colsum(ga * xh)
    sums_ref[1:2, :] += colsum(ga)
    res_ref[...] = res.astype(res_ref.dtype)


def in_call(place, x, gr, gain, grads, slots, part, dtype):
    rows, width = x.shape
    n = len(slots)
    half = rows // ROWS // 2

    def piece(w):
        return pl.BlockSpec((ROWS, w), lambda i, *_: (i + part * half, 0))

    return pl.pallas_call(
        partial(in_kernel, n, len(grads)),
        grid_spec=pltpu.PrefetchScalarGridSpec(
            num_scalar_prefetch=1,
            grid=(half,),
            in_specs=[piece(width), piece(width), fixed((1, width))]
            + [piece(g.shape[1]) for g in grads]
            + [ANY] * n,
            out_specs=[rowed(ROWS, width), fixed((8, width))],
            scratch_shapes=[
                pltpu.VMEM((width, 3 * width), bf16),
                pltpu.SemaphoreType.DMA((n,)),
            ],
        ),
        out_shape=[shape((rows // 2, width), dtype), shape((8, width), f32)],
        compiler_params=params(),
        cost_estimate=cost(4 * rows * width * width, width * (7 * rows + 6 * width)),
        name="in",
    )(place, x, gr, gain, *grads, *slots)


def fence(*trees):
    return lax.optimization_barrier(trees)


def side_by_side(vectors):
    total = sum(v.shape[0] for v in vectors)
    res, at = None, 0
    for v in vectors:
        wide = jnp.pad(v, (at, total - at - v.shape[0]))
        at += v.shape[0]
        res = wide if res is None else res + wide
    return res


def local_swapped(
    sizes, hidden_in, lengths, ln1_gain, ln1_bias, w_qkv, q_bias, v_bias, w_out, out_bias, ln2_gain, ln2_bias,
    w_up, up_bias, w_down, down_bias, cotangent,
):
    ring = Ring(sizes)
    blk = lax.axis_index("blk")
    core = lax.axis_index("cell") % 2
    genes, width = hidden_in.shape[1:]
    units = w_up.shape[0]
    shards = ring.cells
    n = len(OFFSETS)

    def vec(v):
        return v.reshape(1, -1)

    def pick(x, which):
        return lax.dynamic_index_in_dim(x, which, 0, keepdims=False)

    chips_own, chips_sib = ring.chips_of_slots(core), ring.chips_of_slots(1 - core)
    shard_own = 2 * chips_own + core
    shard_sib = 2 * chips_sib + 1 - core
    place = jnp.concatenate([shard_own, shard_sib])
    index = jnp.arange(genes, dtype=jnp.int32)
    index = jnp.concatenate([blk * genes + index, (1 - blk) * genes + index])
    keep = (index < pick(lengths, blk)).astype(f32)[:, None]
    mask = jnp.where(keep > 0, 0.0, far_below)

    x_got = ring.swap_blk(pick(hidden_in, 1 - blk))
    steps = ring.gather(jnp.concatenate([w_qkv, w_out], axis=1), 2)
    slots, sib = next(steps), [None] * n
    w_pair = jnp.concatenate([w_up, w_down], axis=0)
    g_send = pick(cotangent, 1 - blk)
    small = [vec(v) for v in (ln1_gain, ln1_bias, q_bias, v_bias, out_bias, ln2_gain, ln2_bias)]
    small += [place, mask, keep]
    slots[1], slots[5] = fence(slots[1], slots[5])
    slots = steps.send(slots)
    slots[2], slots[6], small, x_got, w_pair = fence(slots[2], slots[6], small, x_got, w_pair)
    ln1_gain, ln1_bias, q_bias, v_bias, out_bias, ln2_gain, ln2_bias, place, mask, keep = small
    slots = steps.send(slots)
    for s in (0, 1, 5, 2, 6):
        sib[s] = ring.swap_core(slots[s])
    x = jnp.concatenate([pick(hidden_in, blk), x_got], axis=0)
    slots[3], x, sib, g_send = fence(slots[3], x, sib, g_send)
    slots = steps.send(slots)
    for s in (3, 4, 7):
        sib[s] = ring.swap_core(slots[s])
    slots[4], w_pair = fence(slots[4], w_pair)
    pair = [w_pair, ring.shift(w_pair, 1)] + [None] * 6
    g_send, slots[7] = fence(g_send, slots[7])
    g_send = [g_send[: genes // 2], g_send[genes // 2 :]]
    g_got = [ring.swap_blk(g_send[0])]

    weights = slots + sib
    a, *qkv = qkv_call(place, x, ln1_gain, ln1_bias, q_bias, v_bias, weights)
    qkv, pair[1], g_got, g_send = fence(qkv, pair[1], g_got, g_send)
    g_got.append(ring.swap_blk(g_send[1]))
    pair[2] = ring.shift(pair[1], 1)
    pairs = width // 128
    cut = 6 * pairs // 10
    attended = [attend_call(mask, keep, qkv, 0, cut)]
    attended, qkv, pair[2], g_got = fence(attended, qkv, pair[2], g_got)
    pair[3] = ring.shift(pair[2], 1)
    g = jnp.concatenate([pick(cotangent, blk)] + g_got, axis=0)
    g_sib = ring.swap_core(g)
    attended.append(attend_call(mask, keep, qkv, cut, pairs - cut))
    o_parts = [t[0] for t in attended]
    m, b = out_call(place, x, o_parts, weights, out_bias, ln2_gain, ln2_bias)
    b, g_sib, pair[0], pair[3] = fence(b, g_sib, pair[0], pair[3])
    b_sib = ring.swap_core(b)
    pair[4] = ring.shift(pair[3], 1)
    pair[5] = ring.shift(pair[0], -1)
    pair[7] = ring.swap_blk(pair[3])

    ub = up_bias.reshape(shards, units)[shard_own]
    near, far = (0, 1, 2, 3), (4, 5, 6, 7)
    ub_near, ub_far = [vec(jnp.concatenate([ub[s] for s in group])) for group in (near, far)]
    h_near, gz_near, sum_near, *acc = ffn_call(
        b, b_sib, g, g_sib, ub_near, [pair[s] for s in near]
    )
    h_near, gz_near, acc, pair[5] = fence(h_near, gz_near, acc, pair[5])
    pair[6] = ring.shift(pair[5], -1)
    parts = [None] * n
    made = ffn_weights_call(gz_near, h_near, b, b_sib, g, g_sib, len(near))
    made, acc = fence(made, acc)
    for s, t in zip(near, made, strict=True):
        parts[s] = [t]
    h_far, gz_far, sum_far, oo, gb_own, os_send, gs_send = ffn_call(
        b, b_sib, g, g_sib, ub_far, [pair[s] for s in far], acc
    )
    up_sums = dict(
        zip(near + far, jnp.split(sum_near[0], 4) + jnp.split(sum_far[0], 4), strict=True)
    )
    mine = shard_own[None, :] == jnp.arange(shards, dtype=jnp.int32)[:, None]
    up_rows = jnp.sum(
        jnp.where(mine[:, :, None], jnp.stack([up_sums[s] for s in range(n)])[None], 0.0), axis=1
    )
    made = ffn_weights_call(gz_far, h_far, b, b_sib, g, g_sib, len(far))
    os_got, gs_got = ring.swap_core(os_send), ring.swap_core(gs_send)
    made, oo, os_got, gs_got = fence(made, oo, os_got, gs_got)
    for s, t in zip(far, made, strict=True):
        parts[s] = [t]
    steps = ring.reduce(parts, 1)
    way = next(steps)
    out_hidden, gr, gatt, mid_sums = mid_call(
        place, oo, os_got, gb_own, gs_got, m, g, keep, vec(down_bias), ln2_gain, weights
    )
    hid_send = [out_hidden[genes : genes + genes // 2], out_hidden[genes + genes // 2 :]]

    def back(first, count, gatt):
        o, lse = attended[0 if first < cut else 1]
        at = first if first < cut else first - cut
        return attend_back_call(mask, qkv, o, gatt, lse, count, (first, at, first))

    early, half = 128 * cut, width // 2
    late = width - early
    backs = [back(0, cut, gatt)]
    backs, gatt, way["ahead"], way["over3"], hid_send = fence(
        backs, gatt, way["ahead"], way["over3"], hid_send
    )
    way = steps.send(way)
    first = att_weights_call(
        place, [[a], o_parts], list(backs[0][:3]) + [gr],
        [(0, i * early, early) for i in range(3)] + [(1, 3 * early + i * half, half) for i in range(2)],
    )
    first, gatt, way, hid_send = fence(first, gatt, way, hid_send)
    way = steps.send(way)
    hid_got = [ring.swap_blk(hid_send[0])]
    first_sib = ring.swap_core(first[n])
    one = (pairs - cut) // 4
    backs.append(back(cut, one, gatt))
    backs, gatt, first, first_sib, up_rows = fence(backs, gatt, first, first_sib, up_rows)
    steps_first = ring.reduce([[first[s], first_sib[s]] for s in range(n)], 3)
    way_first = next(steps_first)
    backs.append(back(cut + one, pairs - cut - one, gatt))
    backs, way_first, way, hid_got, hid_send = fence(backs, way_first, way, hid_got, hid_send)
    hid_got.append(ring.swap_blk(hid_send[1]))
    way = steps.send(way)
    grads = [t[i] for i in range(3) for t in backs]
    in_send, in_sums_send = in_call(place, x, gr, ln1_gain, grads, weights, 1, bf16)
    sums_early = side_by_side(
        [mid_sums[:4].reshape(-1), up_rows.reshape(-1)]
        + [t[i].reshape(-1) for i in (3, 4) for t in backs]
    )
    in_send, backs, way_first, hid_got, way = fence(in_send, backs, way_first, hid_got, way)
    ffn_sum = steps.send(way)
    ffn_sum = [ffn_sum[:units], ffn_sum[units:]]
    ffn_got = [ring.swap_blk(ffn_sum[0])]
    way_first = steps_first.send(way_first)
    in_got = ring.swap_blk(in_send)
    second = att_weights_call(
        place, [[a]], [t[i] for i in range(3) for t in backs[1:]],
        [(0, i * late, late) for i in range(3)],
    )
    second, way_first, grads, sums_early, ffn_got, ffn_sum = fence(
        second, way_first, grads, sums_early, ffn_got, ffn_sum
    )
    ffn_got.append(ring.swap_blk(ffn_sum[1]))
    way_first = steps_first.send(way_first)
    second_sib = ring.swap_core(second[n])
    steps_second = ring.reduce([[second[s], second_sib[s]] for s in range(n)], 3)
    way_second = next(steps_second)
    in_own, in_sums = in_call(place, x, gr, ln1_gain, grads, weights, 0, f32)
    w_up_grad = ffn_sum[0].astype(f32) + ffn_got[0].astype(f32)
    in_own, in_sums, in_sums_send, way_first, way_second, w_up_grad = fence(
        in_own, in_sums, in_sums_send, way_first, way_second, w_up_grad
    )
    way_first = steps_first.send(way_first)
    way_second = steps_second.send(way_second)
    ln1_sums = (in_sums + in_sums_send)[:2].reshape(-1)
    steps_sums = ring.total(side_by_side([sums_early, ln1_sums]))
    sums = next(steps_sums)
    way_first, way_second, sums = fence(way_first, way_second, sums)
    first_sum = steps_first.send(way_first)
    first_got = ring.swap_blk(first_sum)
    way_second = steps_second.send(way_second)
    sums = steps_sums.send(sums)
    way_second, sums = fence(way_second, sums)
    way_second = steps_second.send(way_second)
    sums = steps_sums.send(sums)
    way_second, sums, ffn_got = fence(way_second, sums, ffn_got)
    second_sum = steps_second.send(way_second)
    second_got = ring.swap_blk(second_sum)
    sums = steps_sums.send(sums)
    sums = steps_sums.send(sums)
    down_sum, down_got, first_sum, first_got, in_got, second_sum, _ = fence(
        ffn_sum[1], ffn_got[1], first_sum, first_got, in_got, second_sum, sums[0]
    )
    sums = steps_sums.send(sums)
    w_down_grad, first_rows, second_rows = [
        a.astype(f32) + b.astype(f32)
        for a, b in ((down_sum, down_got), (first_sum, first_got), (second_sum, second_got))
    ]

    def home(own, got):
        got = got.astype(own.dtype)
        return jnp.where(blk == 0, jnp.stack([own, got]), jnp.stack([got, own]))

    hidden = home(out_hidden[:genes], jnp.concatenate(hid_got))
    in_grad = home(in_own, in_got)
    marks = [width] * 4 + [shards * units]
    marks += 2 * [128 * c for c in (cut, one, pairs - cut - one)] + [width] * 2
    pieces, at = [], 0
    for size in marks:
        pieces.append(sums[at : at + size])
        at += size
    ln2_gain_g, ln2_bias_g, out_bias_g, down_bias_g, up_bias_g = pieces[:5]
    q_bias_g, v_bias_g = jnp.concatenate(pieces[5:8]), jnp.concatenate(pieces[8:11])
    ln1_gain_g, ln1_bias_g = pieces[11:]
    w_qkv_grad = jnp.concatenate(
        [
            t
            for i in range(3)
            for t in (
                first_rows[:, i * early : (i + 1) * early],
                second_rows[:, i * late : (i + 1) * late],
            )
        ],
        axis=1,
    )
    return (
        hidden,
        in_grad,
        ln1_gain_g,
        ln1_bias_g,
        w_qkv_grad,
        q_bias_g,
        v_bias_g,
        first_rows[:, 3 * early :],
        out_bias_g,
        ln2_gain_g,
        ln2_bias_g,
        w_up_grad,
        up_bias_g,
        w_down_grad,
        down_bias_g,
    )


def solution(mesh):
    placed = (
        P("cell", "blk", None),
        P("cell"),
        P(),
        P(),
        P("cell", None),
        P(),
        P(),
        P("cell", None),
        P(),
        P(),
        P(),
        P("cell", None),
        P(),
        P("cell", None),
        P(),
        P("cell", "blk", None),
    )
    return jax.shard_map(
        partial(local_swapped, dict(mesh.shape)) if swappable(mesh) else local,
        mesh=mesh,
        in_specs=placed,
        out_specs=(
            P("cell", "blk", None),
            P("cell", "blk", None),
            P(),
            P(),
            P("cell", None),
            P(),
            P(),
            P("cell", None),
            P(),
            P(),
            P(),
            P("cell", None),
            P(),
            P("cell", None),
            P(),
        ),
        check_vma=False,
    )
```

```python
from functools import partial
import math

import jax
import jax.numpy as jnp
from jax import lax
from jax.experimental import pallas as pl
from jax.experimental.pallas import tpu as pltpu
from jax.sharding import PartitionSpec as P

HEAD_DIM = 64


epsilon = 1e-05
far_below = -1e30
row_contract = (((0,), (0,)), ((), ()))
col_contract = (((1,), (1,)), ((), ()))


def passed_along(x, axis, by):
    count = lax.axis_size(axis)
    return lax.ppermute(x, axis, [(i, (i + by) % count) for i in range(count)])


def layer_norm(source, gain_vec, shift_vec):
    row_mean = jnp.mean(source, axis=-1, keepdims=True)
    centered = source - row_mean
    row_var = jnp.mean(centered * centered, axis=-1, keepdims=True)
    return centered * lax.rsqrt(row_var + epsilon) * gain_vec + shift_vec


def local(
    hidden_in,
    lengths,
    ln1_gain,
    ln1_bias,
    w_qkv,
    q_bias,
    v_bias,
    w_out,
    out_bias,
    ln2_gain,
    ln2_bias,
    w_up,
    up_bias,
    w_down,
    down_bias,
    cotangent,
):
    cell_count, local_genes, model_width = hidden_in.shape
    row_count = cell_count * local_genes
    head_count = model_width // HEAD_DIM
    score_scale = 1.0 / math.sqrt(HEAD_DIM)
    cycle_size = lax.axis_size("blk")
    cycle_place = lax.axis_index("blk")
    ratio_ff = up_bias.shape[0] // model_width
    head_shape = (cell_count, local_genes, head_count, HEAD_DIM)
    stat_shape = (cell_count, head_count, local_genes)
    inputs = hidden_in.astype(jnp.float32).reshape(row_count, model_width)
    cot_rows = cotangent.reshape(row_count, model_width)
    gene_index = jnp.arange(local_genes, dtype=jnp.int32)
    query_valid = (cycle_place * local_genes + gene_index)[None, :] < lengths[:, None]
    normed, ln1_pull = jax.vjp(layer_norm, inputs, ln1_gain, ln1_bias)
    normed_low = normed.astype(jnp.bfloat16)
    part_cols = normed_low
    joined = jnp.dot(
        part_cols,
        lax.all_gather(w_qkv, "cell", axis=0, tiled=True),
        preferred_element_type=jnp.float32,
    )
    queries = (joined[:, :model_width] + q_bias).astype(jnp.bfloat16).reshape(head_shape)
    keys_own = joined[:, model_width : 2 * model_width].astype(jnp.bfloat16).reshape(head_shape)
    values_own = (joined[:, 2 * model_width :] + v_bias).astype(jnp.bfloat16).reshape(head_shape)

    def block_scores(key_block, owner_index):
        scores = (
            jnp.einsum("cqhd,ckhd->chqk", queries, key_block, preferred_element_type=jnp.float32)
            * score_scale
        )
        key_valid = (owner_index * local_genes + gene_index)[None, :] < lengths[:, None]
        return (scores, key_valid[:, None, None, :])

    def stats_turn(owner_index, carried, key_block):
        row_top, row_total = carried
        scores, is_valid = block_scores(key_block, owner_index)
        new_top = jnp.maximum(row_top, jnp.max(jnp.where(is_valid, scores, far_below), axis=-1))
        raised = jnp.where(is_valid, jnp.exp(scores - new_top[..., None]), 0.0)
        return (new_top, row_total * jnp.exp(row_top - new_top) + jnp.sum(raised, axis=-1))

    first_stats = stats_turn(
        cycle_place,
        (jnp.full(stat_shape, far_below, jnp.float32), jnp.zeros(stat_shape, jnp.float32)),
        keys_own,
    )

    def stats_step(step_index, carried):
        stats_now, key_block = carried
        key_block = passed_along(key_block, "blk", 1)
        return (
            stats_turn((cycle_place - step_index) % cycle_size, stats_now, key_block),
            key_block,
        )

    final_stats = lax.fori_loop(1, cycle_size, stats_step, (first_stats, keys_own))[0]
    log_total = final_stats[0] + jnp.log(final_stats[1])

    def block_weights(key_block, owner_index):
        scores, is_valid = block_scores(key_block, owner_index)
        return jnp.where(is_valid, jnp.exp(scores - log_total[..., None]), 0.0)

    def mix_turn(owner_index, mixed_sum, key_block, value_block):
        weights = block_weights(key_block, owner_index).astype(jnp.bfloat16)
        return mixed_sum + jnp.einsum(
            "chqk,ckhd->cqhd", weights, value_block, preferred_element_type=jnp.float32
        )

    mixed_start = mix_turn(cycle_place, jnp.zeros(head_shape, jnp.float32), keys_own, values_own)

    def pair_step(step_index, carried):
        inner, key_block, value_block = carried
        key_block, value_block = passed_along((key_block, value_block), "blk", 1)
        return (
            mix_turn((cycle_place - step_index) % cycle_size, inner, key_block, value_block),
            key_block,
            value_block,
        )

    mixed_sum = lax.fori_loop(1, cycle_size, pair_step, (mixed_start, keys_own, values_own))[0]
    mixed_low = (
        jnp.where(query_valid[:, :, None, None], mixed_sum, 0.0)
        .astype(jnp.bfloat16)
        .reshape(row_count, model_width)
    )
    part_cols = mixed_low
    branch = jnp.dot(
        part_cols,
        lax.all_gather(w_out, "cell", axis=0, tiled=True),
        preferred_element_type=jnp.float32,
    )
    middle = inputs + branch + out_bias
    normed2, ln2_pull = jax.vjp(layer_norm, middle, ln2_gain, ln2_bias)
    normed2_low = normed2.astype(jnp.bfloat16)
    gelu_exact = partial(jax.nn.gelu, approximate=False)
    ff_total = up_bias.shape[0]
    out_sum = jnp.zeros((row_count, model_width), jnp.float32)
    ffn_hidden = jnp.zeros((row_count, ff_total), jnp.bfloat16)
    up_piece = lax.all_gather(w_up, "cell", axis=0, tiled=True)
    down_piece = lax.all_gather(w_down, "cell", axis=0, tiled=True)
    pre_gelu = lax.dot_general(
        normed2_low, up_piece, col_contract, preferred_element_type=jnp.float32
    )
    pre_gelu = pre_gelu + up_bias
    activation, gelu_pull = jax.vjp(gelu_exact, pre_gelu)
    active_low = activation.astype(jnp.bfloat16)
    out_sum = out_sum + jnp.dot(active_low, down_piece, preferred_element_type=jnp.float32)
    grad_active = lax.dot_general(
        cot_rows, down_piece, col_contract, preferred_element_type=jnp.float32
    )
    pre_low = gelu_pull(grad_active)[0].astype(jnp.bfloat16)
    back_sum = jnp.dot(pre_low, up_piece, preferred_element_type=jnp.float32)
    ffn_hidden = lax.dynamic_update_slice_in_dim(ffn_hidden, active_low, jnp.int32(0), 1)
    out_sum, back_sum, pre_grads, hidden = (out_sum, back_sum, pre_low, ffn_hidden)
    out_hidden = (middle + out_sum + down_bias).astype(jnp.bfloat16).reshape(hidden_in.shape)
    grad_ln2, ln2_gain_part, ln2_bias_part = ln2_pull(back_sum)
    grad_middle = cot_rows.astype(jnp.float32) + grad_ln2
    branch_grad = grad_middle.astype(jnp.bfloat16)
    grad_mixed = lax.dot_general(
        branch_grad,
        lax.all_gather(w_out, "cell", axis=0, tiled=True),
        col_contract,
        preferred_element_type=jnp.float32,
    )
    grad_out = jnp.where(
        query_valid[:, :, None, None], grad_mixed.astype(jnp.bfloat16).reshape(head_shape), 0.0
    )
    delta = jnp.einsum("cqhd,cqhd->chq", grad_out.astype(jnp.float32), mixed_sum)

    def grad_step(step_index, carried):
        query_grad, key_block, value_block, key_grad, value_grad = carried
        owner_index = (cycle_place - step_index) % cycle_size
        weights = block_weights(key_block, owner_index)
        grad_weights = jnp.einsum(
            "cqhd,ckhd->chqk", grad_out, value_block, preferred_element_type=jnp.float32
        )
        score_grad = (weights * (grad_weights - delta[..., None])).astype(jnp.bfloat16)
        query_grad = (
            query_grad
            + jnp.einsum(
                "chqk,ckhd->cqhd", score_grad, key_block, preferred_element_type=jnp.float32
            )
            * score_scale
        )
        key_grad = (
            key_grad
            + jnp.einsum("chqk,cqhd->ckhd", score_grad, queries, preferred_element_type=jnp.float32)
            * score_scale
        )
        value_grad = value_grad + jnp.einsum(
            "chqk,cqhd->ckhd",
            weights.astype(jnp.bfloat16),
            grad_out,
            preferred_element_type=jnp.float32,
        )
        key_block, value_block, key_grad, value_grad = (
            passed_along(key_block, "blk", 1),
            passed_along(value_block, "blk", 1),
            passed_along(key_grad.astype(jnp.bfloat16), "blk", 1).astype(key_grad.dtype),
            passed_along(value_grad.astype(jnp.bfloat16), "blk", 1).astype(value_grad.dtype),
        )
        return (query_grad, key_block, value_block, key_grad, value_grad)

    zero_heads = jnp.zeros(head_shape, jnp.float32)
    cycle_done = lax.fori_loop(
        0, cycle_size, grad_step, (zero_heads, keys_own, values_own, zero_heads, zero_heads)
    )
    query_low = cycle_done[0].astype(jnp.bfloat16).reshape(row_count, model_width)
    key_low = cycle_done[3].astype(jnp.bfloat16).reshape(row_count, model_width)
    value_low = cycle_done[4].astype(jnp.bfloat16).reshape(row_count, model_width)
    grad_joined = jnp.concatenate([query_low, key_low, value_low], axis=1)
    grad_normed = lax.dot_general(
        grad_joined,
        lax.all_gather(w_qkv, "cell", axis=0, tiled=True),
        col_contract,
        preferred_element_type=jnp.float32,
    )
    grad_ln1, ln1_gain_part, ln1_bias_part = ln1_pull(grad_normed)
    in_grad = (grad_middle + grad_ln1).reshape(hidden_in.shape)
    qkv_term = lax.dot_general(
        normed_low, grad_joined, row_contract, preferred_element_type=jnp.float32
    )
    out_term = lax.dot_general(
        mixed_low, branch_grad, row_contract, preferred_element_type=jnp.float32
    )
    up_term = lax.dot_general(
        pre_grads, normed2_low, row_contract, preferred_element_type=jnp.float32
    )
    down_term = lax.dot_general(hidden, cot_rows, row_contract, preferred_element_type=jnp.float32)
    ffn_term = jnp.concatenate([up_term, down_term], axis=1).reshape(
        lax.axis_size("cell") * (model_width // lax.axis_size("cell")), ratio_ff * 2 * model_width
    )
    summed = lax.psum_scatter(
        jnp.concatenate([qkv_term, out_term, ffn_term], axis=1).astype(jnp.bfloat16),
        "cell",
        scatter_dimension=0,
        tiled=True,
    ).astype(jnp.float32)
    summed = lax.psum(summed.astype(jnp.bfloat16), "blk").astype(jnp.float32)
    own_rows = summed.shape[0]
    w_qkv_grad = summed[:, : 3 * model_width]
    w_out_grad = summed[:, 3 * model_width : 4 * model_width]
    ffn_grads = summed[:, 4 * model_width :].reshape(own_rows * ratio_ff, 2 * model_width)
    w_up_grad = ffn_grads[:, :model_width]
    w_down_grad = ffn_grads[:, model_width:]
    vectors = lax.psum(
        (
            ln1_gain_part,
            ln1_bias_part,
            jnp.sum(query_low, axis=0, dtype=jnp.float32),
            jnp.sum(value_low, axis=0, dtype=jnp.float32),
            jnp.sum(branch_grad, axis=0, dtype=jnp.float32),
            ln2_gain_part,
            ln2_bias_part,
            jnp.sum(pre_grads, axis=0, dtype=jnp.float32),
            jnp.sum(cot_rows, axis=0, dtype=jnp.float32),
        ),
        ("cell", "blk"),
    )
    return (
        out_hidden,
        in_grad,
        vectors[0],
        vectors[1],
        w_qkv_grad,
        vectors[2],
        vectors[3],
        w_out_grad,
        vectors[4],
        vectors[5],
        vectors[6],
        w_up_grad,
        vectors[7],
        w_down_grad,
        vectors[8],
    )


bf16 = jnp.bfloat16
f32 = jnp.float32
NN = (((1,), (0,)), ((), ()))
NT = (((1,), (1,)), ((), ()))
TN = (((0,), (0,)), ((), ()))
AXES = ("cell", "blk")
VMEM_LIMIT = 60 * 2**20
ROWS = 256
COST_PART = 50
OFFSETS = (0, -1, -2, -3, -4, 1, 2, 3)


def swappable(mesh):
    return dict(mesh.shape) == {"cell": 16, "blk": 2}


def dot(a, b, dims):
    return lax.dot_general(a, b, dims, preferred_element_type=f32)


def params():
    return pltpu.CompilerParams(vmem_limit_bytes=VMEM_LIMIT)


def cost(flops, nbytes, trans=0):
    return pl.CostEstimate(
        flops=int(flops) // COST_PART,
        bytes_accessed=int(nbytes) // COST_PART,
        transcendentals=int(trans) // COST_PART,
    )


def shape(dims, dtype):
    return jax.ShapeDtypeStruct(dims, dtype)


ANY = pl.BlockSpec(memory_space=pl.ANY)


def fixed(dims):
    return pl.BlockSpec(dims, lambda *_: (0,) * len(dims))


def rowed(rows, width):
    return pl.BlockSpec((rows, width), lambda i, *_: (i, 0))


class Ring:
    def __init__(self, sizes):
        self.cells, self.blks = sizes["cell"], sizes["blk"]
        self.chips = self.cells // 2
        depth = self.chips // 2
        self.order = [2 * z for z in range(depth)] + [2 * z + 1 for z in reversed(range(depth))]
        self.place = [self.order.index(c) for c in range(self.chips)]

    def permute(self, x, target):
        pairs = []
        for cell in range(self.cells):
            for blk in range(self.blks):
                to_cell, to_blk = target(cell, blk)
                pairs.append((cell * self.blks + blk, to_cell * self.blks + to_blk))
        return lax.ppermute(x, AXES, pairs)

    def shift(self, x, by):
        def target(cell, blk):
            chip, core = cell // 2, cell % 2
            way = 1 - 2 * ((core + blk) % 2)
            return self.order[(self.place[chip] + way * by) % self.chips] * 2 + core, blk

        return self.permute(x, target)

    def swap_core(self, x):
        return self.permute(x, lambda cell, blk: (cell ^ 1, blk))

    def swap_blk(self, x):
        return self.permute(x, lambda cell, blk: (cell, 1 - blk))

    def chips_of_slots(self, core):
        chip = lax.axis_index("cell") // 2
        way = 1 - 2 * ((core + lax.axis_index("blk")) % 2)
        place = jnp.array(self.place, jnp.int32)[chip]
        return jnp.array(self.order, jnp.int32)[
            (place + way * jnp.array(OFFSETS, jnp.int32)) % self.chips
        ]

    def gather(self, x, back):
        slots = [x] + [None] * 7
        for k in range(1, 5):
            slots[k] = self.shift(slots[k - 1], 1)
            if k <= back:
                slots[4 + k] = self.shift(slots[3 + k] if k > 1 else slots[0], -1)
            if k > back + 1:
                slots[3 + k] = self.swap_blk(slots[k - 1])
            slots = yield slots

    def reduce(self, parts, back, alone=False):
        def added(terms):
            total = terms[0].astype(f32)
            for t in terms[1:]:
                total = total + t.astype(f32)
            return total.astype(bf16)

        way = {"ahead": self.shift(added(parts[4]), -1)}
        if back:
            way["behind"] = self.shift(added(parts[4 + back]), 1)
        for k in range(3, back, -1):
            way[f"over{k}"] = self.swap_blk(added(parts[4 + k]))
        way = yield way
        for k in (3, 2, 1):
            extra = [way.pop(f"over{k}")] if f"over{k}" in way else []
            way["ahead"] = self.shift(added([way["ahead"]] + parts[k] + extra), -1)
            if k < back and not (alone and k == 1):
                way["behind"] = self.shift(added([way["behind"]] + parts[4 + k]), 1)
            way = yield way
        if alone:
            way["behind"] = self.shift(added([way["behind"]] + parts[5]), 1)
            way = yield way
        ends = [way["ahead"]] + ([way["behind"]] if back else [])
        yield added(ends + parts[0])

    def total(self, x):
        count = self.cells * self.blks
        bits = [1 << i for i in range(count.bit_length() - 1)]
        for bit in [b for b in bits if b >= self.blks] + [b for b in bits if b < self.blks]:
            other = bit
            moved = self.permute(
                x, lambda cell, blk: divmod((cell * self.blks + blk) ^ other, self.blks)
            )
            x, moved = yield x, moved
            x = x + moved
        yield x


def norm_parts(x):
    mean = jnp.mean(x, axis=-1, keepdims=True)
    centered = x - mean
    var = jnp.mean(centered * centered, axis=-1, keepdims=True)
    scale = lax.rsqrt(var + epsilon)
    return centered * scale, scale


def norm_back(xh, scale, gain, grad):
    e = grad * gain
    return scale * (
        e - jnp.mean(e, axis=-1, keepdims=True) - xh * jnp.mean(e * xh, axis=-1, keepdims=True)
    )


def colsum(x):
    return jnp.sum(x, axis=0, keepdims=True)


def place_rows(slots, target, place_ref, sem, first=0, cols=None):
    height = slots[0].shape[0]
    start, wide = cols or (0, slots[0].shape[1])
    return [
        pltpu.make_async_copy(
            slot.at[:, pl.ds(start, wide)],
            target.at[
                pl.ds(pl.multiple_of(place_ref[i] * height, 16), height),
                pl.ds(first + start, wide),
            ],
            sem.at[i],
        )
        for i, slot in enumerate(slots)
    ]


def qkv_kernel(n, place_ref, x_ref, gain_ref, bias_ref, qb_ref, vb_ref, *refs):
    slots, (a_ref, q_ref, k_ref, v_ref, w, sem) = refs[:n], refs[n:]
    width = x_ref.shape[1]
    first = pl.program_id(0) == 0
    copies = [
        place_rows(slots, w, place_ref, sem.at[j], cols=(j * width, width)) for j in range(3)
    ]

    @pl.when(first)
    def _():
        for group in copies:
            for c in group:
                c.start()

    xh, _ = norm_parts(x_ref[...].astype(f32))
    a_ref[...] = (xh * gain_ref[...] + bias_ref[...]).astype(bf16)
    for j, (res_ref, add_ref) in enumerate(((q_ref, qb_ref), (k_ref, None), (v_ref, vb_ref))):

        @pl.when(first)
        def _(group=copies[j]):
            for c in group:
                c.wait()

        res = dot(a_ref[...], w[:, j * width : (j + 1) * width], NN)
        if add_ref is not None:
            res = res + add_ref[...]
        res_ref[...] = res.astype(bf16)


def qkv_call(place, x, gain, bias, qb, vb, slots):
    rows, width = x.shape
    n = len(slots)
    block = rowed(ROWS, width)
    vec = fixed((1, width))
    return pl.pallas_call(
        partial(qkv_kernel, n),
        grid_spec=pltpu.PrefetchScalarGridSpec(
            num_scalar_prefetch=1,
            grid=(rows // ROWS,),
            in_specs=[block, vec, vec, vec, vec] + [ANY] * n,
            out_specs=[block] * 4,
            scratch_shapes=[
                pltpu.VMEM((width, 3 * width), bf16),
                pltpu.SemaphoreType.DMA((3, n)),
            ],
        ),
        out_shape=[shape((rows, width), bf16)] * 4,
        compiler_params=params(),
        cost_estimate=cost(6 * rows * width * width, 2 * width * (5 * rows + 3 * width)),
        name="qkv",
    )(place, x, gain, bias, qb, vb, *slots)


def head_keys(low, k, v, mask, fill):
    res = []
    for half in range(2):
        mine = low if half == 0 else jnp.logical_not(low)
        res.append(
            (
                jnp.where(mine, k.astype(f32), mask).astype(bf16),
                jnp.where(mine, v.astype(f32), fill).astype(bf16),
            )
        )
    return res


def head_query(low, lane, half, q):
    mine = low if half == 0 else jnp.logical_not(low)
    one = lane == (HEAD_DIM if half == 0 else 0)
    q = q.astype(f32) * (1.0 / math.sqrt(HEAD_DIM))
    return jnp.where(mine, q, jnp.where(one, 1.0, 0.0)).astype(bf16)


def attend_kernel(qrows, ahead, mask_ref, keep_ref, q_ref, k_ref, v_ref, o_ref, lse_ref):
    n = q_ref.shape[0]
    lane = lax.broadcasted_iota(jnp.int32, (n, 128), 1)
    pair = head_keys(lane < HEAD_DIM, k_ref[...], v_ref[...], mask_ref[...], 1.0)
    lane = lane[:qrows]
    low = lane < HEAD_DIM
    items = [(i, half) for i in range(n // qrows) for half in range(2)]

    def scores(i, half):
        q = head_query(low, lane, half, q_ref[pl.ds(i * qrows, qrows), :])
        return dot(q, pair[half][0], NT)

    waiting = [scores(*item) for item in items[:ahead]]
    for at, (i, half) in enumerate(items):
        if at + ahead < len(items):
            waiting.append(scores(*items[at + ahead]))
        s = waiting.pop(0)
        rows = pl.ds(i * qrows, qrows)
        top = jnp.max(s, axis=1, keepdims=True)
        mixed = dot(jnp.exp(s - top).astype(bf16), pair[half][1], NN)
        total = pltpu.roll(mixed, HEAD_DIM, 1)
        o, lse = mixed / total, top + jnp.log(total)
        if half == 0:
            o_first, lse_first = o, lse
            continue
        o_ref[rows, :] = (jnp.where(low, o_first, o) * keep_ref[rows, :]).astype(bf16)
        lse = jnp.transpose(jnp.where(low, lse_first, lse))
        lse_ref[0, :, rows] = lse[:1, :]
        lse_ref[1, :, rows] = lse[HEAD_DIM : HEAD_DIM + 1, :]


def attend_call(mask, keep, qkv, first, count, qrows=256, ahead=2):
    n = qkv[0].shape[0]
    block = pl.BlockSpec((n, 128), lambda h: (0, h + first))
    return pl.pallas_call(
        partial(attend_kernel, qrows, ahead),
        grid=(count,),
        in_specs=[fixed((n, 1)), fixed((n, 1)), block, block, block],
        out_specs=[
            pl.BlockSpec((n, 128), lambda h: (0, h)),
            pl.BlockSpec((2, 1, n), lambda h: (h, 0, 0)),
        ],
        out_shape=[shape((n, 128 * count), bf16), shape((2 * count, 1, n), f32)],
        compiler_params=params(),
        cost_estimate=cost(20 * count * n * n * 128, 8 * n * 128 * count, 2 * count * n * n),
        name="attend",
    )(mask, keep, *qkv)


def attend_back_kernel(
    qrows, mask_ref, q_ref, k_ref, v_ref, o_ref, go_ref, lse_ref,
    gq_ref, gk_ref, gv_ref, sq_ref, sv_ref, gk_sum, gv_sum,
):
    n = q_ref.shape[0]
    lane = lax.broadcasted_iota(jnp.int32, (n, 128), 1)
    k = k_ref[...]
    scale = 1.0 / math.sqrt(HEAD_DIM)
    pair = head_keys(lane < HEAD_DIM, k, v_ref[...], mask_ref[...], 0.0)
    k_turned = jnp.transpose(k)
    prod = jnp.transpose(o_ref[...].astype(f32) * go_ref[...].astype(f32))
    delta = [colsum(prod[half * HEAD_DIM : (half + 1) * HEAD_DIM, :]) for half in range(2)]
    top = lane[:qrows]
    for i in range(n // qrows):
        rows = pl.ds(i * qrows, qrows)
        gq = []
        for half in range(2):
            q_raw, go = q_ref[rows, :], go_ref[rows, :]
            q = head_query(top < HEAD_DIM, top, half, q_raw)
            p = jnp.exp(dot(pair[half][0], q, NT) - lse_ref[half, :, rows])
            gp = dot(pair[half][1], go, NT)
            gs = (p * (gp - delta[half][:, i * qrows : (i + 1) * qrows])).astype(bf16)
            gv = dot(p.astype(bf16), go, NN)
            gk = dot(gs, q_raw, NN)
            if i == 0:
                gv_sum[half], gk_sum[half] = gv, gk
            else:
                gv_sum[half] += gv
                gk_sum[half] += gk
            gq.append(dot(k_turned, gs, NN))
        turned = jnp.concatenate([gq[0][:HEAD_DIM], gq[1][HEAD_DIM:]], axis=0)
        gq_ref[rows, :] = jnp.transpose(turned * scale).astype(bf16)
    low = lane < HEAD_DIM
    gk_ref[...] = (jnp.where(low, gk_sum[0], gk_sum[1]) * scale).astype(bf16)
    gv = jnp.where(low, gv_sum[0], gv_sum[1]).astype(bf16)
    gv_ref[...] = gv
    sq_ref[...] = colsum(gq_ref[...].astype(f32))
    sv_ref[...] = colsum(gv.astype(f32))


def attend_back_call(mask, qkv, o, go, lse, count, firsts, qrows=512):
    n = go.shape[0]

    def block(first):
        return pl.BlockSpec((n, 128), lambda h: (0, h + first))

    own, vec = block(0), pl.BlockSpec((1, 128), lambda h: (0, h))
    at_qkv, at_o, at_go = firsts
    return pl.pallas_call(
        partial(attend_back_kernel, qrows),
        grid=(count,),
        in_specs=[fixed((n, 1))]
        + [block(at_qkv)] * 3
        + [block(at_o), block(at_go), pl.BlockSpec((2, 1, n), lambda h: (h + at_o, 0, 0))],
        out_specs=[own, own, own, vec, vec],
        out_shape=[shape((n, 128 * count), bf16)] * 3 + [shape((1, 128 * count), f32)] * 2,
        scratch_shapes=[pltpu.VMEM((2, n, 128), f32)] * 2,
        compiler_params=params(),
        cost_estimate=cost(32 * count * n * n * 128, 16 * n * 128 * count, 2 * count * n * n),
        name="attend_back",
    )(mask, *qkv, o, go, lse)


def load_wout(slots, place_ref, w, sem):
    wide = w.shape[1]
    start = slots[0].shape[1] - wide
    copies = place_rows(slots, w, place_ref, sem, -start, (start, wide))

    @pl.when(pl.program_id(0) == 0)
    def _():
        for c in copies:
            c.start()
        for c in copies:
            c.wait()


def out_kernel(n, place_ref, x_ref, bias_ref, gain_ref, shift_ref, *refs):
    slots, o_refs, (m_ref, b_ref, w, sem) = refs[:n], refs[n:-4], refs[-4:]
    load_wout(slots, place_ref, w, sem)
    m = x_ref[...].astype(f32) + bias_ref[...]
    first = 0
    for o_ref in o_refs:
        m = m + dot(o_ref[...], w[first : first + o_ref.shape[1], :], NN)
        first += o_ref.shape[1]
    m_ref[...] = m
    xh, _ = norm_parts(m)
    b_ref[...] = (xh * gain_ref[...] + shift_ref[...]).astype(bf16)


def out_call(place, x, o_parts, slots, bias, gain, shift):
    rows, width = x.shape
    n = len(slots)
    vec = fixed((1, width))
    block = rowed(ROWS, width)
    return pl.pallas_call(
        partial(out_kernel, n),
        grid_spec=pltpu.PrefetchScalarGridSpec(
            num_scalar_prefetch=1,
            grid=(rows // ROWS,),
            in_specs=[block, vec, vec, vec]
            + [ANY] * n
            + [rowed(ROWS, o.shape[1]) for o in o_parts],
            out_specs=[block, block],
            scratch_shapes=[pltpu.VMEM((width, width), bf16), pltpu.SemaphoreType.DMA((n,))],
        ),
        out_shape=[shape((rows, width), f32), shape((rows, width), bf16)],
        compiler_params=params(),
        cost_estimate=cost(4 * rows * width * width, width * (10 * rows + 2 * width)),
        name="out",
    )(place, x, bias, gain, shift, *slots, *o_parts)


def gelu_both(z, gh):
    t = 1.0 / (1.0 + jnp.abs(z) * (0.3275911 / math.sqrt(2.0)))
    e = jnp.exp(z * z * -0.5)
    half = (0.254829592, -0.284496736, 1.421413741, -1.453152027, 1.061405429)
    tail = half[4] * 0.5
    for c in half[3::-1]:
        tail = tail * t + 0.5 * c
    tail = tail * t * e
    phi = jnp.where(z > 0, 1.0 - tail, tail)
    return z * phi, gh * (phi + z * e * (1.0 / math.sqrt(2.0 * math.pi)))


def ffn_kernel(n, later, *refs):
    b_own, b_sib, g_own, g_sib, ub_ref = refs[:5]
    slots = refs[5 : 5 + n]
    refs = refs[5 + n :]
    if later:
        acc_o, acc_g = refs[:2]
        refs = refs[2:]
        h_ref, gz_ref, sum_ref, oo_ref, go_ref, os_ref, gs_ref, us, ds, sem = refs
    else:
        h_ref, gz_ref, sum_ref, oo_ref, go_ref, us, ds, sem = refs
    units = us.shape[0] // n
    i = pl.program_id(0)
    near = i < pl.num_programs(0) // 2
    copies = []
    for s, slot in enumerate(slots):
        rows = pl.ds(s * units, units)
        copies.append(
            pltpu.make_async_copy(slot.at[pl.ds(0, units), :], us.at[rows, :], sem.at[0, s])
        )
        copies.append(
            pltpu.make_async_copy(slot.at[pl.ds(units, units), :], ds.at[rows, :], sem.at[1, s])
        )

    @pl.when(i == 0)
    def _():
        for c in copies:
            c.start()
        for c in copies:
            c.wait()
        sum_ref[...] = jnp.zeros_like(sum_ref)

    b = jnp.where(near, b_own[...], b_sib[...])
    g = jnp.where(near, g_own[...], g_sib[...])
    h, gz = gelu_both(dot(b, us[...], NT) + ub_ref[...], dot(g, ds[...], NT))
    h, gz = h.astype(bf16), gz.astype(bf16)
    h_ref[...] = h
    gz_ref[...] = gz
    sum_ref[...] += colsum(gz.astype(f32))
    out = dot(h, ds[...], NN)
    back = dot(gz, us[...], NN)
    if not later:
        oo_ref[...] = out
        go_ref[...] = back
        return
    out = out + acc_o[...]
    back = back + acc_g[...]

    @pl.when(near)
    def _():
        oo_ref[...] = out.astype(bf16)
        go_ref[...] = back.astype(bf16)

    @pl.when(jnp.logical_not(near))
    def _():
        os_ref[...] = out.astype(bf16)
        gs_ref[...] = back.astype(bf16)


def ffn_call(b_own, b_sib, g_own, g_sib, ub, slots, acc=None):
    rows, width = b_own.shape
    half = rows // ROWS
    n = len(slots)
    units = ub.shape[1]
    later = acc is not None
    near = pl.BlockSpec((ROWS, width), lambda i: (jnp.minimum(i, half - 1), 0))
    far = pl.BlockSpec((ROWS, width), lambda i: (jnp.maximum(i - half, 0), 0))
    both = rowed(ROWS, width)
    acc = list(acc or ())
    out_specs = [rowed(ROWS, units), rowed(ROWS, units), fixed((1, units))]
    out_shape = [shape((2 * rows, units), bf16)] * 2 + [shape((1, units), f32)]
    if later:
        out_specs += [near, near, far, far]
        out_shape += [shape((rows, width), bf16)] * 4
    else:
        out_specs += [both, both]
        out_shape += [shape((2 * rows, width), f32)] * 2
    return pl.pallas_call(
        partial(ffn_kernel, n, later),
        grid=(2 * half,),
        in_specs=[near, far, near, far, fixed((1, units))] + [ANY] * n + [both] * len(acc),
        out_specs=out_specs,
        out_shape=out_shape,
        scratch_shapes=[
            pltpu.VMEM((units, width), bf16),
            pltpu.VMEM((units, width), bf16),
            pltpu.SemaphoreType.DMA((2, n)),
        ],
        compiler_params=params(),
        cost_estimate=cost(
            24 * rows * width * units, rows * width * (24 + 16 * later), 4 * rows * units
        ),
        name="ffn",
    )(b_own, b_sib, g_own, g_sib, ub, *slots, *acc)


def ffn_weights_kernel(n, gz, h, b_own, b_sib, g_own, g_sib, *refs):
    outs = refs[:n]
    lv, rv, ov, lsem, rsem, osem = refs[n:]
    rows = b_own.shape[0]
    units = outs[0].shape[0] // 2
    loads = []
    for which, (left, parts) in enumerate(((gz, (b_own, b_sib)), (h, (g_own, g_sib)))):
        loads.append(pltpu.make_async_copy(left, lv.at[which], lsem.at[which]))
        for j, part in enumerate(parts):
            loads.append(
                pltpu.make_async_copy(
                    part, rv.at[which, pl.ds(j * rows, rows), :], rsem.at[which, j]
                )
            )
    for c in loads:
        c.start()
    stores = []
    step = 0
    for which in range(2):
        for c in loads[3 * which : 3 * which + 3]:
            c.wait()
        for pair in range(n // 2):
            slot = step % 2
            if step >= 2:
                for c in stores[2 * (step - 2) : 2 * (step - 2) + 2]:
                    c.wait()
            cols = pl.ds(pair * 2 * units, 2 * units)
            ov[slot] = dot(lv[which, :, cols], rv[which], TN).astype(bf16)
            for j in range(2):
                c = pltpu.make_async_copy(
                    ov.at[slot, pl.ds(j * units, units), :],
                    outs[2 * pair + j].at[pl.ds(which * units, units), :],
                    osem.at[slot, j],
                )
                c.start()
                stores.append(c)
            step += 1
    for c in stores[2 * (step - 2) :]:
        c.wait()


def ffn_weights_call(gz, h, b_own, b_sib, g_own, g_sib, n):
    rows, units = gz.shape
    width = b_own.shape[1]
    return pl.pallas_call(
        partial(ffn_weights_kernel, n),
        in_specs=[ANY] * 6,
        out_specs=[ANY] * n,
        out_shape=[shape((2 * units // n, width), bf16)] * n,
        scratch_shapes=[
            pltpu.VMEM((2, rows, units), bf16),
            pltpu.VMEM((2, rows, width), bf16),
            pltpu.VMEM((2, 2 * units // n, width), bf16),
            pltpu.SemaphoreType.DMA((2,)),
            pltpu.SemaphoreType.DMA((2, 2)),
            pltpu.SemaphoreType.DMA((2, 2)),
        ],
        compiler_params=params(),
        cost_estimate=cost(6 * rows * units * width, 4 * rows * (units + width)),
        name="ffn_weights",
    )(gz, h, b_own, b_sib, g_own, g_sib)


def mid_kernel(
    n, place_ref, oo_ref, os_ref, go_ref, gs_ref, m_ref, g_ref, keep_ref, db_ref, gain_ref, *refs
):
    slots, (hid_ref, gr_ref, gatt_ref, sums_ref, w, sem) = refs[:n], refs[n:]
    load_wout(slots, place_ref, w, sem)

    @pl.when(pl.program_id(0) == 0)
    def _():
        sums_ref[...] = jnp.zeros_like(sums_ref)

    m = m_ref[...]
    g = g_ref[...].astype(f32)
    ff = oo_ref[...].astype(f32) + os_ref[...].astype(f32)
    hid_ref[...] = (m + ff + db_ref[...]).astype(bf16)
    gb = go_ref[...].astype(f32) + gs_ref[...].astype(f32)
    xh, scale = norm_parts(m)
    gm = g + norm_back(xh, scale, gain_ref[...], gb)
    gr = gm.astype(bf16)
    gr_ref[...] = gr
    gatt_ref[...] = (dot(gr, w[...], NT) * keep_ref[...]).astype(bf16)
    sums_ref[0:1, :] += colsum(gb * xh)
    sums_ref[1:2, :] += colsum(gb)
    sums_ref[2:3, :] += colsum(gr.astype(f32))
    sums_ref[3:4, :] += colsum(g)


def mid_call(place, oo, os, go, gs, m, g, keep, db, gain, slots):
    rows, width = m.shape
    n = len(slots)
    block = rowed(ROWS, width)
    vec = fixed((1, width))
    return pl.pallas_call(
        partial(mid_kernel, n),
        grid_spec=pltpu.PrefetchScalarGridSpec(
            num_scalar_prefetch=1,
            grid=(rows // ROWS,),
            in_specs=[block] * 6 + [rowed(ROWS, 1), vec, vec] + [ANY] * n,
            out_specs=[block] * 3 + [fixed((8, width))],
            scratch_shapes=[pltpu.VMEM((width, width), bf16), pltpu.SemaphoreType.DMA((n,))],
        ),
        out_shape=[shape((rows, width), bf16)] * 3 + [shape((8, width), f32)],
        compiler_params=params(),
        cost_estimate=cost(4 * rows * width * width, width * (30 * rows + 2 * width)),
        name="mid",
    )(place, oo, os, go, gs, m, g, keep, db, gain, *slots)


def att_weights_kernel(n, counts, blocks, place_ref, *refs):
    lefts, at = [], 0
    for count in counts[:-1]:
        lefts.append(refs[at : at + count])
        at += count
    rights, refs = refs[at : at + counts[-1]], refs[at + counts[-1] :]
    outs, (lv, tv, rv, ov, lsem, rsem, osem) = refs[: n + 1], refs[n + 1 :]
    height = outs[0].shape[0]
    loads = []
    for i, pieces in enumerate(lefts):
        loads.append([])
        at = 0
        for j, r in enumerate(pieces):
            wide = r.shape[1]
            loads[-1].append(
                pltpu.make_async_copy(r, lv.at[i, :, pl.ds(at, wide)], lsem.at[i, j])
            )
            at += wide
    ends, right_loads = [], []
    for i, r in enumerate(rights):
        start = ends[-1] if ends else 0
        ends.append(start + r.shape[1])
        right_loads.append(
            pltpu.make_async_copy(r, rv.at[:, pl.ds(start, r.shape[1])], rsem.at[i])
        )
    for c in loads[0] + right_loads + [c for group in loads[1:] for c in group]:
        c.start()
    have, arrived = set(), 0
    stores = []
    for step, (left, start, wide) in enumerate(blocks):
        if left not in have:
            for c in loads[left]:
                c.wait()
            tv[left] = jnp.transpose(lv[left])
            have.add(left)
        while arrived < len(ends) and (arrived == 0 or ends[arrived - 1] < start + wide):
            right_loads[arrived].wait()
            arrived += 1
        slot = step % 2
        if step >= 2:
            for c in stores[step - 2]:
                c.wait()
        cols = pl.ds(start, wide)
        ov[slot, :, pl.ds(0, wide)] = dot(tv[left], rv[:, cols], NN).astype(bf16)
        stores.append([])
        for i in range(2 * n):
            rows = pl.ds(pl.multiple_of(place_ref[i] * height, 16), height)
            goal = outs[i].at[:, cols] if i < n else outs[n].at[i - n, :, cols]
            c = pltpu.make_async_copy(ov.at[slot, rows, pl.ds(0, wide)], goal, osem.at[slot, i])
            c.start()
            stores[-1].append(c)
    for group in stores[-2:]:
        for c in group:
            c.wait()


def att_weights_call(place, lefts, rights, blocks):
    rows, width = lefts[0][0].shape[0], sum(l.shape[1] for l in lefts[0])
    n = len(OFFSETS)
    total = sum(r.shape[1] for r in rights)
    wide = max(b[2] for b in blocks)
    height = width // (2 * n)
    return pl.pallas_call(
        partial(att_weights_kernel, n, [len(l) for l in lefts] + [len(rights)], blocks),
        grid_spec=pltpu.PrefetchScalarGridSpec(
            num_scalar_prefetch=1,
            grid=(1,),
            in_specs=[ANY] * (sum(len(l) for l in lefts) + len(rights)),
            out_specs=[ANY] * (n + 1),
            scratch_shapes=[
                pltpu.VMEM((len(lefts), rows, width), bf16),
                pltpu.VMEM((len(lefts), width, rows), bf16),
                pltpu.VMEM((rows, total), bf16),
                pltpu.VMEM((2, width, wide), bf16),
                pltpu.SemaphoreType.DMA((len(lefts), max(len(l) for l in lefts))),
                pltpu.SemaphoreType.DMA((len(rights),)),
                pltpu.SemaphoreType.DMA((2, 2 * n)),
            ],
        ),
        out_shape=[shape((height, total), bf16)] * n + [shape((n, height, total), bf16)],
        compiler_params=params(),
        cost_estimate=cost(3 * rows * width * total, 2 * (rows + width) * total),
        name="att_weights",
    )(place, *[a for l in lefts for a in l], *rights)


def in_kernel(n, pieces, place_ref, x_ref, gr_ref, gain_ref, *refs):
    grads, slots = refs[:pieces], refs[pieces : pieces + n]
    res_ref, sums_ref, w, sem = refs[pieces + n :]
    copies = place_rows(slots, w, place_ref, sem, cols=(0, w.shape[1]))

    @pl.when(pl.program_id(0) == 0)
    def _():
        for c in copies:
            c.start()
        for c in copies:
            c.wait()
        sums_ref[...] = jnp.zeros_like(sums_ref)

    ga = None
    col = 0
    for r in grads:
        part = dot(r[...], w[:, col : col + r.shape[1]], NT)
        ga = part if ga is None else ga + part
        col += r.shape[1]
    xh, scale = norm_parts(x_ref[...].astype(f32))
    res = gr_ref[...].astype(f32) + norm_back(xh, scale, gain_ref[...], ga)
    sums_ref[0:1, :] += colsum(ga * xh)
    sums_ref[1:2, :] += colsum(ga)
    res_ref[...] = res.astype(res_ref.dtype)


def in_call(place, x, gr, gain, grads, slots, part, dtype):
    rows, width = x.shape
    n = len(slots)
    half = rows // ROWS // 2

    def piece(w):
        return pl.BlockSpec((ROWS, w), lambda i, *_: (i + part * half, 0))

    return pl.pallas_call(
        partial(in_kernel, n, len(grads)),
        grid_spec=pltpu.PrefetchScalarGridSpec(
            num_scalar_prefetch=1,
            grid=(half,),
            in_specs=[piece(width), piece(width), fixed((1, width))]
            + [piece(g.shape[1]) for g in grads]
            + [ANY] * n,
            out_specs=[rowed(ROWS, width), fixed((8, width))],
            scratch_shapes=[
                pltpu.VMEM((width, 3 * width), bf16),
                pltpu.SemaphoreType.DMA((n,)),
            ],
        ),
        out_shape=[shape((rows // 2, width), dtype), shape((8, width), f32)],
        compiler_params=params(),
        cost_estimate=cost(4 * rows * width * width, width * (7 * rows + 6 * width)),
        name="in",
    )(place, x, gr, gain, *grads, *slots)


def fence(*trees):
    return lax.optimization_barrier(trees)


def side_by_side(vectors):
    total = sum(v.shape[0] for v in vectors)
    res, at = None, 0
    for v in vectors:
        wide = jnp.pad(v, (at, total - at - v.shape[0]))
        at += v.shape[0]
        res = wide if res is None else res + wide
    return res


def local_swapped(
    sizes, hidden_in, lengths, ln1_gain, ln1_bias, w_qkv, q_bias, v_bias, w_out, out_bias, ln2_gain, ln2_bias,
    w_up, up_bias, w_down, down_bias, cotangent,
):
    ring = Ring(sizes)
    blk = lax.axis_index("blk")
    core = lax.axis_index("cell") % 2
    genes, width = hidden_in.shape[1:]
    units = w_up.shape[0]
    shards = ring.cells
    n = len(OFFSETS)

    def vec(v):
        return v.reshape(1, -1)

    def pick(x, which):
        return lax.dynamic_index_in_dim(x, which, 0, keepdims=False)

    chips_own, chips_sib = ring.chips_of_slots(core), ring.chips_of_slots(1 - core)
    shard_own = 2 * chips_own + core
    shard_sib = 2 * chips_sib + 1 - core
    place = jnp.concatenate([shard_own, shard_sib])
    index = jnp.arange(genes, dtype=jnp.int32)
    index = jnp.concatenate([blk * genes + index, (1 - blk) * genes + index])
    keep = (index < pick(lengths, blk)).astype(f32)[:, None]
    mask = jnp.where(keep > 0, 0.0, far_below)

    x_got = ring.swap_blk(pick(hidden_in, 1 - blk))
    steps = ring.gather(jnp.concatenate([w_qkv, w_out], axis=1), 1)
    slots, sib = next(steps), [None] * n
    w_pair = jnp.concatenate([w_up, w_down], axis=0)
    g_send = pick(cotangent, 1 - blk)
    small = [vec(v) for v in (ln1_gain, ln1_bias, q_bias, v_bias, out_bias, ln2_gain, ln2_bias)]
    small += [place, mask, keep]
    slots[1], slots[5] = fence(slots[1], slots[5])
    slots = steps.send(slots)
    slots[2], small, w_pair = fence(slots[2], small, w_pair)
    ln1_gain, ln1_bias, q_bias, v_bias, out_bias, ln2_gain, ln2_bias, place, mask, keep = small
    slots = steps.send(slots)
    for s in (0, 1, 5, 2):
        sib[s] = ring.swap_core(slots[s])
    x = jnp.concatenate([pick(hidden_in, blk), x_got], axis=0)
    slots[3], x, sib, g_send = fence(slots[3], x, sib, g_send)
    slots = steps.send(slots)
    for s in (3, 4, 6, 7):
        sib[s] = ring.swap_core(slots[s])
    slots[4], w_pair = fence(slots[4], w_pair)
    pair = [w_pair, ring.shift(w_pair, 1)] + [None] * 6
    g_send, slots[7] = fence(g_send, slots[7])
    g_send = [g_send[: genes // 2], g_send[genes // 2 :]]
    g_got = [ring.swap_blk(g_send[0])]

    weights = slots + sib
    a, *qkv = qkv_call(place, x, ln1_gain, ln1_bias, q_bias, v_bias, weights)
    qkv, pair[1], g_got, g_send = fence(qkv, pair[1], g_got, g_send)
    g_got.append(ring.swap_blk(g_send[1]))
    pair[2] = ring.shift(pair[1], 1)
    pairs = width // 128
    cut = 6 * pairs // 10
    attended = [attend_call(mask, keep, qkv, 0, cut)]
    attended, qkv, pair[2], g_got = fence(attended, qkv, pair[2], g_got)
    pair[3] = ring.shift(pair[2], 1)
    g = jnp.concatenate([pick(cotangent, blk)] + g_got, axis=0)
    g_sib = ring.swap_core(g)
    attended.append(attend_call(mask, keep, qkv, cut, pairs - cut))
    o_parts = [t[0] for t in attended]
    m, b = out_call(place, x, o_parts, weights, out_bias, ln2_gain, ln2_bias)
    b, g_sib, pair[0], pair[3] = fence(b, g_sib, pair[0], pair[3])
    b_sib = ring.swap_core(b)
    pair[4] = ring.shift(pair[3], 1)
    pair[5] = ring.shift(pair[0], -1)
    pair[7] = ring.swap_blk(pair[3])

    ub = up_bias.reshape(shards, units)[shard_own]
    near, far = (0, 1, 2, 3), (4, 5, 6, 7)
    ub_near, ub_far = [vec(jnp.concatenate([ub[s] for s in group])) for group in (near, far)]
    h_near, gz_near, sum_near, *acc = ffn_call(
        b, b_sib, g, g_sib, ub_near, [pair[s] for s in near]
    )
    h_near, gz_near, acc, pair[5] = fence(h_near, gz_near, acc, pair[5])
    pair[6] = ring.shift(pair[5], -1)
    parts = [None] * n
    made = ffn_weights_call(gz_near, h_near, b, b_sib, g, g_sib, len(near))
    made, acc = fence(made, acc)
    for s, t in zip(near, made, strict=True):
        parts[s] = [t]
    h_far, gz_far, sum_far, oo, gb_own, os_send, gs_send = ffn_call(
        b, b_sib, g, g_sib, ub_far, [pair[s] for s in far], acc
    )
    up_sums = dict(
        zip(near + far, jnp.split(sum_near[0], 4) + jnp.split(sum_far[0], 4), strict=True)
    )
    mine = shard_own[None, :] == jnp.arange(shards, dtype=jnp.int32)[:, None]
    up_rows = jnp.sum(
        jnp.where(mine[:, :, None], jnp.stack([up_sums[s] for s in range(n)])[None], 0.0), axis=1
    )
    made = ffn_weights_call(gz_far, h_far, b, b_sib, g, g_sib, len(far))
    os_got, gs_got = ring.swap_core(os_send), ring.swap_core(gs_send)
    made, oo, os_got, gs_got = fence(made, oo, os_got, gs_got)
    for s, t in zip(far, made, strict=True):
        parts[s] = [t]
    steps = ring.reduce(parts, 1)
    way = next(steps)
    out_hidden, gr, gatt, mid_sums = mid_call(
        place, oo, os_got, gb_own, gs_got, m, g, keep, vec(down_bias), ln2_gain, weights
    )
    hid_send = [out_hidden[genes : genes + genes // 2], out_hidden[genes + genes // 2 :]]

    def back(first, count, gatt):
        o, lse = attended[0 if first < cut else 1]
        at = first if first < cut else first - cut
        return attend_back_call(mask, qkv, o, gatt, lse, count, (first, at, first))

    early, half = 128 * cut, width // 2
    late = width - early
    backs = [back(0, cut, gatt)]
    backs, gatt, way["ahead"], way["over3"], hid_send = fence(
        backs, gatt, way["ahead"], way["over3"], hid_send
    )
    way = steps.send(way)
    first = att_weights_call(
        place, [[a], o_parts], list(backs[0][:3]) + [gr],
        [(0, i * early, early) for i in range(3)] + [(1, 3 * early + i * half, half) for i in range(2)],
    )
    first, gatt, way, hid_send = fence(first, gatt, way, hid_send)
    way = steps.send(way)
    hid_got = [ring.swap_blk(hid_send[0])]
    first_sib = ring.swap_core(first[n])
    one = (pairs - cut) // 4
    backs.append(back(cut, one, gatt))
    backs, gatt, first, first_sib, up_rows = fence(backs, gatt, first, first_sib, up_rows)
    steps_first = ring.reduce([[first[s], first_sib[s]] for s in range(n)], 3)
    way_first = next(steps_first)
    backs.append(back(cut + one, pairs - cut - one, gatt))
    backs, way_first, way, hid_got, hid_send = fence(backs, way_first, way, hid_got, hid_send)
    way_first = steps_first.send(way_first)
    hid_got.append(ring.swap_blk(hid_send[1]))
    way = steps.send(way)
    grads = [t[i] for i in range(3) for t in backs]
    in_send, in_sums_send = in_call(place, x, gr, ln1_gain, grads, weights, 1, bf16)
    sums_early = side_by_side(
        [mid_sums[:4].reshape(-1), up_rows.reshape(-1)]
        + [t[i].reshape(-1) for i in (3, 4) for t in backs]
    )
    in_send, backs, way_first, hid_got, way = fence(in_send, backs, way_first, hid_got, way)
    ffn_sum = steps.send(way)
    ffn_sum = [ffn_sum[:units], ffn_sum[units:]]
    ffn_got = [ring.swap_blk(ffn_sum[0])]
    way_first = steps_first.send(way_first)
    in_got = ring.swap_blk(in_send)
    second = att_weights_call(
        place, [[a]], [t[i] for i in range(3) for t in backs[1:]],
        [(0, i * late, late) for i in range(3)],
    )
    second, way_first, grads, sums_early, ffn_got, ffn_sum = fence(
        second, way_first, grads, sums_early, ffn_got, ffn_sum
    )
    ffn_got.append(ring.swap_blk(ffn_sum[1]))
    way_first = steps_first.send(way_first)
    second_sib = ring.swap_core(second[n])
    steps_second = ring.reduce([[second[s], second_sib[s]] for s in range(n)], 3)
    way_second = next(steps_second)
    in_own, in_sums = in_call(place, x, gr, ln1_gain, grads, weights, 0, f32)
    w_up_grad = ffn_sum[0].astype(f32) + ffn_got[0].astype(f32)
    in_own, in_sums, in_sums_send, way_first, way_second, w_up_grad = fence(
        in_own, in_sums, in_sums_send, way_first, way_second, w_up_grad
    )
    first_sum = steps_first.send(way_first)
    first_got = ring.swap_blk(first_sum)
    way_second = steps_second.send(way_second)
    ln1_sums = (in_sums + in_sums_send)[:2].reshape(-1)
    steps_sums = ring.total(side_by_side([sums_early, ln1_sums]))
    sums = next(steps_sums)
    sums = steps_sums.send(sums)
    way_second, sums = fence(way_second, sums)
    way_second = steps_second.send(way_second)
    sums = steps_sums.send(sums)
    way_second, sums = fence(way_second, sums)
    way_second = steps_second.send(way_second)
    sums = steps_sums.send(sums)
    way_second, sums = fence(way_second, sums)
    second_sum = steps_second.send(way_second)
    second_got = ring.swap_blk(second_sum)
    sums = steps_sums.send(sums)
    down_sum, down_got, first_sum, first_got, in_got, second_sum, _ = fence(
        ffn_sum[1], ffn_got[1], first_sum, first_got, in_got, second_sum, sums[0]
    )
    sums = steps_sums.send(sums)
    w_down_grad, first_rows, second_rows = [
        a.astype(f32) + b.astype(f32)
        for a, b in ((down_sum, down_got), (first_sum, first_got), (second_sum, second_got))
    ]

    def home(own, got):
        got = got.astype(own.dtype)
        return jnp.where(blk == 0, jnp.stack([own, got]), jnp.stack([got, own]))

    hidden = home(out_hidden[:genes], jnp.concatenate(hid_got))
    in_grad = home(in_own, in_got)
    marks = [width] * 4 + [shards * units]
    marks += 2 * [128 * c for c in (cut, one, pairs - cut - one)] + [width] * 2
    pieces, at = [], 0
    for size in marks:
        pieces.append(sums[at : at + size])
        at += size
    ln2_gain_g, ln2_bias_g, out_bias_g, down_bias_g, up_bias_g = pieces[:5]
    q_bias_g, v_bias_g = jnp.concatenate(pieces[5:8]), jnp.concatenate(pieces[8:11])
    ln1_gain_g, ln1_bias_g = pieces[11:]
    w_qkv_grad = jnp.concatenate(
        [
            t
            for i in range(3)
            for t in (
                first_rows[:, i * early : (i + 1) * early],
                second_rows[:, i * late : (i + 1) * late],
            )
        ],
        axis=1,
    )
    return (
        hidden,
        in_grad,
        ln1_gain_g,
        ln1_bias_g,
        w_qkv_grad,
        q_bias_g,
        v_bias_g,
        first_rows[:, 3 * early :],
        out_bias_g,
        ln2_gain_g,
        ln2_bias_g,
        w_up_grad,
        up_bias_g,
        w_down_grad,
        down_bias_g,
    )


def solution(mesh):
    placed = (
        P("cell", "blk", None),
        P("cell"),
        P(),
        P(),
        P("cell", None),
        P(),
        P(),
        P("cell", None),
        P(),
        P(),
        P(),
        P("cell", None),
        P(),
        P("cell", None),
        P(),
        P("cell", "blk", None),
    )
    return jax.shard_map(
        partial(local_swapped, dict(mesh.shape)) if swappable(mesh) else local,
        mesh=mesh,
        in_specs=placed,
        out_specs=(
            P("cell", "blk", None),
            P("cell", "blk", None),
            P(),
            P(),
            P("cell", None),
            P(),
            P(),
            P("cell", None),
            P(),
            P(),
            P(),
            P("cell", None),
            P(),
            P("cell", None),
            P(),
        ),
        check_vma=False,
    )
```
